512 devices in a mesh: blk: 64 (over y_lo, z, core), along: 8 (over x, y_hi).
Axes of the slice: x: 4, y: 4 (y_hi: 2, y_lo: 2; y = y_hi * 2 + y_lo), z: 16, core: 2. Of those that a mesh axis runs over, the one named last changes fastest.
Arguments:
- values: float32 [3, 64, 192, 256], P(None, 'blk', 'along'), may hold values from -6 to 6
- offsets: float32 [3, 64, 192, 256], P(None, 'blk', 'along'), may hold values from 0 to 1
- stiffness: float32 [64, 192, 256], P('blk', 'along'), may hold values from 0.5 to 2
- leaf_basis: float32 [64, 192, 64, 256], P('blk', 'along'), may hold values from -0.375 to 0.375
- transfer: float32 [64, 192, 64, 64], P('blk', 'along'), may hold values from -0.15625 to 0.15625
- slab_transfer_matrices: float32 [64, 8, 64, 64], P('blk', 'along'), may hold values from -0.25 to 0.25
- leaf_coupling_matrices: float32 [64, 30, 64, 64], P('blk'), may hold values from -0.375 to 0.375
- leaf_admissible_mask: int32 [64, 30], P('blk'), may hold values 0 or 1
- top_coupling: float32 [64, 64, 64, 64], P('blk'), may hold values from -0.75 to 0.75
- top_admissible: int32 [64, 64], P('blk'), may hold values 0 or 1
Outputs:
- product: float32 [3, 64, 192, 256], P(None, 'blk', 'along')
The draws below stay inside these ranges and needn't reach their ends.
All inputs are finite; a program needn't handle non-finite values. No bound on the sum of `leaf_admissible_mask` or of `top_admissible` on one device may be relied on, other than what follows from the above.
Results may differ from the reference program's by a relative error of at most 0.0001.
Values sent between devices are 32-bit elements; how exact they have to be, the bound alone decides.
No kernel may reach another device: no remote copies, remote signals or barrier semaphores. Data moves between devices by JAX's collectives and lax.ppermute only.
A program may use at most 64 MiB of HBM per device.

```python
import math
import jax
import jax.numpy as jnp
from jax import lax

LEAF = 256
BASIS_RANK = 64
RHS = 3
LD = 24
REACH = 6
SECTOR_COUNT = 64
NAX = 192
SLOT_COUNT = 30


def set_ends(array, key, least, high):
    index_at = [jax.random.randint(jax.random.fold_in(key, axis), (), 0, length) for axis, length in enumerate(array.shape)]
    longest = array.shape.index(max(array.shape))
    next_to = index_at[:longest] + [(index_at[longest] + 1) % array.shape[longest]] + index_at[longest + 1:]
    return array.at[tuple(index_at)].set(least).at[tuple(next_to)].set(high)


def steps_of(rng, shape, cuts, low, high):
    def one(axis_at, parts):
        draws = jax.random.uniform(jax.random.fold_in(jax.random.fold_in(rng, 6), axis_at), (parts,), jnp.float32, low / len(cuts), high / len(cuts))
        return jnp.repeat(jnp.exp(draws), shape[axis_at] // parts).reshape((-1,) + (1,) * (len(shape) - axis_at - 1))

    gain = one(*cuts[0])
    for cut in cuts[1:]:
        gain = gain * one(*cut)
    return gain


def bell_draw(rng, dims, deviation, limit, split=(), held_as=jnp.bfloat16):
    entries = deviation * jax.random.normal(rng, dims, jnp.float32)
    if split:
        entries = entries * steps_of(rng, dims, split, -0.22, 0.18)
    return jnp.clip(entries, -limit, limit).astype(held_as)


def setup_inputs(seed: int = 0) -> dict:
    keys = jax.random.split(jax.random.key(seed), 11)
    values = bell_draw(keys[0], (RHS, SECTOR_COUNT, NAX, LEAF), 1.0, 6.0, ((1, 64), (2, 8)), jnp.float32)
    offsets = jnp.clip(1.0 * jax.random.uniform(keys[1], (3, SECTOR_COUNT, NAX, LEAF), jnp.float32) ** steps_of(keys[1], (3, SECTOR_COUNT, NAX, LEAF), ((1, 64), (2, 8)), -0.2, 0.2), 0.0, 1.0)
    stiffness = jnp.clip(jnp.exp(math.log(2.0) - 1.3862944 * jax.random.uniform(keys[2], (SECTOR_COUNT, NAX, LEAF), jnp.float32) ** steps_of(keys[2], (SECTOR_COUNT, NAX, LEAF), ((0, 64), (1, 8)), -0.2, 0.2)), 0.5, 2.0)
    leaf_basis = bell_draw(keys[3], (SECTOR_COUNT, NAX, BASIS_RANK, LEAF), LEAF ** -0.5, 0.375, ((0, 64), (1, 8)), jnp.float32)
    transfer = bell_draw(keys[4], (SECTOR_COUNT, NAX, BASIS_RANK, BASIS_RANK), (BASIS_RANK * LD) ** -0.5, 0.15625, ((0, 64), (1, 8)), jnp.float32)
    slab_transfer_matrices = bell_draw(keys[5], (SECTOR_COUNT, NAX // LD, BASIS_RANK, BASIS_RANK), (BASIS_RANK * NAX // LD) ** -0.5, 0.25, ((0, 64), (1, 8)), jnp.float32)
    leaf_coupling_matrices = bell_draw(keys[6], (SECTOR_COUNT, SLOT_COUNT, BASIS_RANK, BASIS_RANK), (4 * BASIS_RANK) ** -0.5, 0.375, ((0, 64),), jnp.float32)
    leaf_admissible_mask = set_ends((jax.random.randint(keys[7], (SECTOR_COUNT, SLOT_COUNT), 0, 4) < 3).astype(jnp.int32), jax.random.fold_in(keys[7], 1), 0, 1)
    top_coupling = bell_draw(keys[8], (SECTOR_COUNT, SECTOR_COUNT, BASIS_RANK, BASIS_RANK), BASIS_RANK ** -0.5, 0.75, ((0, 64),), jnp.float32)
    top_admissible = set_ends((jax.random.randint(keys[9], (SECTOR_COUNT, SECTOR_COUNT), 0, 4) < 3).astype(jnp.int32), jax.random.fold_in(keys[9], 1), 0, 1)
    return {"values": values, "offsets": offsets, "stiffness": stiffness, "leaf_basis": leaf_basis, "transfer": transfer, "slab_transfer_matrices": slab_transfer_matrices, "leaf_coupling_matrices": leaf_coupling_matrices, "leaf_admissible_mask": leaf_admissible_mask, "top_coupling": top_coupling, "top_admissible": top_admissible}


SHARPNESS = 2.0
KERNEL_SCALE = 0.125
HIGHEST_ACCURACY = lax.Precision.HIGHEST


def near_field(padded):
    leaves = padded.shape[2] - 2
    center = padded[:, 1:2, 1:1 + leaves]
    result = jnp.zeros((3, 1, leaves, padded.shape[3]), jnp.float32)
    for around in (-1, 0, 1):
        for along_step in (-1, 0, 1):
            source = padded[:, 1 + around:2 + around, 1 + along_step:1 + along_step + leaves]
            gap_around = around + source[0][..., None, :] - center[0][..., :, None]
            gap_along = along_step + source[1][..., None, :] - center[1][..., :, None]
            gap_radial = source[2][..., None, :] - center[2][..., :, None]
            squared = gap_around * gap_around + gap_along * gap_along + gap_radial * gap_radial
            kernel = KERNEL_SCALE * center[3][..., :, None] * source[3][..., None, :] * jnp.exp(-SHARPNESS * squared)
            result = result + jnp.einsum('alij,ralj->rali', kernel, source[4:], precision=HIGHEST_ACCURACY)
    return result


def slot_number(around, along_step, reach):
    block = around - 2 if around > 0 else reach - 1 + (-around - 2)
    return 3 * block + along_step + 1


def reference(values, offsets, stiffness, leaf_basis, transfer, slab_transfer_matrices, leaf_coupling_matrices, leaf_admissible_mask, top_coupling, top_admissible):
    stacked = jnp.concatenate([offsets, stiffness[None], values], 0)
    stacked = jnp.pad(stacked, ((0, 0), (0, 0), (1, 1), (0, 0)))
    stacked = jnp.concatenate([stacked[:, -1:], stacked, stacked[:, :1]], 1)

    def one_sector(sector):
        block = lax.dynamic_slice_in_dim(stacked, sector, 3, 1)
        return near_field(block)[:, 0]

    near = lax.map(one_sector, jnp.arange(SECTOR_COUNT, dtype=jnp.int32))
    near = jnp.transpose(near, (1, 0, 2, 3))

    coefs = jnp.einsum('slki,rsli->rslk', leaf_basis, values, precision=HIGHEST_ACCURACY)
    padded_coefs = jnp.pad(coefs, ((0, 0), (0, 0), (1, 1), (0, 0)))
    far_leaf = jnp.zeros(coefs.shape, jnp.float32)
    offsets_list = list(range(2, REACH + 1)) + [-step for step in range(2, REACH + 1)]
    for around in offsets_list:
        rolled = jnp.roll(padded_coefs, -around, axis=1)
        for along_step in (-1, 0, 1):
            slot = slot_number(around, along_step, REACH)
            partner = rolled[:, :, 1 + along_step:1 + along_step + NAX]
            coupling = leaf_coupling_matrices[:, slot] * leaf_admissible_mask[:, slot].astype(jnp.float32)[:, None, None]
            far_leaf = far_leaf + jnp.einsum('skq,rslq->rslk', coupling, partner, precision=HIGHEST_ACCURACY)

    slabs = NAX // LD
    grouped = coefs.reshape(RHS, SECTOR_COUNT, slabs, LD, BASIS_RANK)
    links = transfer.reshape(SECTOR_COUNT, slabs, LD, BASIS_RANK, BASIS_RANK)
    slab_coefficient_rows = jnp.einsum('splqk,rsplq->rspk', links, grouped, precision=HIGHEST_ACCURACY)
    sector_coefs = jnp.einsum('spqk,rspq->rsk', slab_transfer_matrices, slab_coefficient_rows, precision=HIGHEST_ACCURACY)

    indices = jnp.arange(SECTOR_COUNT, dtype=jnp.int32)
    apart = (indices[None, :] - indices[:, None]) % SECTOR_COUNT
    distant = jnp.logical_and(apart > REACH, apart < SECTOR_COUNT - REACH).astype(jnp.float32)
    allowed = top_admissible.astype(jnp.float32) * distant
    sector_local_coefs = jnp.einsum('stkq,rtq->rsk', top_coupling * allowed[:, :, None, None], sector_coefs, precision=HIGHEST_ACCURACY)

    slab_local_coefs = jnp.einsum('spqk,rsk->rspq', slab_transfer_matrices, sector_local_coefs, precision=HIGHEST_ACCURACY)
    leaf_down = jnp.einsum('splqk,rspk->rsplq', links, slab_local_coefs, precision=HIGHEST_ACCURACY).reshape(RHS, SECTOR_COUNT, NAX, BASIS_RANK)
    leaf_local = far_leaf + leaf_down
    return near + jnp.einsum('slki,rslk->rsli', leaf_basis, leaf_local, precision=HIGHEST_ACCURACY)
```

```python
import functools
import math

import jax
import jax.numpy as jnp
from jax import lax
from jax.experimental import pallas as pl
from jax.experimental.pallas import tpu as pltpu
from jax.sharding import PartitionSpec as P

REACH = 6
LEAF = 256
RANK = 64
RHS = 3
LD = 24
TALL = LD + 2
ROWS = 32
SHARPNESS = 2.0
KERNEL_SCALE = 0.125
LOG2E = math.log2(math.e)
F32 = jnp.float32
BF16 = jnp.bfloat16
EXACT = lax.Precision.HIGHEST
VMEM = pl.BlockSpec(memory_space=pltpu.VMEM)
SMEM = pl.BlockSpec(memory_space=pltpu.SMEM)
BY_LAST = (((1,), (1,)), ((), ()))
MIB = 2**20


def call(kernel, outs, ins, scratch=(), flops=0, vmem=48):
    return pl.pallas_call(
        kernel,
        out_shape=outs,
        in_specs=ins,
        out_specs=jax.tree.map(lambda _: VMEM, outs),
        scratch_shapes=list(scratch),
        compiler_params=pltpu.CompilerParams(vmem_limit_bytes=vmem * MIB),
        cost_estimate=pl.CostEstimate(flops=flops, bytes_accessed=1 << 20, transcendentals=0),
    )


def shaped(*shape):
    return jax.ShapeDtypeStruct(shape, F32)


def halves(x):
    high = x.astype(BF16).astype(F32)
    return high, x - high


def upward_kernel(at_ref, values_ref, offsets_ref, stiffness_ref, basis_ref, transfer_ref, slab_ref, wire_ref, slots_ref):
    lane = lax.broadcasted_iota(jnp.int32, (RANK, 128), 1)

    def leaf(l, carry):
        sums, columns = carry
        row = pl.ds(l, 1)
        new_sums = []
        for r in range(3):
            wire_ref[l, r : r + 1, :] = offsets_ref[r, row, :] - 0.5
            wire_ref[l, 4 + r : 5 + r, :] = values_ref[r, row, :]
        wire_ref[l, 3:4, :] = stiffness_ref[row, :]
        basis = basis_ref[l]
        transfer = transfer_ref[l]
        for r in range(3):
            column = jnp.sum(basis * values_ref[r, row, :], axis=1, keepdims=True)
            new_sums.append(sums[r] + transfer * column)
            columns = jnp.where(lane == r * ROWS + l, column, columns)
        return tuple(new_sums), columns

    nothing = jnp.zeros((RANK, RANK), F32)
    sums, columns = lax.fori_loop(
        0, LD, leaf, ((nothing,) * 3, jnp.zeros((RANK, 128), F32)), unroll=4
    )
    rows = jnp.transpose(columns, (1, 0))
    coefs = jnp.concatenate(
        [rows[:LD], rows[ROWS : ROWS + LD], rows[2 * ROWS : 2 * ROWS + LD], jnp.zeros((LD, RANK), F32)], 1
    )
    for l in range(LD):
        wire_ref[l, 7:8, :] = coefs[l : l + 1]
    slab_rows = jnp.concatenate(
        [jnp.sum(s, axis=0, keepdims=True) for s in sums] + [jnp.zeros((5, RANK), F32)], 0
    )
    share = jnp.dot(slab_rows, slab_ref[...], precision=EXACT, preferred_element_type=F32)
    share = jnp.concatenate([share, jnp.zeros((8, 128 - RANK), F32)], 1)
    here = at_ref[0]
    for j in range(8):
        slots_ref[j, :, :LEAF] = jnp.where(j < here, wire_ref[0], wire_ref[LD - 1])
        slots_ref[j, :, LEAF:] = share


def joined_kernel(at_ref, came_ref, wire_ref, tall_ref, whole_ref):
    here = at_ref[0]
    total = came_ref[0, :, LEAF:]
    for j in range(1, 8):
        total = total + came_ref[j, :, LEAF:]
    packed = jnp.concatenate(
        [
            jnp.concatenate([total[0:1, :RANK], total[1:2, :RANK]], 1),
            jnp.concatenate([total[2:3, :RANK], jnp.zeros((1, RANK), F32)], 1),
        ],
        0,
    )
    whole_ref[...] = jnp.broadcast_to(packed[None], whole_ref.shape)
    lower = came_ref[jnp.maximum(here - 1, 0), :, :LEAF]
    upper = came_ref[jnp.minimum(here + 1, 7), :, :LEAF]
    tall_ref[0] = jnp.where(here > 0, lower, 0.0)
    tall_ref[1 : LD + 1] = wire_ref[...]
    tall_ref[LD + 1] = jnp.where(here < 7, upper, 0.0)


def source_side(leaf, around, steps, slot, points_ref, loads_ref):
    high, low = halves(leaf)
    points_ref[slot] = jnp.transpose(jnp.concatenate([high, low, low, high], 0), (1, 0)).astype(BF16)
    c0, c1, c2 = leaf[0:1], leaf[1:2], leaf[2:3]
    flat = (c0 + around) * (c0 + around) + c2 * c2
    for step in steps:
        weight = jnp.exp2((-SHARPNESS * LOG2E) * (flat + (c1 + step) * (c1 + step))) * leaf[3:4]
        loads_ref[slot, step + 1] = jnp.concatenate(halves(leaf * weight), 0).astype(BF16)


def target_points(leaf):
    row = lax.broadcasted_iota(jnp.int32, leaf.shape, 0)
    high, low = halves(jnp.where(row < 3, leaf * (2 * SHARPNESS * LOG2E), 0.0))
    return jnp.concatenate([high, low, high, low], 0).astype(BF16)


def pair_kernel(target, points_ref, slot, pairs_ref, place):
    power = jnp.dot(points_ref[slot], target, preferred_element_type=F32)
    pair = jnp.exp2(power)
    high = pair.astype(BF16)
    pairs_ref[place, 0] = high
    pairs_ref[place, 1] = (pair - high.astype(F32)).astype(BF16)


def pair_sum(leaf, loads_ref, slot, pairs_ref, place, around, step):
    c0, c1, c2 = leaf[0:1], leaf[1:2], leaf[2:3]
    loads = loads_ref[slot, step + 1]
    rows = jnp.dot(loads, pairs_ref[place, 0], preferred_element_type=F32) + jnp.dot(
        loads, pairs_ref[place, 1], preferred_element_type=F32
    )
    power = (2 * SHARPNESS * LOG2E) * (around * c0 + step * c1) - (SHARPNESS * LOG2E) * (c0 * c0 + c1 * c1 + c2 * c2)
    weight = jnp.exp2(power) * (KERNEL_SCALE * leaf[3:4])
    return weight * (rows[:8] + rows[8:])


def near_own_kernel(wire_ref, near_ref, points_ref, loads_ref, pairs_ref):
    points_ref[0] = jnp.zeros((LEAF, 32), BF16)
    points_ref[LD + 1] = jnp.zeros((LEAF, 32), BF16)
    loads_ref[0] = jnp.zeros((3, 16, LEAF), BF16)
    loads_ref[LD + 1] = jnp.zeros((3, 16, LEAF), BF16)

    def prepare(l, _):
        source_side(wire_ref[l], 0, (-1, 0, 1), l + 1, points_ref, loads_ref)
        return 0

    lax.fori_loop(0, LD, prepare, 0, unroll=12)

    def leaf(l, _):
        here = wire_ref[l]
        target = target_points(here)
        for step in (-1, 0, 1):
            pair_kernel(target, points_ref, l + 1 + step, pairs_ref, step + 1)
        total = jnp.zeros((8, LEAF), F32)
        for step in (-1, 0, 1):
            total = total + pair_sum(here, loads_ref, l + 1 + step, pairs_ref, step + 1, 0, step)
        near_ref[l] = total
        return 0

    lax.fori_loop(0, LD, leaf, 0)


def near_cross_kernel(tall_ref, lower_ref, upper_ref, near_ref, points_ref, loads_ref, pairs_ref):
    for around, came_ref, base in ((-1, lower_ref, 0), (1, upper_ref, TALL)):

        def prepare(l, _, around=around, came_ref=came_ref, base=base):
            source_side(came_ref[l], around, (-1, 0, 1), base + l, points_ref, loads_ref)
            return 0

        lax.fori_loop(0, TALL, prepare, 0, unroll=13)
    source_side(tall_ref[0], 0, (-1,), 2 * TALL, points_ref, loads_ref)
    source_side(tall_ref[LD + 1], 0, (1,), 2 * TALL + 1, points_ref, loads_ref)

    def leaf(l, _):
        here = tall_ref[l + 1]
        target = target_points(here)
        sides = [(around, base, step) for around, base in ((-1, 0), (1, TALL)) for step in (-1, 0, 1)]
        for place, (around, base, step) in enumerate(sides):
            pair_kernel(target, points_ref, base + l + 1 + step, pairs_ref, place)
        total = jnp.zeros((8, LEAF), F32)
        for place, (around, base, step) in enumerate(sides):
            total = total + pair_sum(here, loads_ref, base + l + 1 + step, pairs_ref, place, around, step)
        near_ref[l] = total
        return 0

    lax.fori_loop(0, LD, leaf, 0)
    for l, slot, step in ((0, 2 * TALL, -1), (LD - 1, 2 * TALL + 1, 1)):
        here = tall_ref[l + 1]
        pair_kernel(target_points(here), points_ref, slot, pairs_ref, 0)
        near_ref[l] += pair_sum(here, loads_ref, slot, pairs_ref, 0, 0, step)


def near_scratch(leaves, places):
    return [
        pltpu.VMEM((leaves, LEAF, 32), BF16),
        pltpu.VMEM((leaves, 3, 16, LEAF), BF16),
        pltpu.VMEM((places, 2, LEAF, LEAF), BF16),
    ]


def window_kernel(lower_ref, tall_ref, upper_ref, window_ref, head_ref, tail_ref):
    for i, came_ref in enumerate((lower_ref, tall_ref, upper_ref)):
        rows = jnp.concatenate(
            [came_ref[l, 7:8, :] for l in range(TALL)] + [jnp.zeros((ROWS - TALL, LEAF), F32)], 0
        )
        window_ref[i] = rows
        if i < 2:
            head_ref[i] = rows
        if i > 0:
            tail_ref[i - 1] = rows


def far_kernel(mask_ref, below_ref, above_ref, far_below_ref, far_above_ref, coupling_ref, basis_ref, own_ref, cross_ref, part_ref):
    held = {-4 + i: below_ref[i] for i in range(3)}
    held |= {2 + i: above_ref[i] for i in range(3)}
    held |= {-6 + i: far_below_ref[i] for i in range(2)}
    held |= {5 + i: far_above_ref[i] for i in range(2)}
    total = jnp.zeros((3 * ROWS, 3 * RANK), F32)
    for q in range(2 * (REACH - 1)):
        around = q + 2 if q < REACH - 1 else 3 - q
        rows = held[around]
        stacked = jnp.concatenate([rows[:, r * RANK : (r + 1) * RANK] for r in range(3)], 0)
        coupling = jnp.concatenate(
            [coupling_ref[3 * q + b] * mask_ref[0, 3 * q + b].astype(F32) for b in range(3)], 0
        )
        total = total + lax.dot_general(stacked, coupling, BY_LAST, precision=EXACT, preferred_element_type=F32)
    far = []
    for r in range(3):
        block = total[r * ROWS : (r + 1) * ROWS]
        far.append(
            block[0:LD, :RANK] + block[1 : LD + 1, RANK : 2 * RANK] + block[2 : LD + 2, 2 * RANK :]
        )
        far.append(jnp.zeros((ROWS - LD, RANK), F32))
    columns = jnp.transpose(jnp.concatenate(far, 0), (1, 0))
    for l in range(LD):
        basis = basis_ref[l]
        for r in range(3):
            at = r * ROWS + l
            down = jnp.sum(basis * columns[:, at : at + 1], axis=0, keepdims=True)
            part_ref[r, l : l + 1, :] = down + own_ref[l, 4 + r : 5 + r, :] + cross_ref[l, 4 + r : 5 + r, :]


def downward_kernel(at_ref, admissible_ref, every_ref, top_ref, slab_ref, transfer_ref, basis_ref, part_ref, out_ref):
    here = at_ref[1]
    sectors = top_ref.shape[0]

    def couple(t, sums):
        apart = lax.rem(t - here + sectors, sectors)
        distant = jnp.logical_and(apart > REACH, apart < sectors - REACH)
        allowed = jnp.where(distant, admissible_ref[0, t], 0).astype(F32)
        coupling = top_ref[t]
        both = every_ref[t] * allowed
        rows = (both[0:1, :RANK], both[0:1, RANK:], both[1:2, :RANK])
        return tuple(s + coupling * row for s, row in zip(sums, rows))

    nothing = jnp.zeros((RANK, RANK), F32)
    sums = lax.fori_loop(0, sectors, couple, (nothing,) * 3, unroll=8)
    lane = lax.broadcasted_iota(jnp.int32, (RANK, 128), 1)
    columns = jnp.zeros((RANK, 128), F32)
    for r in range(3):
        columns = jnp.where(lane == r, jnp.sum(sums[r], axis=1, keepdims=True), columns)
    local = jnp.transpose(columns, (1, 0))[:8]
    slab = lax.dot_general(local, slab_ref[...], BY_LAST, precision=EXACT, preferred_element_type=F32)

    def leaf(l, _):
        basis = basis_ref[l]
        transfer = transfer_ref[l]
        for r in range(3):
            column = jnp.sum(transfer * slab[r : r + 1], axis=1, keepdims=True)
            down = jnp.sum(basis * column, axis=0, keepdims=True)
            out_ref[r, pl.ds(l, 1), :] = part_ref[r, pl.ds(l, 1), :] + down
        return 0

    lax.fori_loop(0, LD, leaf, 0, unroll=4)


def passed_along(x, axis, by):
    count = lax.axis_size(axis)
    return lax.ppermute(x, axis, [(i, (i + by) % count) for i in range(count)])


def body(
    values,
    offsets,
    stiffness,
    leaf_basis,
    transfer,
    slab_transfer_matrices,
    leaf_coupling_matrices,
    leaf_admissible_mask,
    top_coupling,
    top_admissible,
):
    at = jnp.stack([lax.axis_index("along"), lax.axis_index("blk")]).astype(jnp.int32)
    sectors = lax.axis_size("blk")
    values = values[:, 0]
    offsets = offsets[:, 0]
    basis = leaf_basis[0]
    transfer = transfer[0]
    slab = slab_transfer_matrices[0, 0]

    wire, slots = call(
        upward_kernel, (shaped(LD, 8, LEAF), shaped(8, 8, LEAF + 128)), [SMEM] + [VMEM] * 6, flops=10**9
    )(at, values, offsets, stiffness[0], basis, transfer, slab)
    came = lax.all_to_all(slots, "along", 0, 0, tiled=True)
    own = call(
        near_own_kernel, shaped(LD, 8, LEAF), [VMEM], near_scratch(TALL, 3), flops=9 * 10**9
    )(wire)
    tall, whole = call(
        joined_kernel, (shaped(TALL, 8, LEAF), shaped(sectors, 2, 128)), [SMEM, VMEM, VMEM], flops=10**8
    )(at, came, wire)
    lower = passed_along(tall, "blk", 1)
    upper = passed_along(tall, "blk", -1)
    every = lax.all_to_all(whole, "blk", 0, 0, tiled=True)
    window, head, tail = call(
        window_kernel,
        (shaped(3, ROWS, LEAF), shaped(2, ROWS, LEAF), shaped(2, ROWS, LEAF)),
        [VMEM] * 3,
        flops=10**8,
    )(lower, tall, upper)
    below = passed_along(window, "blk", 3)
    above = passed_along(window, "blk", -3)
    far_below = passed_along(head, "blk", 5)
    far_above = passed_along(tail, "blk", -5)
    cross = call(
        near_cross_kernel, shaped(LD, 8, LEAF), [VMEM] * 3, near_scratch(2 * TALL + 2, 6), flops=18 * 10**9
    )(tall, lower, upper)
    part = call(far_kernel, shaped(RHS, LD, LEAF), [SMEM] + [VMEM] * 8, flops=2 * 10**9)(
        leaf_admissible_mask, below, above, far_below, far_above, leaf_coupling_matrices[0], basis, own, cross
    )
    out = call(downward_kernel, shaped(RHS, LD, LEAF), [SMEM] * 2 + [VMEM] * 6, flops=2 * 10**9)(
        at, top_admissible, every, top_coupling[0], slab, transfer, basis, part
    )
    return out[:, None]


def solution(mesh):
    return jax.shard_map(
        body,
        mesh=mesh,
        in_specs=(
            P(None, "blk", "along", None),
            P(None, "blk", "along", None),
            P("blk", "along", None),
            P("blk", "along", None, None),
            P("blk", "along", None, None),
            P("blk", "along", None, None),
            P("blk", None, None, None),
            P("blk", None),
            P("blk", None, None, None),
            P("blk", None),
        ),
        out_specs=P(None, "blk", "along", None),
        check_vma=False,
    )
```

```python
import functools
import math

import jax
import jax.numpy as jnp
from jax import lax
from jax.experimental import pallas as pl
from jax.experimental.pallas import tpu as pltpu
from jax.sharding import PartitionSpec as P

REACH = 6
LEAF = 256
RANK = 64
RHS = 3
LD = 24
TALL = LD + 2
ROWS = 32
SHARPNESS = 2.0
KERNEL_SCALE = 0.125
LOG2E = math.log2(math.e)
F32 = jnp.float32
BF16 = jnp.bfloat16
EXACT = lax.Precision.HIGHEST
VMEM = pl.BlockSpec(memory_space=pltpu.VMEM)
HBM = pl.BlockSpec(memory_space=pltpu.HBM)
SMEM = pl.BlockSpec(memory_space=pltpu.SMEM)
BY_LAST = (((1,), (1,)), ((), ()))
MIB = 2**20
FULL = 60 * MIB + 128 * 1024
OWN_TURN = 3
CROSS_TURN = 2
UP_PARTS = 4
UP_LEAVES = LD // UP_PARTS


def call(kernel, outs, ins, scratch=(), flops=0, bytes=1 << 20, vmem=16 * MIB):
    return pl.pallas_call(
        kernel,
        out_shape=outs,
        in_specs=ins,
        out_specs=jax.tree.map(lambda _: VMEM, outs),
        scratch_shapes=list(scratch),
        compiler_params=pltpu.CompilerParams(vmem_limit_bytes=vmem),
        cost_estimate=pl.CostEstimate(flops=flops, bytes_accessed=bytes, transcendentals=0),
    )


def shaped(*shape):
    return jax.ShapeDtypeStruct(shape, F32)


def halves(x):
    high = x.astype(BF16).astype(F32)
    return high, x - high


def upward_kernel(
    at_ref, values_hbm, offsets_hbm, stiffness_hbm, basis_hbm, transfer_hbm, slab_hbm, wire_ref, slots_ref,
    values_ref, offsets_ref, stiffness_ref, basis_ref, transfer_ref, slab_ref, sems,
):
    lane = lax.broadcasted_iota(jnp.int32, (RANK, 128), 1)
    small = [
        pltpu.make_async_copy(source, target, sems.at[n])
        for n, (source, target) in enumerate(
            ((values_hbm, values_ref), (offsets_hbm, offsets_ref), (stiffness_hbm, stiffness_ref), (slab_hbm, slab_ref))
        )
    ]
    large = []
    for part in range(UP_PARTS):
        piece = pl.ds(part * UP_LEAVES, UP_LEAVES)
        large.append(
            [
                pltpu.make_async_copy(source.at[piece], target.at[piece], sems.at[4 + 2 * part + n])
                for n, (source, target) in enumerate(((basis_hbm, basis_ref), (transfer_hbm, transfer_ref)))
            ]
        )
    for copy in small + [copy for pair in large for copy in pair]:
        copy.start()
    for copy in small:
        copy.wait()

    def record(l, _):
        row = pl.ds(l, 1)
        for r in range(3):
            wire_ref[l, r : r + 1, :] = offsets_ref[r, row, :] - 0.5
            wire_ref[l, 4 + r : 5 + r, :] = values_ref[r, row, :]
        wire_ref[l, 3:4, :] = stiffness_ref[row, :]
        return 0

    lax.fori_loop(0, LD, record, 0, unroll=4)

    def leaf(l, carry):
        sums, columns = carry
        row = pl.ds(l, 1)
        new_sums = []
        basis = basis_ref[l]
        transfer = transfer_ref[l]
        for r in range(3):
            column = jnp.sum(basis * values_ref[r, row, :], axis=1, keepdims=True)
            new_sums.append(sums[r] + transfer * column)
            columns = jnp.where(lane == r * ROWS + l, column, columns)
        return tuple(new_sums), columns

    nothing = jnp.zeros((RANK, RANK), F32)
    carry = ((nothing,) * 3, jnp.zeros((RANK, 128), F32))
    for part in range(UP_PARTS):
        for copy in large[part]:
            copy.wait()
        carry = lax.fori_loop(part * UP_LEAVES, (part + 1) * UP_LEAVES, leaf, carry, unroll=UP_LEAVES)
    sums, columns = carry
    rows = jnp.transpose(columns, (1, 0))
    coefs = jnp.concatenate(
        [rows[:LD], rows[ROWS : ROWS + LD], rows[2 * ROWS : 2 * ROWS + LD], jnp.zeros((LD, RANK), F32)], 1
    )
    for l in range(LD):
        wire_ref[l, 7:8, :] = coefs[l : l + 1]
    slab_rows = jnp.concatenate(
        [jnp.sum(s, axis=0, keepdims=True) for s in sums] + [jnp.zeros((5, RANK), F32)], 0
    )
    share = jnp.dot(slab_rows, slab_ref[...], precision=EXACT, preferred_element_type=F32)
    share = jnp.concatenate([share, jnp.zeros((8, 128 - RANK), F32)], 1)
    here = at_ref[0]
    for j in range(8):
        slots_ref[j, :, :LEAF] = jnp.where(j < here, wire_ref[0], wire_ref[LD - 1])
        slots_ref[j, :, LEAF:] = share


def joined_kernel(at_ref, came_ref, wire_ref, tall_ref, whole_ref):
    here = at_ref[0]
    total = came_ref[0, :, LEAF:]
    for j in range(1, 8):
        total = total + came_ref[j, :, LEAF:]
    packed = jnp.concatenate(
        [
            jnp.concatenate([total[0:1, :RANK], total[1:2, :RANK]], 1),
            jnp.concatenate([total[2:3, :RANK], jnp.zeros((1, RANK), F32)], 1),
        ],
        0,
    )
    whole_ref[...] = jnp.broadcast_to(packed[None], whole_ref.shape)
    lower = came_ref[jnp.maximum(here - 1, 0), :, :LEAF]
    upper = came_ref[jnp.minimum(here + 1, 7), :, :LEAF]
    tall_ref[0] = jnp.where(here > 0, lower, 0.0)
    tall_ref[1 : LD + 1] = wire_ref[...]
    tall_ref[LD + 1] = jnp.where(here < 7, upper, 0.0)


def source_side(leaf, around, steps, slot, points_ref, loads_ref):
    high, low = halves(leaf)
    points_ref[slot] = jnp.transpose(jnp.concatenate([high, low, low, high], 0), (1, 0)).astype(BF16)
    c0, c1, c2 = leaf[0:1], leaf[1:2], leaf[2:3]
    flat = (c0 + around) * (c0 + around) + c2 * c2
    for step in steps:
        weight = jnp.exp2((-SHARPNESS * LOG2E) * (flat + (c1 + step) * (c1 + step))) * leaf[3:4]
        loads_ref[slot, step + 1] = jnp.concatenate(halves(leaf * weight), 0).astype(BF16)


def target_points(leaf):
    row = lax.broadcasted_iota(jnp.int32, leaf.shape, 0)
    high, low = halves(jnp.where(row < 3, leaf * (2 * SHARPNESS * LOG2E), 0.0))
    return jnp.concatenate([high, low, high, low], 0).astype(BF16)


def pair_kernel(target, points_ref, slot, pairs_ref, place):
    power = jnp.dot(points_ref[slot], target, preferred_element_type=F32)
    pair = jnp.exp2(power)
    high = pair.astype(BF16)
    pairs_ref[place, 0] = high
    pairs_ref[place, 1] = (pair - high.astype(F32)).astype(BF16)


def pair_sum(leaf, loads_ref, slot, pairs_ref, place, around, step):
    c0, c1, c2 = leaf[0:1], leaf[1:2], leaf[2:3]
    loads = loads_ref[slot, step + 1]
    rows = jnp.dot(loads, pairs_ref[place, 0], preferred_element_type=F32) + jnp.dot(
        loads, pairs_ref[place, 1], preferred_element_type=F32
    )
    power = (2 * SHARPNESS * LOG2E) * (around * c0 + step * c1) - (SHARPNESS * LOG2E) * (c0 * c0 + c1 * c1 + c2 * c2)
    weight = jnp.exp2(power) * (KERNEL_SCALE * leaf[3:4])
    return weight * (rows[:8] + rows[8:])


def near_own_kernel(wire_ref, near_ref, points_ref, loads_ref, pairs_ref):
    points_ref[0] = jnp.zeros((LEAF, 32), BF16)
    points_ref[LD + 1] = jnp.zeros((LEAF, 32), BF16)
    loads_ref[0] = jnp.zeros((3, 16, LEAF), BF16)
    loads_ref[LD + 1] = jnp.zeros((3, 16, LEAF), BF16)

    def prepare(l, _):
        source_side(wire_ref[l], 0, (-1, 0, 1), l + 1, points_ref, loads_ref)
        return 0

    lax.fori_loop(0, LD, prepare, 0, unroll=12)

    def turn(g, _):
        leaves = [g * OWN_TURN + n for n in range(OWN_TURN)]
        places = [(n, step) for n in range(OWN_TURN) for step in (-1, 0, 1)]
        targets = [target_points(wire_ref[l]) for l in leaves]
        for place, (n, step) in enumerate(places):
            pair_kernel(targets[n], points_ref, leaves[n] + 1 + step, pairs_ref, place)
        totals = [jnp.zeros((8, LEAF), F32)] * OWN_TURN
        for place, (n, step) in enumerate(places):
            totals[n] += pair_sum(wire_ref[leaves[n]], loads_ref, leaves[n] + 1 + step, pairs_ref, place, 0, step)
        for n in range(OWN_TURN):
            near_ref[leaves[n]] = totals[n]
        return 0

    lax.fori_loop(0, LD // OWN_TURN, turn, 0)


def near_cross_kernel(tall_ref, lower_ref, upper_ref, own_ref, near_ref, points_ref, loads_ref, pairs_ref):
    for around, came_ref, base in ((-1, lower_ref, 0), (1, upper_ref, TALL)):

        def prepare(l, _, around=around, came_ref=came_ref, base=base):
            source_side(came_ref[l], around, (-1, 0, 1), base + l, points_ref, loads_ref)
            return 0

        lax.fori_loop(0, TALL, prepare, 0, unroll=13)
    source_side(tall_ref[0], 0, (-1,), 2 * TALL, points_ref, loads_ref)
    source_side(tall_ref[LD + 1], 0, (1,), 2 * TALL + 1, points_ref, loads_ref)

    def turn(g, _):
        leaves = [g * CROSS_TURN + n for n in range(CROSS_TURN)]
        places = [
            (n, around, base, step)
            for n in range(CROSS_TURN)
            for around, base in ((-1, 0), (1, TALL))
            for step in (-1, 0, 1)
        ]
        targets = [target_points(tall_ref[l + 1]) for l in leaves]
        for place, (n, around, base, step) in enumerate(places):
            pair_kernel(targets[n], points_ref, base + leaves[n] + 1 + step, pairs_ref, place)
        totals = [jnp.zeros((8, LEAF), F32)] * CROSS_TURN
        for place, (n, around, base, step) in enumerate(places):
            slot = base + leaves[n] + 1 + step
            totals[n] += pair_sum(tall_ref[leaves[n] + 1], loads_ref, slot, pairs_ref, place, around, step)
        for n in range(CROSS_TURN):
            near_ref[leaves[n]] = own_ref[leaves[n]] + totals[n]
        return 0

    lax.fori_loop(0, LD // CROSS_TURN, turn, 0)
    for l, slot, step in ((0, 2 * TALL, -1), (LD - 1, 2 * TALL + 1, 1)):
        here = tall_ref[l + 1]
        pair_kernel(target_points(here), points_ref, slot, pairs_ref, 0)
        near_ref[l] += pair_sum(here, loads_ref, slot, pairs_ref, 0, 0, step)


def near_scratch(leaves, places):
    return [
        pltpu.VMEM((leaves, LEAF, 32), BF16),
        pltpu.VMEM((leaves, 3, 16, LEAF), BF16),
        pltpu.VMEM((places, 2, LEAF, LEAF), BF16),
    ]


def window_kernel(lower_ref, tall_ref, upper_ref, window_ref, head_ref, tail_ref):
    for i, came_ref in enumerate((lower_ref, tall_ref, upper_ref)):
        rows = jnp.concatenate(
            [came_ref[l, 7:8, :] for l in range(TALL)] + [jnp.zeros((ROWS - TALL, LEAF), F32)], 0
        )
        window_ref[i] = rows
        if i < 2:
            head_ref[i] = rows
        if i > 0:
            tail_ref[i - 1] = rows


def exact_by_last(x, y):
    return lax.dot_general(x, y, BY_LAST, precision=EXACT, preferred_element_type=F32)


def three_by_last(x, y):
    (xh, xl), (yh, yl) = halves(x), halves(y)
    xh, xl, yh, yl = (z.astype(BF16) for z in (xh, xl, yh, yl))
    high = lax.dot_general(xh, yh, BY_LAST, preferred_element_type=F32)
    cross = lax.dot_general(xl, yh, BY_LAST, preferred_element_type=F32)
    return high + (cross + lax.dot_general(xh, yl, BY_LAST, preferred_element_type=F32))


def finish_kernel(
    at_ref, mask_ref, admissible_ref, below_ref, above_ref, far_below_ref, far_above_ref, near_ref, every_ref,
    slab_ref, coupling_ref, top_ref, transfer_ref, basis_ref, out_ref, far_ref,
):
    held = {-4 + i: below_ref[i] for i in range(3)}
    held |= {2 + i: above_ref[i] for i in range(3)}
    held |= {-6 + i: far_below_ref[i] for i in range(2)}
    held |= {5 + i: far_above_ref[i] for i in range(2)}
    total = jnp.zeros((3 * ROWS, 3 * RANK), F32)
    for q in range(2 * (REACH - 1)):
        around = q + 2 if q < REACH - 1 else 3 - q
        rows = held[around]
        stacked = jnp.concatenate([rows[:, r * RANK : (r + 1) * RANK] for r in range(3)], 0)
        coupling = jnp.concatenate(
            [coupling_ref[3 * q + b] * mask_ref[0, 3 * q + b].astype(F32) for b in range(3)], 0
        )
        total = total + three_by_last(stacked, coupling)
    far = []
    for r in range(3):
        block = total[r * ROWS : (r + 1) * ROWS]
        rows = block[0:LD, :RANK] + block[1 : LD + 1, RANK : 2 * RANK] + block[2 : LD + 2, 2 * RANK :]
        far.append(jnp.concatenate([rows, jnp.zeros((ROWS - LD, RANK), F32)], 0))
    far.append(jnp.zeros((ROWS, RANK), F32))
    columns = jnp.transpose(jnp.concatenate(far, 0), (1, 0))
    far_columns = [columns[:, r * ROWS : (r + 1) * ROWS] for r in range(3)]
    for r in range(3):
        far_ref[r] = jnp.concatenate([far_columns[r], jnp.zeros((RANK, RANK - ROWS), F32)], 1)

    here = at_ref[1]
    sectors = top_ref.shape[0]

    def couple(t, sums):
        apart = lax.rem(t - here + sectors, sectors)
        distant = jnp.logical_and(apart > REACH, apart < sectors - REACH)
        allowed = jnp.where(distant, admissible_ref[0, t], 0).astype(F32)
        coupling = top_ref[t]
        both = every_ref[t] * allowed
        rows = (both[0:1, :RANK], both[0:1, RANK:], both[1:2, :RANK])
        return tuple(s + coupling * row for s, row in zip(sums, rows))

    nothing = jnp.zeros((RANK, RANK), F32)
    sums = lax.fori_loop(0, sectors, couple, (nothing,) * 3, unroll=16)
    lane = lax.broadcasted_iota(jnp.int32, (RANK, 128), 1)
    columns = jnp.zeros((RANK, 128), F32)
    for r in range(3):
        columns = jnp.where(lane == r, jnp.sum(sums[r], axis=1, keepdims=True), columns)
    local = jnp.transpose(columns, (1, 0))[:8]
    slab = exact_by_last(local, slab_ref[...])

    place = lax.broadcasted_iota(jnp.int32, (RANK, RANK), 1)

    def leaf(l, _):
        basis = basis_ref[l]
        transfer = transfer_ref[l]
        near = near_ref[l]
        for r in range(3):
            terms = transfer * slab[r : r + 1] + jnp.where(place == l, far_ref[r], 0.0)
            column = jnp.sum(terms, axis=1, keepdims=True)
            out_ref[r, pl.ds(l, 1), :] = jnp.sum(basis * column, axis=0, keepdims=True) + near[4 + r : 5 + r]
        return 0

    lax.fori_loop(0, LD, leaf, 0, unroll=8)


def upward(*args):
    outs = (shaped(LD, 8, LEAF), shaped(8, 8, LEAF + 128))
    scratch = [pltpu.VMEM(x.shape, F32) for x in args[1:]] + [pltpu.SemaphoreType.DMA((4 + 2 * UP_PARTS,))]
    return call(upward_kernel, outs, [SMEM] + [HBM] * 6, scratch, flops=10**9, vmem=FULL)(*args)


def near_own(wire):
    scratch = near_scratch(TALL, 3 * OWN_TURN)
    return call(near_own_kernel, shaped(LD, 8, LEAF), [VMEM], scratch, flops=9 * 10**9)(wire)


def near_cross(*args):
    scratch = near_scratch(2 * TALL + 2, 6 * CROSS_TURN)
    return call(near_cross_kernel, shaped(LD, 8, LEAF), [VMEM] * 4, scratch, flops=18 * 10**9, bytes=10**8)(*args)


def finish(*args):
    return call(finish_kernel, shaped(RHS, LD, LEAF), [SMEM] * 3 + [VMEM] * 11, [pltpu.VMEM((3, RANK, RANK), F32)], flops=4 * 10**9)(
        *args
    )


def passed_along(x, axis, by):
    count = lax.axis_size(axis)
    return lax.ppermute(x, axis, [(i, (i + by) % count) for i in range(count)])


def body(
    values,
    offsets,
    stiffness,
    leaf_basis,
    transfer,
    slab_transfer_matrices,
    leaf_coupling_matrices,
    leaf_admissible_mask,
    top_coupling,
    top_admissible,
):
    at = jnp.stack([lax.axis_index("along"), lax.axis_index("blk")]).astype(jnp.int32)
    sectors = lax.axis_size("blk")
    values = values[:, 0]
    offsets = offsets[:, 0]
    basis = leaf_basis[0]
    transfer = transfer[0]
    slab = slab_transfer_matrices[0, 0]

    wire, slots = upward(at, values, offsets, stiffness[0], basis, transfer, slab)
    came = lax.all_to_all(slots, "along", 0, 0, tiled=True)
    own = near_own(wire)
    came, own = lax.optimization_barrier((came, own))
    tall, whole = call(
        joined_kernel, (shaped(TALL, 8, LEAF), shaped(sectors, 2, 128)), [SMEM, VMEM, VMEM], flops=10**8
    )(at, came, wire)
    lower = passed_along(tall, "blk", 1)
    upper = passed_along(tall, "blk", -1)
    every = lax.all_to_all(whole, "blk", 0, 0, tiled=True)
    window, head, tail = call(
        window_kernel,
        (shaped(3, ROWS, LEAF), shaped(2, ROWS, LEAF), shaped(2, ROWS, LEAF)),
        [VMEM] * 3,
        flops=10**8,
    )(lower, tall, upper)
    below = passed_along(window, "blk", 3)
    above = passed_along(window, "blk", -3)
    far_below = passed_along(head, "blk", 5)
    far_above = passed_along(tail, "blk", -5)
    near = near_cross(tall, lower, upper, own)
    out = finish(
        at, leaf_admissible_mask, top_admissible, below, above, far_below, far_above, near, every,
        slab, leaf_coupling_matrices[0], top_coupling[0], transfer, basis,
    )
    return out[:, None]


def solution(mesh):
    return jax.shard_map(
        body,
        mesh=mesh,
        in_specs=(
            P(None, "blk", "along", None),
            P(None, "blk", "along", None),
            P("blk", "along", None),
            P("blk", "along", None, None),
            P("blk", "along", None, None),
            P("blk", "along", None, None),
            P("blk", None, None, None),
            P("blk", None),
            P("blk", None, None, None),
            P("blk", None),
        ),
        out_specs=P(None, "blk", "along", None),
        check_vma=False,
    )
```

```python
import functools
import math

import jax
import jax.numpy as jnp
from jax import lax
from jax.experimental import pallas as pl
from jax.experimental.pallas import tpu as pltpu
from jax.sharding import PartitionSpec as P

REACH = 6
LEAF = 256
RANK = 64
RHS = 3
LD = 24
TALL = LD + 2
ROWS = 32
SHARPNESS = 2.0
KERNEL_SCALE = 0.125
LOG2E = math.log2(math.e)
F32 = jnp.float32
BF16 = jnp.bfloat16
EXACT = lax.Precision.HIGHEST
VMEM = pl.BlockSpec(memory_space=pltpu.VMEM)
HBM = pl.BlockSpec(memory_space=pltpu.HBM)
SMEM = pl.BlockSpec(memory_space=pltpu.SMEM)
BY_LAST = (((1,), (1,)), ((), ()))
MIB = 2**20
FULL = 60 * MIB + 128 * 1024
OWN_TURN = 3
GROUP = 8
UP_PARTS = 4
UP_LEAVES = LD // UP_PARTS


def call(kernel, outs, ins, scratch=(), flops=0, bytes=1 << 20, vmem=16 * MIB):
    return pl.pallas_call(
        kernel,
        out_shape=outs,
        in_specs=ins,
        out_specs=jax.tree.map(lambda _: VMEM, outs),
        scratch_shapes=list(scratch),
        compiler_params=pltpu.CompilerParams(vmem_limit_bytes=vmem),
        cost_estimate=pl.CostEstimate(flops=flops, bytes_accessed=bytes, transcendentals=0),
    )


def shaped(*shape):
    return jax.ShapeDtypeStruct(shape, F32)


def halves(x):
    high = x.astype(BF16).astype(F32)
    return high, x - high


def upward_kernel(
    at_ref, values_hbm, offsets_hbm, stiffness_hbm, basis_hbm, transfer_hbm, slab_hbm, wire_ref, slots_ref,
    values_ref, offsets_ref, stiffness_ref, basis_ref, transfer_ref, slab_ref, sems,
):
    lane = lax.broadcasted_iota(jnp.int32, (RANK, 128), 1)
    small = [
        pltpu.make_async_copy(source, target, sems.at[n])
        for n, (source, target) in enumerate(
            ((values_hbm, values_ref), (offsets_hbm, offsets_ref), (stiffness_hbm, stiffness_ref), (slab_hbm, slab_ref))
        )
    ]
    large = []
    for part in range(UP_PARTS):
        piece = pl.ds(part * UP_LEAVES, UP_LEAVES)
        large.append(
            [
                pltpu.make_async_copy(source.at[piece], target.at[piece], sems.at[4 + 2 * part + n])
                for n, (source, target) in enumerate(((basis_hbm, basis_ref), (transfer_hbm, transfer_ref)))
            ]
        )
    for copy in small + [copy for pair in large for copy in pair]:
        copy.start()
    for copy in small:
        copy.wait()

    def record(l, _):
        row = pl.ds(l, 1)
        for r in range(3):
            wire_ref[l, r : r + 1, :] = offsets_ref[r, row, :] - 0.5
            wire_ref[l, 4 + r : 5 + r, :] = values_ref[r, row, :]
        wire_ref[l, 3:4, :] = stiffness_ref[row, :]
        return 0

    lax.fori_loop(0, LD, record, 0, unroll=4)

    def leaf(l, carry):
        sums, columns = carry
        row = pl.ds(l, 1)
        new_sums = []
        basis = basis_ref[l]
        transfer = transfer_ref[l]
        for r in range(3):
            column = jnp.sum(basis * values_ref[r, row, :], axis=1, keepdims=True)
            new_sums.append(sums[r] + transfer * column)
            columns = jnp.where(lane == r * ROWS + l, column, columns)
        return tuple(new_sums), columns

    nothing = jnp.zeros((RANK, RANK), F32)
    carry = ((nothing,) * 3, jnp.zeros((RANK, 128), F32))
    for part in range(UP_PARTS):
        for copy in large[part]:
            copy.wait()
        carry = lax.fori_loop(part * UP_LEAVES, (part + 1) * UP_LEAVES, leaf, carry, unroll=UP_LEAVES)
    sums, columns = carry
    rows = jnp.transpose(columns, (1, 0))
    coefs = jnp.concatenate(
        [rows[:LD], rows[ROWS : ROWS + LD], rows[2 * ROWS : 2 * ROWS + LD], jnp.zeros((LD, RANK), F32)], 1
    )
    for l in range(LD):
        wire_ref[l, 7:8, :] = coefs[l : l + 1]
    slab_rows = jnp.concatenate(
        [jnp.sum(s, axis=0, keepdims=True) for s in sums] + [jnp.zeros((5, RANK), F32)], 0
    )
    share = jnp.dot(slab_rows, slab_ref[...], precision=EXACT, preferred_element_type=F32)
    share = jnp.concatenate([share, jnp.zeros((8, 128 - RANK), F32)], 1)
    here = at_ref[0]
    for j in range(8):
        slots_ref[j, :, :LEAF] = jnp.where(j < here, wire_ref[0], wire_ref[LD - 1])
        slots_ref[j, :, LEAF:] = share


def joined_kernel(at_ref, came_ref, wire_ref, tall_ref, rows_ref):
    here = at_ref[0]
    total = came_ref[0, :, LEAF:]
    for j in range(1, 8):
        total = total + came_ref[j, :, LEAF:]
    lower = came_ref[jnp.maximum(here - 1, 0), :, :LEAF]
    upper = came_ref[jnp.minimum(here + 1, 7), :, :LEAF]
    tall_ref[0] = jnp.where(here > 0, lower, 0.0)
    tall_ref[1 : LD + 1] = wire_ref[...]
    tall_ref[LD + 1] = jnp.where(here < 7, upper, 0.0)
    share = jnp.concatenate([total[r : r + 1, :RANK] for r in range(3)] + [jnp.zeros((1, RANK), F32)], 1)
    rows = jnp.concatenate(
        [tall_ref[l, 7:8, :] for l in range(TALL)] + [share, jnp.zeros((ROWS - TALL - 1, LEAF), F32)], 0
    )
    for j in range(GROUP):
        rows_ref[j] = rows


def group_kernel(group_ref, low_ref, high_ref, shares_ref):
    low_ref[...] = group_ref[GROUP - REACH :]
    high_ref[...] = group_ref[:REACH]
    shares = jnp.concatenate([group_ref[j, TALL : TALL + 1, :] for j in range(GROUP)], 0)
    shares_ref[...] = jnp.broadcast_to(shares[None], shares_ref.shape)


def source_side(leaf, around, steps, slot, points_ref, loads_ref):
    high, low = halves(leaf)
    points_ref[slot] = jnp.transpose(jnp.concatenate([high, low, low, high], 0), (1, 0)).astype(BF16)
    c0, c1, c2 = leaf[0:1], leaf[1:2], leaf[2:3]
    flat = (c0 + around) * (c0 + around) + c2 * c2
    for step in steps:
        weight = jnp.exp2((-SHARPNESS * LOG2E) * (flat + (c1 + step) * (c1 + step))) * leaf[3:4]
        loads_ref[slot, step + 1] = jnp.concatenate(halves(leaf * weight), 0).astype(BF16)


def target_points(leaf):
    row = lax.broadcasted_iota(jnp.int32, leaf.shape, 0)
    high, low = halves(jnp.where(row < 3, leaf * (2 * SHARPNESS * LOG2E), 0.0))
    return jnp.concatenate([high, low, high, low], 0).astype(BF16)


def pair_kernel(target, points_ref, slot, pairs_ref, place):
    power = jnp.dot(points_ref[slot], target, preferred_element_type=F32)
    pair = jnp.exp2(power)
    high = pair.astype(BF16)
    pairs_ref[place, 0] = high
    pairs_ref[place, 1] = (pair - high.astype(F32)).astype(BF16)


def pair_sum(leaf, loads_ref, slot, pairs_ref, place, around, step):
    c0, c1, c2 = leaf[0:1], leaf[1:2], leaf[2:3]
    loads = loads_ref[slot, step + 1]
    rows = jnp.dot(loads, pairs_ref[place, 0], preferred_element_type=F32) + jnp.dot(
        loads, pairs_ref[place, 1], preferred_element_type=F32
    )
    power = (2 * SHARPNESS * LOG2E) * (around * c0 + step * c1) - (SHARPNESS * LOG2E) * (c0 * c0 + c1 * c1 + c2 * c2)
    weight = jnp.exp2(power) * (KERNEL_SCALE * leaf[3:4])
    return weight * (rows[:8] + rows[8:])


def near_own_kernel(wire_ref, near_ref, points_ref, loads_ref, pairs_ref):
    points_ref[0] = jnp.zeros((LEAF, 32), BF16)
    points_ref[LD + 1] = jnp.zeros((LEAF, 32), BF16)
    loads_ref[0] = jnp.zeros((3, 16, LEAF), BF16)
    loads_ref[LD + 1] = jnp.zeros((3, 16, LEAF), BF16)

    def prepare(l, _):
        source_side(wire_ref[l], 0, (-1, 0, 1), l + 1, points_ref, loads_ref)
        return 0

    lax.fori_loop(0, LD, prepare, 0, unroll=12)

    def turn(g, _):
        leaves = [g * OWN_TURN + n for n in range(OWN_TURN)]
        places = [(n, step) for n in range(OWN_TURN) for step in (-1, 0, 1)]
        targets = [target_points(wire_ref[l]) for l in leaves]
        for place, (n, step) in enumerate(places):
            pair_kernel(targets[n], points_ref, leaves[n] + 1 + step, pairs_ref, place)
        totals = [jnp.zeros((8, LEAF), F32)] * OWN_TURN
        for place, (n, step) in enumerate(places):
            totals[n] += pair_sum(wire_ref[leaves[n]], loads_ref, leaves[n] + 1 + step, pairs_ref, place, 0, step)
        for n in range(OWN_TURN):
            near_ref[leaves[n]] = totals[n]
        return 0

    lax.fori_loop(0, LD // OWN_TURN, turn, 0)


def near_side_kernel(around, tall_ref, came_ref, before_ref, near_ref, points_ref, loads_ref, pairs_ref):
    def prepare(l, _):
        source_side(came_ref[l], around, (-1, 0, 1), l, points_ref, loads_ref)
        return 0

    lax.fori_loop(0, TALL, prepare, 0, unroll=13)

    def turn(g, _):
        leaves = [g * OWN_TURN + n for n in range(OWN_TURN)]
        places = [(n, step) for n in range(OWN_TURN) for step in (-1, 0, 1)]
        targets = [target_points(tall_ref[l + 1]) for l in leaves]
        for place, (n, step) in enumerate(places):
            pair_kernel(targets[n], points_ref, leaves[n] + 1 + step, pairs_ref, place)
        totals = [before_ref[l] for l in leaves]
        for place, (n, step) in enumerate(places):
            slot = leaves[n] + 1 + step
            totals[n] += pair_sum(tall_ref[leaves[n] + 1], loads_ref, slot, pairs_ref, place, around, step)
        for n in range(OWN_TURN):
            near_ref[leaves[n]] = totals[n]
        return 0

    lax.fori_loop(0, LD // OWN_TURN, turn, 0)
    end, l, step = ((0, 0, -1), None, (LD + 1, LD - 1, 1))[around + 1]
    here = tall_ref[l + 1]
    source_side(tall_ref[end], 0, (step,), TALL, points_ref, loads_ref)
    pair_kernel(target_points(here), points_ref, TALL, pairs_ref, 0)
    near_ref[l] += pair_sum(here, loads_ref, TALL, pairs_ref, 0, 0, step)


def near_scratch(leaves, places):
    return [
        pltpu.VMEM((leaves, LEAF, 32), BF16),
        pltpu.VMEM((leaves, 3, 16, LEAF), BF16),
        pltpu.VMEM((places, 2, LEAF, LEAF), BF16),
    ]


def exact_by_last(x, y):
    return lax.dot_general(x, y, BY_LAST, precision=EXACT, preferred_element_type=F32)


def three_by_last(x, y):
    (xh, xl), (yh, yl) = halves(x), halves(y)
    xh, xl, yh, yl = (z.astype(BF16) for z in (xh, xl, yh, yl))
    high = lax.dot_general(xh, yh, BY_LAST, preferred_element_type=F32)
    cross = lax.dot_general(xl, yh, BY_LAST, preferred_element_type=F32)
    return high + (cross + lax.dot_general(xh, yl, BY_LAST, preferred_element_type=F32))


def finish_kernel(
    at_ref, mask_ref, admissible_ref, group_ref, below_ref, above_ref, near_ref, every_ref,
    slab_ref, coupling_ref, top_ref, transfer_ref, basis_ref, out_ref, far_ref, ring_ref,
):
    ring_ref[:REACH] = below_ref[...]
    ring_ref[REACH : REACH + GROUP] = group_ref[...]
    ring_ref[REACH + GROUP :] = above_ref[...]
    here = at_ref[1]
    member = lax.rem(here, GROUP)
    total = jnp.zeros((3 * ROWS, 3 * RANK), F32)
    for q in range(2 * (REACH - 1)):
        around = q + 2 if q < REACH - 1 else 3 - q
        rows = ring_ref[member + (REACH + around)]
        stacked = jnp.concatenate([rows[:, r * RANK : (r + 1) * RANK] for r in range(3)], 0)
        coupling = jnp.concatenate(
            [coupling_ref[3 * q + b] * mask_ref[0, 3 * q + b].astype(F32) for b in range(3)], 0
        )
        total = total + three_by_last(stacked, coupling)
    far = []
    for r in range(3):
        block = total[r * ROWS : (r + 1) * ROWS]
        rows = block[0:LD, :RANK] + block[1 : LD + 1, RANK : 2 * RANK] + block[2 : LD + 2, 2 * RANK :]
        far.append(jnp.concatenate([rows, jnp.zeros((ROWS - LD, RANK), F32)], 0))
    far.append(jnp.zeros((ROWS, RANK), F32))
    columns = jnp.transpose(jnp.concatenate(far, 0), (1, 0))
    far_columns = [columns[:, r * ROWS : (r + 1) * ROWS] for r in range(3)]
    for r in range(3):
        far_ref[r] = jnp.concatenate([far_columns[r], jnp.zeros((RANK, RANK - ROWS), F32)], 1)

    sectors = top_ref.shape[0]

    def couple(t, sums):
        apart = lax.rem(t - here + sectors, sectors)
        distant = jnp.logical_and(apart > REACH, apart < sectors - REACH)
        allowed = jnp.where(distant, admissible_ref[0, t], 0).astype(F32)
        coupling = top_ref[t]
        row = every_ref[pl.ds(t, 1), :] * allowed
        return tuple(s + coupling * row[:, r * RANK : (r + 1) * RANK] for r, s in enumerate(sums))

    nothing = jnp.zeros((RANK, RANK), F32)
    sums = lax.fori_loop(0, sectors, couple, (nothing,) * 3, unroll=16)
    lane = lax.broadcasted_iota(jnp.int32, (RANK, 128), 1)
    columns = jnp.zeros((RANK, 128), F32)
    for r in range(3):
        columns = jnp.where(lane == r, jnp.sum(sums[r], axis=1, keepdims=True), columns)
    local = jnp.transpose(columns, (1, 0))[:8]
    slab = exact_by_last(local, slab_ref[...])

    place = lax.broadcasted_iota(jnp.int32, (RANK, RANK), 1)

    def leaf(l, _):
        basis = basis_ref[l]
        transfer = transfer_ref[l]
        near = near_ref[l]
        for r in range(3):
            terms = transfer * slab[r : r + 1] + jnp.where(place == l, far_ref[r], 0.0)
            column = jnp.sum(terms, axis=1, keepdims=True)
            out_ref[r, pl.ds(l, 1), :] = jnp.sum(basis * column, axis=0, keepdims=True) + near[4 + r : 5 + r]
        return 0

    lax.fori_loop(0, LD, leaf, 0, unroll=8)


def upward(*args):
    outs = (shaped(LD, 8, LEAF), shaped(8, 8, LEAF + 128))
    scratch = [pltpu.VMEM(x.shape, F32) for x in args[1:]] + [pltpu.SemaphoreType.DMA((4 + 2 * UP_PARTS,))]
    return call(upward_kernel, outs, [SMEM] + [HBM] * 6, scratch, flops=10**9, vmem=FULL)(*args)


def near_own(wire):
    scratch = near_scratch(TALL, 3 * OWN_TURN)
    return call(near_own_kernel, shaped(LD, 8, LEAF), [VMEM], scratch, flops=9 * 10**9)(wire)


def near_side(around, *args):
    kernel = functools.partial(near_side_kernel, around)
    scratch = near_scratch(TALL + 1, 3 * OWN_TURN)
    cost = 10**8 if around < 0 else 20 * 10**6
    return call(kernel, shaped(LD, 8, LEAF), [VMEM] * 3, scratch, flops=90 * cost, bytes=cost)(*args)


def finish(*args):
    scratch = [pltpu.VMEM((3, RANK, RANK), F32), pltpu.VMEM((GROUP + 2 * REACH, ROWS, LEAF), F32)]
    return call(finish_kernel, shaped(RHS, LD, LEAF), [SMEM] * 3 + [VMEM] * 10, scratch, flops=4 * 10**9)(*args)


def passed_along(x, axis, by):
    count = lax.axis_size(axis)
    return lax.ppermute(x, axis, [(i, (i + by) % count) for i in range(count)])


def body(
    values,
    offsets,
    stiffness,
    leaf_basis,
    transfer,
    slab_transfer_matrices,
    leaf_coupling_matrices,
    leaf_admissible_mask,
    top_coupling,
    top_admissible,
):
    at = jnp.stack([lax.axis_index("along"), lax.axis_index("blk")]).astype(jnp.int32)
    sectors = lax.axis_size("blk")
    values = values[:, 0]
    offsets = offsets[:, 0]
    basis = leaf_basis[0]
    transfer = transfer[0]
    slab = slab_transfer_matrices[0, 0]

    wire, slots = upward(at, values, offsets, stiffness[0], basis, transfer, slab)
    came = lax.all_to_all(slots, "along", 0, 0, tiled=True)
    own = near_own(wire)
    came, own = lax.optimization_barrier((came, own))
    tall, rows = call(
        joined_kernel, (shaped(TALL, 8, LEAF), shaped(GROUP, ROWS, LEAF)), [SMEM, VMEM, VMEM], flops=10**8
    )(at, came, wire)
    beside = [[g * GROUP + j for j in range(GROUP)] for g in range(sectors // GROUP)]
    across = [[g * GROUP + j for g in range(sectors // GROUP)] for j in range(GROUP)]
    group = lax.all_to_all(rows, "blk", 0, 0, tiled=True, axis_index_groups=beside)
    lower = passed_along(tall, "blk", 1)
    upper = passed_along(tall, "blk", -1)
    low, high, shares = call(
        group_kernel,
        (shaped(REACH, ROWS, LEAF), shaped(REACH, ROWS, LEAF), shaped(sectors // GROUP, GROUP, LEAF)),
        [VMEM],
        flops=10**8,
    )(group)
    below = passed_along(low, "blk", GROUP)
    above = passed_along(high, "blk", -GROUP)
    every = lax.all_to_all(shares, "blk", 0, 0, tiled=True, axis_index_groups=across)
    near = near_side(-1, tall, lower, own)
    every, upper, near = lax.optimization_barrier((every, upper, near))
    near = near_side(1, tall, upper, near)
    out = finish(
        at, leaf_admissible_mask, top_admissible, group, below, above, near, every.reshape(sectors, LEAF),
        slab, leaf_coupling_matrices[0], top_coupling[0], transfer, basis,
    )
    return out[:, None]


def solution(mesh):
    return jax.shard_map(
        body,
        mesh=mesh,
        in_specs=(
            P(None, "blk", "along", None),
            P(None, "blk", "along", None),
            P("blk", "along", None),
            P("blk", "along", None, None),
            P("blk", "along", None, None),
            P("blk", "along", None, None),
            P("blk", None, None, None),
            P("blk", None),
            P("blk", None, None, None),
            P("blk", None),
        ),
        out_specs=P(None, "blk", "along", None),
        check_vma=False,
    )
```

```python
import functools
import math

import jax
import jax.numpy as jnp
from jax import lax
from jax.experimental import pallas as pl
from jax.experimental.pallas import tpu as pltpu
from jax.sharding import PartitionSpec as P

REACH = 6
LEAF = 256
RANK = 64
RHS = 3
LD = 24
TALL = LD + 2
ROWS = 32
PACKED = 40
SHARPNESS = 2.0
KERNEL_SCALE = 0.125
LOG2E = math.log2(math.e)
F32 = jnp.float32
BF16 = jnp.bfloat16
EXACT = lax.Precision.HIGHEST
VMEM = pl.BlockSpec(memory_space=pltpu.VMEM)
HBM = pl.BlockSpec(memory_space=pltpu.HBM)
SMEM = pl.BlockSpec(memory_space=pltpu.SMEM)
BY_LAST = (((1,), (1,)), ((), ()))
MIB = 2**20
FULL = 60 * MIB + 128 * 1024
OWN_TURN = 3
CROSS_TURN = 2
UP_PARTS = 4
UP_LEAVES = LD // UP_PARTS


def call(kernel, outs, ins, scratch=(), flops=0, bytes=1 << 20, vmem=16 * MIB):
    return pl.pallas_call(
        kernel,
        out_shape=outs,
        in_specs=ins,
        out_specs=jax.tree.map(lambda _: VMEM, outs),
        scratch_shapes=list(scratch),
        compiler_params=pltpu.CompilerParams(vmem_limit_bytes=vmem),
        cost_estimate=pl.CostEstimate(flops=flops, bytes_accessed=bytes, transcendentals=0),
    )


def shaped(*shape):
    return jax.ShapeDtypeStruct(shape, F32)


def halves(x):
    high = x.astype(BF16).astype(F32)
    return high, x - high


def upward_kernel(
    at_ref, values_hbm, offsets_hbm, stiffness_hbm, basis_hbm, transfer_hbm, slab_hbm, wire_ref, slots_ref,
    values_ref, offsets_ref, stiffness_ref, basis_ref, transfer_ref, slab_ref, sems,
):
    lane = lax.broadcasted_iota(jnp.int32, (RANK, 128), 1)
    small = [
        pltpu.make_async_copy(source, target, sems.at[n])
        for n, (source, target) in enumerate(
            ((values_hbm, values_ref), (offsets_hbm, offsets_ref), (stiffness_hbm, stiffness_ref), (slab_hbm, slab_ref))
        )
    ]
    large = []
    for part in range(UP_PARTS):
        piece = pl.ds(part * UP_LEAVES, UP_LEAVES)
        large.append(
            [
                pltpu.make_async_copy(source.at[piece], target.at[piece], sems.at[4 + 2 * part + n])
                for n, (source, target) in enumerate(((basis_hbm, basis_ref), (transfer_hbm, transfer_ref)))
            ]
        )
    for copy in small + [copy for pair in large for copy in pair]:
        copy.start()
    for copy in small:
        copy.wait()

    def record(l, _):
        row = pl.ds(l, 1)
        for r in range(3):
            wire_ref[l, r : r + 1, :] = offsets_ref[r, row, :] - 0.5
            wire_ref[l, 4 + r : 5 + r, :] = values_ref[r, row, :]
        wire_ref[l, 3:4, :] = stiffness_ref[row, :]
        return 0

    lax.fori_loop(0, LD, record, 0, unroll=4)

    def leaf(l, carry):
        sums, columns = carry
        row = pl.ds(l, 1)
        new_sums = []
        basis = basis_ref[l]
        transfer = transfer_ref[l]
        for r in range(3):
            column = jnp.sum(basis * values_ref[r, row, :], axis=1, keepdims=True)
            new_sums.append(sums[r] + transfer * column)
            columns = jnp.where(lane == r * ROWS + l, column, columns)
        return tuple(new_sums), columns

    nothing = jnp.zeros((RANK, RANK), F32)
    carry = ((nothing,) * 3, jnp.zeros((RANK, 128), F32))
    for part in range(UP_PARTS):
        for copy in large[part]:
            copy.wait()
        carry = lax.fori_loop(part * UP_LEAVES, (part + 1) * UP_LEAVES, leaf, carry, unroll=UP_LEAVES)
    sums, columns = carry
    rows = jnp.transpose(columns, (1, 0))
    coefs = jnp.concatenate(
        [rows[:LD], rows[ROWS : ROWS + LD], rows[2 * ROWS : 2 * ROWS + LD], jnp.zeros((LD, RANK), F32)], 1
    )
    for l in range(LD):
        wire_ref[l, 7:8, :] = coefs[l : l + 1]
    slab_rows = jnp.concatenate(
        [jnp.sum(s, axis=0, keepdims=True) for s in sums] + [jnp.zeros((5, RANK), F32)], 0
    )
    share = jnp.dot(slab_rows, slab_ref[...], precision=EXACT, preferred_element_type=F32)
    share = jnp.concatenate([share, jnp.zeros((8, 128 - RANK), F32)], 1)
    here = at_ref[0]
    for j in range(8):
        slots_ref[j, :, :LEAF] = jnp.where(j < here, wire_ref[0], wire_ref[LD - 1])
        slots_ref[j, :, LEAF:] = share


def joined_kernel(at_ref, came_ref, wire_ref, tall_ref, whole_ref):
    here = at_ref[0]
    total = came_ref[0, :, LEAF:]
    for j in range(1, 8):
        total = total + came_ref[j, :, LEAF:]
    packed = jnp.concatenate(
        [
            jnp.concatenate([total[0:1, :RANK], total[1:2, :RANK]], 1),
            jnp.concatenate([total[2:3, :RANK], jnp.zeros((1, RANK), F32)], 1),
        ],
        0,
    )
    whole_ref[...] = jnp.broadcast_to(packed[None], whole_ref.shape)
    lower = came_ref[jnp.maximum(here - 1, 0), :, :LEAF]
    upper = came_ref[jnp.minimum(here + 1, 7), :, :LEAF]
    tall_ref[0] = jnp.where(here > 0, lower, 0.0)
    tall_ref[1 : LD + 1] = wire_ref[...]
    tall_ref[LD + 1] = jnp.where(here < 7, upper, 0.0)


def source_side(leaf, around, steps, slot, points_ref, loads_ref):
    high, low = halves(leaf)
    points_ref[slot] = jnp.transpose(jnp.concatenate([high, low, low, high], 0), (1, 0)).astype(BF16)
    c0, c1, c2 = leaf[0:1], leaf[1:2], leaf[2:3]
    flat = (c0 + around) * (c0 + around) + c2 * c2
    for step in steps:
        weight = jnp.exp2((-SHARPNESS * LOG2E) * (flat + (c1 + step) * (c1 + step))) * leaf[3:4]
        loads_ref[slot, step + 1] = jnp.concatenate(halves(leaf * weight), 0).astype(BF16)


def target_points(leaf):
    row = lax.broadcasted_iota(jnp.int32, leaf.shape, 0)
    high, low = halves(jnp.where(row < 3, leaf * (2 * SHARPNESS * LOG2E), 0.0))
    return jnp.concatenate([high, low, high, low], 0).astype(BF16)


def pair_kernel(target, points_ref, slot, pairs_ref, place):
    power = jnp.dot(points_ref[slot], target, preferred_element_type=F32)
    pair = jnp.exp2(power)
    high = pair.astype(BF16)
    pairs_ref[place, 0] = high
    pairs_ref[place, 1] = (pair - high.astype(F32)).astype(BF16)


def pair_sum(leaf, loads_ref, slot, pairs_ref, place, around, step):
    c0, c1, c2 = leaf[0:1], leaf[1:2], leaf[2:3]
    loads = loads_ref[slot, step + 1]
    rows = jnp.dot(loads, pairs_ref[place, 0], preferred_element_type=F32) + jnp.dot(
        loads, pairs_ref[place, 1], preferred_element_type=F32
    )
    power = (2 * SHARPNESS * LOG2E) * (around * c0 + step * c1) - (SHARPNESS * LOG2E) * (c0 * c0 + c1 * c1 + c2 * c2)
    weight = jnp.exp2(power) * (KERNEL_SCALE * leaf[3:4])
    return weight * (rows[:8] + rows[8:])


def near_own_kernel(wire_ref, near_ref, points_ref, loads_ref, pairs_ref):
    points_ref[0] = jnp.zeros((LEAF, 32), BF16)
    points_ref[LD + 1] = jnp.zeros((LEAF, 32), BF16)
    loads_ref[0] = jnp.zeros((3, 16, LEAF), BF16)
    loads_ref[LD + 1] = jnp.zeros((3, 16, LEAF), BF16)

    def prepare(l, _):
        source_side(wire_ref[l], 0, (-1, 0, 1), l + 1, points_ref, loads_ref)
        return 0

    lax.fori_loop(0, LD, prepare, 0, unroll=12)

    def turn(g, _):
        leaves = [g * OWN_TURN + n for n in range(OWN_TURN)]
        places = [(n, step) for n in range(OWN_TURN) for step in (-1, 0, 1)]
        targets = [target_points(wire_ref[l]) for l in leaves]
        for place, (n, step) in enumerate(places):
            pair_kernel(targets[n], points_ref, leaves[n] + 1 + step, pairs_ref, place)
        totals = [jnp.zeros((8, LEAF), F32)] * OWN_TURN
        for place, (n, step) in enumerate(places):
            totals[n] += pair_sum(wire_ref[leaves[n]], loads_ref, leaves[n] + 1 + step, pairs_ref, place, 0, step)
        for n in range(OWN_TURN):
            near_ref[leaves[n]] = totals[n]
        return 0

    lax.fori_loop(0, LD // OWN_TURN, turn, 0)


def near_cross_kernel(tall_ref, lower_ref, upper_ref, near_ref, points_ref, loads_ref, pairs_ref):
    for around, came_ref, base in ((-1, lower_ref, 0), (1, upper_ref, TALL)):

        def prepare(l, _, around=around, came_ref=came_ref, base=base):
            source_side(came_ref[l], around, (-1, 0, 1), base + l, points_ref, loads_ref)
            return 0

        lax.fori_loop(0, TALL, prepare, 0, unroll=13)
    source_side(tall_ref[0], 0, (-1,), 2 * TALL, points_ref, loads_ref)
    source_side(tall_ref[LD + 1], 0, (1,), 2 * TALL + 1, points_ref, loads_ref)

    def turn(g, _):
        leaves = [g * CROSS_TURN + n for n in range(CROSS_TURN)]
        places = [
            (n, around, base, step)
            for n in range(CROSS_TURN)
            for around, base in ((-1, 0), (1, TALL))
            for step in (-1, 0, 1)
        ]
        targets = [target_points(tall_ref[l + 1]) for l in leaves]
        for place, (n, around, base, step) in enumerate(places):
            pair_kernel(targets[n], points_ref, base + leaves[n] + 1 + step, pairs_ref, place)
        totals = [jnp.zeros((8, LEAF), F32)] * CROSS_TURN
        for place, (n, around, base, step) in enumerate(places):
            slot = base + leaves[n] + 1 + step
            totals[n] += pair_sum(tall_ref[leaves[n] + 1], loads_ref, slot, pairs_ref, place, around, step)
        for n in range(CROSS_TURN):
            near_ref[leaves[n]] = totals[n]
        return 0

    lax.fori_loop(0, LD // CROSS_TURN, turn, 0)
    for l, slot, step in ((0, 2 * TALL, -1), (LD - 1, 2 * TALL + 1, 1)):
        here = tall_ref[l + 1]
        pair_kernel(target_points(here), points_ref, slot, pairs_ref, 0)
        near_ref[l] += pair_sum(here, loads_ref, slot, pairs_ref, 0, 0, step)


def near_scratch(leaves, places):
    return [
        pltpu.VMEM((leaves, LEAF, 32), BF16),
        pltpu.VMEM((leaves, 3, 16, LEAF), BF16),
        pltpu.VMEM((places, 2, LEAF, LEAF), BF16),
    ]


def window_kernel(lower_ref, tall_ref, upper_ref, window_ref, head_ref, tail_ref):
    for i, came_ref in enumerate((lower_ref, tall_ref, upper_ref)):
        rows = jnp.concatenate([came_ref[l, 7:8, :] for l in range(TALL)], 0)
        third = rows[:, 2 * RANK : 3 * RANK]
        third = jnp.concatenate([third[: TALL // 2], third[TALL // 2 :]], 1)
        packed = jnp.concatenate([rows[:, : 2 * RANK], third, jnp.zeros((PACKED - TALL - TALL // 2, 128), F32)], 0)
        window_ref[i] = packed
        if i < 2:
            head_ref[i] = packed
        if i > 0:
            tail_ref[i - 1] = packed


def exact_by_last(x, y):
    return lax.dot_general(x, y, BY_LAST, precision=EXACT, preferred_element_type=F32)


def three_by_last(x, y):
    (xh, xl), (yh, yl) = halves(x), halves(y)
    xh, xl, yh, yl = (z.astype(BF16) for z in (xh, xl, yh, yl))
    high = lax.dot_general(xh, yh, BY_LAST, preferred_element_type=F32)
    cross = lax.dot_general(xl, yh, BY_LAST, preferred_element_type=F32)
    return high + (cross + lax.dot_general(xh, yl, BY_LAST, preferred_element_type=F32))


def finish_kernel(at_ref, mask_ref, admissible_ref, *refs):
    count = (len(refs) - 3) // 2
    held_in, out_ref, local = refs[:count], refs[count], refs[count + 1 : 2 * count + 1]
    far_ref, sems = refs[2 * count + 1 :]
    copies = [pltpu.make_async_copy(held_in[n], local[n], sems.at[n]) for n in range(count)]
    for copy in copies:
        copy.start()
    (coupling_ref, below_ref, above_ref, far_below_ref, far_above_ref) = local[:5]
    (top_ref, every_ref, slab_ref, transfer_ref, basis_ref, own_ref, cross_ref) = local[5:]

    for copy in copies[:5]:
        copy.wait()
    held = {-4 + i: below_ref[i] for i in range(3)}
    held |= {2 + i: above_ref[i] for i in range(3)}
    held |= {-6 + i: far_below_ref[i] for i in range(2)}
    held |= {5 + i: far_above_ref[i] for i in range(2)}
    total = jnp.zeros((3 * ROWS, 3 * RANK), F32)
    for q in range(2 * (REACH - 1)):
        around = q + 2 if q < REACH - 1 else 3 - q
        rows = held[around]
        gap = jnp.zeros((ROWS - TALL, RANK), F32)
        third = rows[TALL : TALL + TALL // 2]
        stacked = jnp.concatenate(
            [rows[:TALL, :RANK], gap, rows[:TALL, RANK:], gap, third[:, :RANK], third[:, RANK:], gap], 0
        )
        coupling = jnp.concatenate(
            [coupling_ref[3 * q + b] * mask_ref[0, 3 * q + b].astype(F32) for b in range(3)], 0
        )
        total = total + three_by_last(stacked, coupling)
    far = []
    for r in range(3):
        block = total[r * ROWS : (r + 1) * ROWS]
        rows = block[0:LD, :RANK] + block[1 : LD + 1, RANK : 2 * RANK] + block[2 : LD + 2, 2 * RANK :]
        far.append(jnp.concatenate([rows, jnp.zeros((ROWS - LD, RANK), F32)], 0))
    far.append(jnp.zeros((ROWS, RANK), F32))
    columns = jnp.transpose(jnp.concatenate(far, 0), (1, 0))
    far_columns = [columns[:, r * ROWS : (r + 1) * ROWS] for r in range(3)]
    for r in range(3):
        far_ref[r] = jnp.concatenate([far_columns[r], jnp.zeros((RANK, RANK - ROWS), F32)], 1)

    here = at_ref[1]
    sectors = top_ref.shape[0]

    def couple(t, sums):
        apart = lax.rem(t - here + sectors, sectors)
        distant = jnp.logical_and(apart > REACH, apart < sectors - REACH)
        allowed = jnp.where(distant, admissible_ref[0, t], 0).astype(F32)
        coupling = top_ref[t]
        both = every_ref[t] * allowed
        rows = (both[0:1, :RANK], both[0:1, RANK:], both[1:2, :RANK])
        return tuple(s + coupling * row for s, row in zip(sums, rows))

    for copy in copies[5:8]:
        copy.wait()
    nothing = jnp.zeros((RANK, RANK), F32)
    sums = lax.fori_loop(0, sectors, couple, (nothing,) * 3, unroll=16)
    lane = lax.broadcasted_iota(jnp.int32, (RANK, 128), 1)
    columns = jnp.zeros((RANK, 128), F32)
    for r in range(3):
        columns = jnp.where(lane == r, jnp.sum(sums[r], axis=1, keepdims=True), columns)
    local = jnp.transpose(columns, (1, 0))[:8]
    slab = exact_by_last(local, slab_ref[...])

    for copy in copies[8:]:
        copy.wait()
    place = lax.broadcasted_iota(jnp.int32, (RANK, RANK), 1)

    def leaf(l, _):
        basis = basis_ref[l]
        transfer = transfer_ref[l]
        near = own_ref[l] + cross_ref[l]
        for r in range(3):
            terms = transfer * slab[r : r + 1] + jnp.where(place == l, far_ref[r], 0.0)
            column = jnp.sum(terms, axis=1, keepdims=True)
            out_ref[r, pl.ds(l, 1), :] = jnp.sum(basis * column, axis=0, keepdims=True) + near[4 + r : 5 + r]
        return 0

    lax.fori_loop(0, LD, leaf, 0, unroll=8)


def upward(*args):
    outs = (shaped(LD, 8, LEAF), shaped(8, 8, LEAF + 128))
    scratch = [pltpu.VMEM(x.shape, F32) for x in args[1:]] + [pltpu.SemaphoreType.DMA((4 + 2 * UP_PARTS,))]
    return call(upward_kernel, outs, [SMEM] + [HBM] * 6, scratch, flops=10**9, vmem=FULL)(*args)


def near_own(wire):
    scratch = near_scratch(TALL, 3 * OWN_TURN)
    return call(near_own_kernel, shaped(LD, 8, LEAF), [VMEM], scratch, flops=9 * 10**9)(wire)


def near_cross(*args):
    scratch = near_scratch(2 * TALL + 2, 6 * CROSS_TURN)
    return call(near_cross_kernel, shaped(LD, 8, LEAF), [VMEM] * 3, scratch, flops=18 * 10**9, bytes=10**8)(*args)


def finish(*args):
    held = args[3:]
    scratch = [pltpu.VMEM(x.shape, F32) for x in held]
    scratch += [pltpu.VMEM((3, RANK, RANK), F32), pltpu.SemaphoreType.DMA((len(held),))]
    ins = [SMEM] * 3 + [HBM] * len(held)
    return call(finish_kernel, shaped(RHS, LD, LEAF), ins, scratch, flops=4 * 10**9, vmem=FULL)(*args)


def passed_along(x, axis, by):
    count = lax.axis_size(axis)
    return lax.ppermute(x, axis, [(i, (i + by) % count) for i in range(count)])


def body(
    values,
    offsets,
    stiffness,
    leaf_basis,
    transfer,
    slab_transfer_matrices,
    leaf_coupling_matrices,
    leaf_admissible_mask,
    top_coupling,
    top_admissible,
):
    at = jnp.stack([lax.axis_index("along"), lax.axis_index("blk")]).astype(jnp.int32)
    sectors = lax.axis_size("blk")
    values = values[:, 0]
    offsets = offsets[:, 0]
    basis = leaf_basis[0]
    transfer = transfer[0]
    slab = slab_transfer_matrices[0, 0]

    wire, slots = upward(at, values, offsets, stiffness[0], basis, transfer, slab)
    came = lax.all_to_all(slots, "along", 0, 0, tiled=True)
    own = near_own(wire)
    came, own = lax.optimization_barrier((came, own))
    tall, whole = call(
        joined_kernel, (shaped(TALL, 8, LEAF), shaped(sectors, 2, 128)), [SMEM, VMEM, VMEM], flops=10**8
    )(at, came, wire)
    lower = passed_along(tall, "blk", 1)
    upper = passed_along(tall, "blk", -1)
    every = lax.all_to_all(whole, "blk", 0, 0, tiled=True)
    window, head, tail = call(
        window_kernel,
        (shaped(3, PACKED, 128), shaped(2, PACKED, 128), shaped(2, PACKED, 128)),
        [VMEM] * 3,
        flops=10**8,
    )(lower, tall, upper)
    below = passed_along(window, "blk", 3)
    above = passed_along(window, "blk", -3)
    far_below = passed_along(head, "blk", 5)
    far_above = passed_along(tail, "blk", -5)
    cross = near_cross(tall, lower, upper)
    out = finish(
        at, leaf_admissible_mask, top_admissible, leaf_coupling_matrices[0], below, above, far_below, far_above,
        top_coupling[0], every, slab, transfer, basis, own, cross,
    )
    return out[:, None]


def solution(mesh):
    return jax.shard_map(
        body,
        mesh=mesh,
        in_specs=(
            P(None, "blk", "along", None),
            P(None, "blk", "along", None),
            P("blk", "along", None),
            P("blk", "along", None, None),
            P("blk", "along", None, None),
            P("blk", "along", None, None),
            P("blk", None, None, None),
            P("blk", None),
            P("blk", None, None, None),
            P("blk", None),
        ),
        out_specs=P(None, "blk", "along", None),
        check_vma=False,
    )
```

```python
import functools
import math

import jax
import jax.numpy as jnp
from jax import lax
from jax.experimental import pallas as pl
from jax.experimental.pallas import tpu as pltpu
from jax.sharding import PartitionSpec as P

REACH = 6
LEAF = 256
RANK = 64
RHS = 3
LD = 24
TALL = LD + 2
ROWS = 32
PACKED = 40
SHARPNESS = 2.0
KERNEL_SCALE = 0.125
LOG2E = math.log2(math.e)
F32 = jnp.float32
BF16 = jnp.bfloat16
EXACT = lax.Precision.HIGHEST
VMEM = pl.BlockSpec(memory_space=pltpu.VMEM)
HBM = pl.BlockSpec(memory_space=pltpu.HBM)
SMEM = pl.BlockSpec(memory_space=pltpu.SMEM)
BY_LAST = (((1,), (1,)), ((), ()))
MIB = 2**20
FULL = 60 * MIB + 128 * 1024
OWN_TURN = 3
UP_PARTS = 4
UP_LEAVES = LD // UP_PARTS


def call(kernel, outs, ins, scratch=(), flops=0, bytes=1 << 20, vmem=16 * MIB):
    return pl.pallas_call(
        kernel,
        out_shape=outs,
        in_specs=ins,
        out_specs=jax.tree.map(lambda _: VMEM, outs),
        scratch_shapes=list(scratch),
        compiler_params=pltpu.CompilerParams(vmem_limit_bytes=vmem),
        cost_estimate=pl.CostEstimate(flops=flops, bytes_accessed=bytes, transcendentals=0),
    )


def shaped(*shape):
    return jax.ShapeDtypeStruct(shape, F32)


def halves(x):
    high = x.astype(BF16).astype(F32)
    return high, x - high


def upward_kernel(
    at_ref, values_hbm, offsets_hbm, stiffness_hbm, basis_hbm, transfer_hbm, slab_hbm, wire_ref, slots_ref,
    values_ref, offsets_ref, stiffness_ref, basis_ref, transfer_ref, slab_ref, sems,
):
    lane = lax.broadcasted_iota(jnp.int32, (RANK, 128), 1)
    small = [
        pltpu.make_async_copy(source, target, sems.at[n])
        for n, (source, target) in enumerate(
            ((values_hbm, values_ref), (offsets_hbm, offsets_ref), (stiffness_hbm, stiffness_ref), (slab_hbm, slab_ref))
        )
    ]
    large = []
    for part in range(UP_PARTS):
        piece = pl.ds(part * UP_LEAVES, UP_LEAVES)
        large.append(
            [
                pltpu.make_async_copy(source.at[piece], target.at[piece], sems.at[4 + 2 * part + n])
                for n, (source, target) in enumerate(((basis_hbm, basis_ref), (transfer_hbm, transfer_ref)))
            ]
        )
    for copy in small + [copy for pair in large for copy in pair]:
        copy.start()
    for copy in small:
        copy.wait()

    def record(l, _):
        row = pl.ds(l, 1)
        for r in range(3):
            wire_ref[l, r : r + 1, :] = offsets_ref[r, row, :] - 0.5
            wire_ref[l, 4 + r : 5 + r, :] = values_ref[r, row, :]
        wire_ref[l, 3:4, :] = stiffness_ref[row, :]
        return 0

    lax.fori_loop(0, LD, record, 0, unroll=4)

    def leaf(l, carry):
        sums, columns = carry
        row = pl.ds(l, 1)
        new_sums = []
        basis = basis_ref[l]
        transfer = transfer_ref[l]
        for r in range(3):
            column = jnp.sum(basis * values_ref[r, row, :], axis=1, keepdims=True)
            new_sums.append(sums[r] + transfer * column)
            columns = jnp.where(lane == r * ROWS + l, column, columns)
        return tuple(new_sums), columns

    nothing = jnp.zeros((RANK, RANK), F32)
    carry = ((nothing,) * 3, jnp.zeros((RANK, 128), F32))
    for part in range(UP_PARTS):
        for copy in large[part]:
            copy.wait()
        carry = lax.fori_loop(part * UP_LEAVES, (part + 1) * UP_LEAVES, leaf, carry, unroll=UP_LEAVES)
    sums, columns = carry
    rows = jnp.transpose(columns, (1, 0))
    coefs = jnp.concatenate(
        [rows[:LD], rows[ROWS : ROWS + LD], rows[2 * ROWS : 2 * ROWS + LD], jnp.zeros((LD, RANK), F32)], 1
    )
    for l in range(LD):
        wire_ref[l, 7:8, :] = coefs[l : l + 1]
    slab_rows = jnp.concatenate(
        [jnp.sum(s, axis=0, keepdims=True) for s in sums] + [jnp.zeros((5, RANK), F32)], 0
    )
    share = jnp.dot(slab_rows, slab_ref[...], precision=EXACT, preferred_element_type=F32)
    share = jnp.concatenate([share, jnp.zeros((8, 128 - RANK), F32)], 1)
    here = at_ref[0]
    for j in range(8):
        slots_ref[j, :, :LEAF] = jnp.where(j < here, wire_ref[0], wire_ref[LD - 1])
        slots_ref[j, :, LEAF:] = share


def joined_kernel(at_ref, came_ref, wire_ref, tall_ref, whole_ref):
    here = at_ref[0]
    total = came_ref[0, :, LEAF:]
    for j in range(1, 8):
        total = total + came_ref[j, :, LEAF:]
    packed = jnp.concatenate(
        [
            jnp.concatenate([total[0:1, :RANK], total[1:2, :RANK]], 1),
            jnp.concatenate([total[2:3, :RANK], jnp.zeros((1, RANK), F32)], 1),
        ],
        0,
    )
    whole_ref[...] = jnp.broadcast_to(packed[None], whole_ref.shape)
    lower = came_ref[jnp.maximum(here - 1, 0), :, :LEAF]
    upper = came_ref[jnp.minimum(here + 1, 7), :, :LEAF]
    tall_ref[0] = jnp.where(here > 0, lower, 0.0)
    tall_ref[1 : LD + 1] = wire_ref[...]
    tall_ref[LD + 1] = jnp.where(here < 7, upper, 0.0)


def source_side(leaf, around, steps, slot, points_ref, loads_ref):
    high, low = halves(leaf)
    points_ref[slot] = jnp.transpose(jnp.concatenate([high, low, low, high], 0), (1, 0)).astype(BF16)
    c0, c1, c2 = leaf[0:1], leaf[1:2], leaf[2:3]
    flat = (c0 + around) * (c0 + around) + c2 * c2
    for step in steps:
        weight = jnp.exp2((-SHARPNESS * LOG2E) * (flat + (c1 + step) * (c1 + step))) * leaf[3:4]
        loads_ref[slot, step + 1] = jnp.concatenate(halves(leaf * weight), 0).astype(BF16)


def target_points(leaf):
    row = lax.broadcasted_iota(jnp.int32, leaf.shape, 0)
    high, low = halves(jnp.where(row < 3, leaf * (2 * SHARPNESS * LOG2E), 0.0))
    return jnp.concatenate([high, low, high, low], 0).astype(BF16)


def pair_kernel(target, points_ref, slot, pairs_ref, place):
    power = jnp.dot(points_ref[slot], target, preferred_element_type=F32)
    pair = jnp.exp2(power)
    high = pair.astype(BF16)
    pairs_ref[place, 0] = high
    pairs_ref[place, 1] = (pair - high.astype(F32)).astype(BF16)


def pair_sum(leaf, loads_ref, slot, pairs_ref, place, around, step):
    c0, c1, c2 = leaf[0:1], leaf[1:2], leaf[2:3]
    loads = loads_ref[slot, step + 1]
    rows = jnp.dot(loads, pairs_ref[place, 0], preferred_element_type=F32) + jnp.dot(
        loads, pairs_ref[place, 1], preferred_element_type=F32
    )
    power = (2 * SHARPNESS * LOG2E) * (around * c0 + step * c1) - (SHARPNESS * LOG2E) * (c0 * c0 + c1 * c1 + c2 * c2)
    weight = jnp.exp2(power) * (KERNEL_SCALE * leaf[3:4])
    return weight * (rows[:8] + rows[8:])


def near_own_kernel(wire_ref, near_ref, points_ref, loads_ref, pairs_ref):
    points_ref[0] = jnp.zeros((LEAF, 32), BF16)
    points_ref[LD + 1] = jnp.zeros((LEAF, 32), BF16)
    loads_ref[0] = jnp.zeros((3, 16, LEAF), BF16)
    loads_ref[LD + 1] = jnp.zeros((3, 16, LEAF), BF16)

    def prepare(l, _):
        source_side(wire_ref[l], 0, (-1, 0, 1), l + 1, points_ref, loads_ref)
        return 0

    lax.fori_loop(0, LD, prepare, 0, unroll=12)

    def turn(g, _):
        leaves = [g * OWN_TURN + n for n in range(OWN_TURN)]
        places = [(n, step) for n in range(OWN_TURN) for step in (-1, 0, 1)]
        targets = [target_points(wire_ref[l]) for l in leaves]
        for place, (n, step) in enumerate(places):
            pair_kernel(targets[n], points_ref, leaves[n] + 1 + step, pairs_ref, place)
        totals = [jnp.zeros((8, LEAF), F32)] * OWN_TURN
        for place, (n, step) in enumerate(places):
            totals[n] += pair_sum(wire_ref[leaves[n]], loads_ref, leaves[n] + 1 + step, pairs_ref, place, 0, step)
        for n in range(OWN_TURN):
            near_ref[leaves[n]] = totals[n]
        return 0

    lax.fori_loop(0, LD // OWN_TURN, turn, 0)


def near_side_kernel(beyond, at_ref, tall_ref, came_ref, near_ref, points_ref, loads_ref, pairs_ref):
    odd = lax.rem(at_ref[1], 2)
    around = ((2 * odd - 1) if beyond else (1 - 2 * odd)).astype(F32)

    def prepare(l, _):
        source_side(came_ref[l], around, (-1, 0, 1), l, points_ref, loads_ref)
        return 0

    lax.fori_loop(0, TALL, prepare, 0, unroll=13)
    end, end_leaf, end_step = (LD + 1, LD - 1, 1) if beyond else (0, 0, -1)
    source_side(tall_ref[end], 0, (end_step,), TALL, points_ref, loads_ref)

    def turn(g, _):
        leaves = [g * OWN_TURN + n for n in range(OWN_TURN)]
        places = [(n, step) for n in range(OWN_TURN) for step in (-1, 0, 1)]
        targets = [target_points(tall_ref[l + 1]) for l in leaves]
        for place, (n, step) in enumerate(places):
            pair_kernel(targets[n], points_ref, leaves[n] + 1 + step, pairs_ref, place)
        totals = [jnp.zeros((8, LEAF), F32)] * OWN_TURN
        for place, (n, step) in enumerate(places):
            slot = leaves[n] + 1 + step
            totals[n] += pair_sum(tall_ref[leaves[n] + 1], loads_ref, slot, pairs_ref, place, around, step)
        for n in range(OWN_TURN):
            near_ref[leaves[n]] = totals[n]
        return 0

    lax.fori_loop(0, LD // OWN_TURN, turn, 0)
    here = tall_ref[end_leaf + 1]
    pair_kernel(target_points(here), points_ref, TALL, pairs_ref, 0)
    near_ref[end_leaf] += pair_sum(here, loads_ref, TALL, pairs_ref, 0, 0, end_step)


def near_scratch(leaves, places):
    return [
        pltpu.VMEM((leaves, LEAF, 32), BF16),
        pltpu.VMEM((leaves, 3, 16, LEAF), BF16),
        pltpu.VMEM((places, 2, LEAF, LEAF), BF16),
    ]


def packed(rows):
    third = rows[:, 2 * RANK : 3 * RANK]
    third = jnp.concatenate([third[: TALL // 2], third[TALL // 2 :]], 1)
    return jnp.concatenate([rows[:, : 2 * RANK], third, jnp.zeros((PACKED - TALL - TALL // 2, 128), F32)], 0)


def coefs_of(tall_ref):
    return jnp.concatenate([tall_ref[l, 7:8, :] for l in range(TALL)], 0)


def pair_records_kernel(tall_ref, partner_ref, records_ref):
    records_ref[:TALL] = tall_ref[...]
    rows = jnp.concatenate([coefs_of(partner_ref), jnp.zeros((ROWS - TALL, LEAF), F32)], 0)
    for n in range(ROWS // 8):
        records_ref[TALL + n] = rows[8 * n : 8 * n + 8]


def beside_kernel(at_ref, came_ref, beside_ref):
    even = lax.rem(at_ref[1], 2) == 0
    first = packed(coefs_of(came_ref))
    second = packed(jnp.concatenate([came_ref[TALL + n] for n in range(ROWS // 8)], 0)[:TALL])
    beside_ref[0] = jnp.where(even, second, first)
    beside_ref[1] = jnp.where(even, first, second)


def window_kernel(at_ref, tall_ref, partner_ref, beside_ref, other_ref, window_ref, onward_ref):
    even = lax.rem(at_ref[1], 2) == 0
    own, partner = packed(coefs_of(tall_ref)), packed(coefs_of(partner_ref))
    beside, other = [beside_ref[n] for n in range(2)], [other_ref[n] for n in range(2)]
    low = [jnp.where(even, beside[n], other[n]) for n in range(2)]
    high = [jnp.where(even, other[n], beside[n]) for n in range(2)]
    window = low + [jnp.where(even, own, partner), jnp.where(even, partner, own)] + high
    for n in range(6):
        window_ref[n] = window[n]
    for n in range(4):
        onward_ref[n] = jnp.where(even, window[n + 2], window[n])


def exact_by_last(x, y):
    return lax.dot_general(x, y, BY_LAST, precision=EXACT, preferred_element_type=F32)


def three_by_last(x, y):
    (xh, xl), (yh, yl) = halves(x), halves(y)
    xh, xl, yh, yl = (z.astype(BF16) for z in (xh, xl, yh, yl))
    high = lax.dot_general(xh, yh, BY_LAST, preferred_element_type=F32)
    cross = lax.dot_general(xl, yh, BY_LAST, preferred_element_type=F32)
    return high + (cross + lax.dot_general(xh, yl, BY_LAST, preferred_element_type=F32))


def finish_kernel(at_ref, mask_ref, admissible_ref, *refs):
    count = len(refs) - 3
    local, out_ref = refs[:count], refs[count]
    far_ref, ring_ref = refs[count + 1 :]
    coupling_ref, window_ref, onward_ref, back_ref = local[:4]
    top_ref, every_ref, slab_ref, transfer_ref, basis_ref, own_ref, side_ref, beyond_ref = local[4:]

    here = at_ref[1]
    odd = lax.rem(here, 2)
    for n in range(4):
        ring_ref[n] = jnp.where(odd == 0, onward_ref[n], back_ref[n])
        ring_ref[n + 10] = jnp.where(odd == 0, back_ref[n], onward_ref[n])
    for n in range(6):
        ring_ref[n + 4] = window_ref[n]
    total = jnp.zeros((3 * ROWS, 3 * RANK), F32)
    for q in range(2 * (REACH - 1)):
        around = q + 2 if q < REACH - 1 else 3 - q
        rows = ring_ref[odd + (REACH + around)]
        gap = jnp.zeros((ROWS - TALL, RANK), F32)
        third = rows[TALL : TALL + TALL // 2]
        stacked = jnp.concatenate(
            [rows[:TALL, :RANK], gap, rows[:TALL, RANK:], gap, third[:, :RANK], third[:, RANK:], gap], 0
        )
        coupling = jnp.concatenate(
            [coupling_ref[3 * q + b] * mask_ref[0, 3 * q + b].astype(F32) for b in range(3)], 0
        )
        total = total + three_by_last(stacked, coupling)
    far = []
    for r in range(3):
        block = total[r * ROWS : (r + 1) * ROWS]
        rows = block[0:LD, :RANK] + block[1 : LD + 1, RANK : 2 * RANK] + block[2 : LD + 2, 2 * RANK :]
        far.append(jnp.concatenate([rows, jnp.zeros((ROWS - LD, RANK), F32)], 0))
    far.append(jnp.zeros((ROWS, RANK), F32))
    columns = jnp.transpose(jnp.concatenate(far, 0), (1, 0))
    far_columns = [columns[:, r * ROWS : (r + 1) * ROWS] for r in range(3)]
    for r in range(3):
        far_ref[r] = jnp.concatenate([far_columns[r], jnp.zeros((RANK, RANK - ROWS), F32)], 1)

    sectors = top_ref.shape[0]

    def couple(t, sums):
        apart = lax.rem(t - here + sectors, sectors)
        distant = jnp.logical_and(apart > REACH, apart < sectors - REACH)
        allowed = jnp.where(distant, admissible_ref[0, t], 0).astype(F32)
        coupling = top_ref[t]
        both = every_ref[t] * allowed
        rows = (both[0:1, :RANK], both[0:1, RANK:], both[1:2, :RANK])
        return tuple(s + coupling * row for s, row in zip(sums, rows))

    nothing = jnp.zeros((RANK, RANK), F32)
    sums = lax.fori_loop(0, sectors, couple, (nothing,) * 3, unroll=16)
    lane = lax.broadcasted_iota(jnp.int32, (RANK, 128), 1)
    columns = jnp.zeros((RANK, 128), F32)
    for r in range(3):
        columns = jnp.where(lane == r, jnp.sum(sums[r], axis=1, keepdims=True), columns)
    local = jnp.transpose(columns, (1, 0))[:8]
    slab = exact_by_last(local, slab_ref[...])

    place = lax.broadcasted_iota(jnp.int32, (RANK, RANK), 1)

    def leaf(l, _):
        basis = basis_ref[l]
        transfer = transfer_ref[l]
        near = own_ref[l] + side_ref[l] + beyond_ref[l]
        for r in range(3):
            terms = transfer * slab[r : r + 1] + jnp.where(place == l, far_ref[r], 0.0)
            column = jnp.sum(terms, axis=1, keepdims=True)
            out_ref[r, pl.ds(l, 1), :] = jnp.sum(basis * column, axis=0, keepdims=True) + near[4 + r : 5 + r]
        return 0

    lax.fori_loop(0, LD, leaf, 0, unroll=8)


def upward(*args):
    outs = (shaped(LD, 8, LEAF), shaped(8, 8, LEAF + 128))
    scratch = [pltpu.VMEM(x.shape, F32) for x in args[1:]] + [pltpu.SemaphoreType.DMA((4 + 2 * UP_PARTS,))]
    return call(upward_kernel, outs, [SMEM] + [HBM] * 6, scratch, flops=10**9, vmem=FULL)(*args)


def near_own(wire):
    scratch = near_scratch(TALL, 3 * OWN_TURN)
    return call(near_own_kernel, shaped(LD, 8, LEAF), [VMEM], scratch, flops=9 * 10**9)(wire)


def near_side(beyond, *args):
    kernel = functools.partial(near_side_kernel, beyond)
    scratch = near_scratch(TALL + 1, 3 * OWN_TURN)
    return call(kernel, shaped(LD, 8, LEAF), [SMEM, VMEM, VMEM], scratch, flops=9 * 10**9, bytes=2 * 10**7)(*args)


def finish(*args):
    scratch = [pltpu.VMEM((3, RANK, RANK), F32), pltpu.VMEM((14, PACKED, 128), F32)]
    ins = [SMEM] * 3 + [VMEM] * (len(args) - 3)
    return call(finish_kernel, shaped(RHS, LD, LEAF), ins, scratch, flops=4 * 10**9)(*args)


def body(
    values,
    offsets,
    stiffness,
    leaf_basis,
    transfer,
    slab_transfer_matrices,
    leaf_coupling_matrices,
    leaf_admissible_mask,
    top_coupling,
    top_admissible,
):
    at = jnp.stack([lax.axis_index("along"), lax.axis_index("blk")]).astype(jnp.int32)
    sectors = lax.axis_size("blk")
    values = values[:, 0]
    offsets = offsets[:, 0]
    basis = leaf_basis[0]
    transfer = transfer[0]
    slab = slab_transfer_matrices[0, 0]

    wire, slots = upward(at, values, offsets, stiffness[0], basis, transfer, slab)
    came = lax.all_to_all(slots, "along", 0, 0, tiled=True)
    own = near_own(wire)
    came, own = lax.optimization_barrier((came, own))
    tall, whole = call(
        joined_kernel, (shaped(TALL, 8, LEAF), shaped(sectors, 2, 128)), [SMEM, VMEM, VMEM], flops=10**8
    )(at, came, wire)
    flip = [(i, i ^ 1) for i in range(sectors)]
    step_out = [(i, (i + 1 if i % 2 else i - 1) % sectors) for i in range(sectors)]
    stride = [(i, (i + 3 if i % 2 else i - 3) % sectors) for i in range(sectors)]
    partner = lax.ppermute(tall, "blk", flip)
    records = call(pair_records_kernel, shaped(TALL + ROWS // 8, 8, LEAF), [VMEM] * 2)(tall, partner)
    records, whole, partner = lax.optimization_barrier((records, whole, partner))
    came = lax.ppermute(records, "blk", step_out)
    side = near_side(False, at, tall, partner)
    came, side = lax.optimization_barrier((came, side))
    every = lax.all_to_all(whole, "blk", 0, 0, tiled=True)
    beside = call(beside_kernel, shaped(2, PACKED, 128), [SMEM, VMEM])(at, came)
    other = lax.ppermute(beside, "blk", flip)
    window, onward = call(
        window_kernel, (shaped(6, PACKED, 128), shaped(4, PACKED, 128)), [SMEM] + [VMEM] * 4
    )(at, tall, partner, beside, other)
    onward = lax.ppermute(onward, "blk", stride)
    window, came, every = lax.optimization_barrier((window, came, every))
    beyond = near_side(True, at, tall, came)
    back = lax.ppermute(onward, "blk", flip)
    out = finish(
        at, leaf_admissible_mask, top_admissible, leaf_coupling_matrices[0], window, onward, back,
        top_coupling[0], every, slab, transfer, basis, own, side, beyond,
    )
    return out[:, None]


def solution(mesh):
    return jax.shard_map(
        body,
        mesh=mesh,
        in_specs=(
            P(None, "blk", "along", None),
            P(None, "blk", "along", None),
            P("blk", "along", None),
            P("blk", "along", None, None),
            P("blk", "along", None, None),
            P("blk", "along", None, None),
            P("blk", None, None, None),
            P("blk", None),
            P("blk", None, None, None),
            P("blk", None),
        ),
        out_specs=P(None, "blk", "along", None),
        check_vma=False,
    )
```

```python
import functools
import math

import jax
import jax.numpy as jnp
from jax import lax
from jax.experimental import pallas as pl
from jax.experimental.pallas import tpu as pltpu
from jax.sharding import PartitionSpec as P

REACH = 6
LEAF = 256
RANK = 64
RHS = 3
LD = 24
TALL = LD + 2
ROWS = 32
PACKED = 40
SHARPNESS = 2.0
KERNEL_SCALE = 0.125
LOG2E = math.log2(math.e)
F32 = jnp.float32
BF16 = jnp.bfloat16
EXACT = lax.Precision.HIGHEST
VMEM = pl.BlockSpec(memory_space=pltpu.VMEM)
HBM = pl.BlockSpec(memory_space=pltpu.HBM)
SMEM = pl.BlockSpec(memory_space=pltpu.SMEM)
BY_LAST = (((1,), (1,)), ((), ()))
MIB = 2**20
FULL = 60 * MIB + 128 * 1024
TURN_OWN = 6
TURN = 3
UP_PARTS = 4
UP_LEAVES = LD // UP_PARTS


def call(kernel, outs, ins, scratch=(), flops=0, bytes=1 << 20, vmem=16 * MIB):
    return pl.pallas_call(
        kernel,
        out_shape=outs,
        in_specs=ins,
        out_specs=jax.tree.map(lambda _: VMEM, outs),
        scratch_shapes=list(scratch),
        compiler_params=pltpu.CompilerParams(vmem_limit_bytes=vmem),
        cost_estimate=pl.CostEstimate(flops=flops, bytes_accessed=bytes, transcendentals=0),
    )


def shaped(*shape):
    return jax.ShapeDtypeStruct(shape, F32)


def halves(x):
    high = x.astype(BF16).astype(F32)
    return high, x - high


def upward_kernel(
    at_ref, values_hbm, offsets_hbm, stiffness_hbm, basis_hbm, transfer_hbm, slab_hbm, wire_ref, slots_ref,
    values_ref, offsets_ref, stiffness_ref, basis_ref, transfer_ref, slab_ref, sems,
):
    lane = lax.broadcasted_iota(jnp.int32, (RANK, 128), 1)
    small = [
        pltpu.make_async_copy(source, target, sems.at[n])
        for n, (source, target) in enumerate(
            ((values_hbm, values_ref), (offsets_hbm, offsets_ref), (stiffness_hbm, stiffness_ref), (slab_hbm, slab_ref))
        )
    ]
    large = []
    for part in range(UP_PARTS):
        piece = pl.ds(part * UP_LEAVES, UP_LEAVES)
        large.append(
            [
                pltpu.make_async_copy(source.at[piece], target.at[piece], sems.at[4 + 2 * part + n])
                for n, (source, target) in enumerate(((basis_hbm, basis_ref), (transfer_hbm, transfer_ref)))
            ]
        )
    for copy in small + [copy for pair in large for copy in pair]:
        copy.start()
    for copy in small:
        copy.wait()

    def record(l, _):
        row = pl.ds(l, 1)
        for r in range(3):
            wire_ref[l, r : r + 1, :] = offsets_ref[r, row, :] - 0.5
            wire_ref[l, 4 + r : 5 + r, :] = values_ref[r, row, :]
        wire_ref[l, 3:4, :] = stiffness_ref[row, :]
        return 0

    lax.fori_loop(0, LD, record, 0, unroll=4)

    def leaf(l, carry):
        sums, columns = carry
        row = pl.ds(l, 1)
        new_sums = []
        basis = basis_ref[l]
        transfer = transfer_ref[l]
        for r in range(3):
            column = jnp.sum(basis * values_ref[r, row, :], axis=1, keepdims=True)
            new_sums.append(sums[r] + transfer * column)
            columns = jnp.where(lane == r * ROWS + l, column, columns)
        return tuple(new_sums), columns

    nothing = jnp.zeros((RANK, RANK), F32)
    carry = ((nothing,) * 3, jnp.zeros((RANK, 128), F32))
    for part in range(UP_PARTS):
        for copy in large[part]:
            copy.wait()
        carry = lax.fori_loop(part * UP_LEAVES, (part + 1) * UP_LEAVES, leaf, carry, unroll=UP_LEAVES)
    sums, columns = carry
    rows = jnp.transpose(columns, (1, 0))
    coefs = jnp.concatenate(
        [rows[:LD], rows[ROWS : ROWS + LD], rows[2 * ROWS : 2 * ROWS + LD], jnp.zeros((LD, RANK), F32)], 1
    )
    for l in range(LD):
        wire_ref[l, 7:8, :] = coefs[l : l + 1]
    slab_rows = jnp.concatenate(
        [jnp.sum(s, axis=0, keepdims=True) for s in sums] + [jnp.zeros((5, RANK), F32)], 0
    )
    share = jnp.dot(slab_rows, slab_ref[...], precision=EXACT, preferred_element_type=F32)
    share = jnp.concatenate([share, jnp.zeros((8, 128 - RANK), F32)], 1)
    here = at_ref[0]
    for j in range(8):
        slots_ref[j, :, :LEAF] = jnp.where(j < here, wire_ref[0], wire_ref[LD - 1])
        slots_ref[j, :, LEAF:] = share


def tall_kernel(at_ref, came_ref, wire_ref, tall_ref):
    here = at_ref[0]
    lower = came_ref[jnp.maximum(here - 1, 0), :, :LEAF]
    upper = came_ref[jnp.minimum(here + 1, 7), :, :LEAF]
    tall_ref[0] = jnp.where(here > 0, lower, 0.0)
    tall_ref[1 : LD + 1] = wire_ref[...]
    tall_ref[LD + 1] = jnp.where(here < 7, upper, 0.0)


def whole_kernel(came_ref, whole_ref):
    total = came_ref[0, :, LEAF:]
    for j in range(1, 8):
        total = total + came_ref[j, :, LEAF:]
    both = jnp.concatenate(
        [
            jnp.concatenate([total[0:1, :RANK], total[1:2, :RANK]], 1),
            jnp.concatenate([total[2:3, :RANK], jnp.zeros((1, RANK), F32)], 1),
        ],
        0,
    )
    whole_ref[...] = jnp.broadcast_to(both[None], whole_ref.shape)


def source_side(leaf, around, steps, slot, points_ref, loads_ref):
    high, low = halves(leaf)
    points_ref[slot] = jnp.transpose(jnp.concatenate([high, low, low, high], 0), (1, 0)).astype(BF16)
    c0, c1, c2 = leaf[0:1], leaf[1:2], leaf[2:3]
    flat = (c0 + around) * (c0 + around) + c2 * c2
    for step in steps:
        weight = jnp.exp2((-SHARPNESS * LOG2E) * (flat + (c1 + step) * (c1 + step))) * leaf[3:4]
        loads_ref[slot, step + 1] = jnp.concatenate(halves(leaf * weight), 0).astype(BF16)


def target_points(leaf):
    row = lax.broadcasted_iota(jnp.int32, leaf.shape, 0)
    high, low = halves(jnp.where(row < 3, leaf * (2 * SHARPNESS * LOG2E), 0.0))
    return jnp.concatenate([high, low, high, low], 0).astype(BF16)


def pair_kernel(target, points_ref, slot, pairs_ref, place):
    power = jnp.dot(points_ref[slot], target, preferred_element_type=F32)
    pair = jnp.exp2(power)
    high = pair.astype(BF16)
    pairs_ref[place, 0] = high
    pairs_ref[place, 1] = (pair - high.astype(F32)).astype(BF16)


def pair_sum(leaf, loads_ref, slot, pairs_ref, place, around, step):
    c0, c1, c2 = leaf[0:1], leaf[1:2], leaf[2:3]
    loads = loads_ref[slot, step + 1]
    rows = jnp.dot(loads, pairs_ref[place, 0], preferred_element_type=F32) + jnp.dot(
        loads, pairs_ref[place, 1], preferred_element_type=F32
    )
    power = (2 * SHARPNESS * LOG2E) * (around * c0 + step * c1) - (SHARPNESS * LOG2E) * (c0 * c0 + c1 * c1 + c2 * c2)
    weight = jnp.exp2(power) * (KERNEL_SCALE * leaf[3:4])
    return weight * (rows[:8] + rows[8:])


def near_own_kernel(wire_ref, near_ref, points_ref, loads_ref, pairs_ref):
    points_ref[0] = jnp.zeros((LEAF, 32), BF16)
    points_ref[LD + 1] = jnp.zeros((LEAF, 32), BF16)
    loads_ref[0] = jnp.zeros((3, 16, LEAF), BF16)
    loads_ref[LD + 1] = jnp.zeros((3, 16, LEAF), BF16)

    def prepare(l, _):
        source_side(wire_ref[l], 0, (-1, 0, 1), l + 1, points_ref, loads_ref)
        return 0

    lax.fori_loop(0, LD, prepare, 0, unroll=12)

    def turn(g, _):
        leaves = [g * TURN_OWN + n for n in range(TURN_OWN)]
        places = [(n, step) for n in range(TURN_OWN) for step in (-1, 0, 1)]
        targets = [target_points(wire_ref[l]) for l in leaves]
        for place, (n, step) in enumerate(places):
            pair_kernel(targets[n], points_ref, leaves[n] + 1 + step, pairs_ref, place)
        totals = [jnp.zeros((8, LEAF), F32)] * TURN_OWN
        for place, (n, step) in enumerate(places):
            totals[n] += pair_sum(wire_ref[leaves[n]], loads_ref, leaves[n] + 1 + step, pairs_ref, place, 0, step)
        for n in range(TURN_OWN):
            near_ref[leaves[n]] = totals[n]
        return 0

    lax.fori_loop(0, LD // TURN_OWN, turn, 0)


def near_side_kernel(beyond, at_ref, tall_ref, came_ref, near_ref, points_ref, loads_ref, pairs_ref):
    odd = lax.rem(at_ref[1], 2)
    around = ((2 * odd - 1) if beyond else (1 - 2 * odd)).astype(F32)

    def prepare(l, _):
        source_side(came_ref[l], around, (-1, 0, 1), l, points_ref, loads_ref)
        return 0

    lax.fori_loop(0, TALL, prepare, 0, unroll=13)
    end, end_leaf, end_step = (LD + 1, LD - 1, 1) if beyond else (0, 0, -1)
    source_side(tall_ref[end], 0, (end_step,), TALL, points_ref, loads_ref)

    def turn(g, _):
        leaves = [g * TURN + n for n in range(TURN)]
        places = [(n, step) for n in range(TURN) for step in (-1, 0, 1)]
        targets = [target_points(tall_ref[l + 1]) for l in leaves]
        for place, (n, step) in enumerate(places):
            pair_kernel(targets[n], points_ref, leaves[n] + 1 + step, pairs_ref, place)
        totals = [jnp.zeros((8, LEAF), F32)] * TURN
        for place, (n, step) in enumerate(places):
            slot = leaves[n] + 1 + step
            totals[n] += pair_sum(tall_ref[leaves[n] + 1], loads_ref, slot, pairs_ref, place, around, step)
        for n in range(TURN):
            near_ref[leaves[n]] = totals[n]
        return 0

    lax.fori_loop(0, LD // TURN, turn, 0)
    here = tall_ref[end_leaf + 1]
    pair_kernel(target_points(here), points_ref, TALL, pairs_ref, 0)
    near_ref[end_leaf] += pair_sum(here, loads_ref, TALL, pairs_ref, 0, 0, end_step)


def near_scratch(leaves, places):
    return [
        pltpu.VMEM((leaves, LEAF, 32), BF16),
        pltpu.VMEM((leaves, 3, 16, LEAF), BF16),
        pltpu.VMEM((places, 2, LEAF, LEAF), BF16),
    ]


def packed(rows):
    third = rows[:, 2 * RANK : 3 * RANK]
    third = jnp.concatenate([third[: TALL // 2], third[TALL // 2 :]], 1)
    return jnp.concatenate([rows[:, : 2 * RANK], third, jnp.zeros((PACKED - TALL - TALL // 2, 128), F32)], 0)


def coefs_of(tall_ref):
    return jnp.concatenate([tall_ref[l, 7:8, :] for l in range(TALL)], 0)


def pair_records_kernel(tall_ref, partner_ref, records_ref):
    records_ref[:TALL] = tall_ref[...]
    rows = jnp.concatenate([coefs_of(partner_ref), jnp.zeros((ROWS - TALL, LEAF), F32)], 0)
    for n in range(ROWS // 8):
        records_ref[TALL + n] = rows[8 * n : 8 * n + 8]


def beside_kernel(at_ref, came_ref, beside_ref):
    even = lax.rem(at_ref[1], 2) == 0
    first = packed(coefs_of(came_ref))
    second = packed(jnp.concatenate([came_ref[TALL + n] for n in range(ROWS // 8)], 0)[:TALL])
    beside_ref[0] = jnp.where(even, second, first)
    beside_ref[1] = jnp.where(even, first, second)


def chip_kernel(at_ref, tall_ref, partner_ref, chip_ref):
    even = lax.rem(at_ref[1], 2) == 0
    own, partner = packed(coefs_of(tall_ref)), packed(coefs_of(partner_ref))
    chip_ref[0] = jnp.where(even, own, partner)
    chip_ref[1] = jnp.where(even, partner, own)


def window_kernel(at_ref, chip_ref, beside_ref, other_ref, window_ref, onward_ref):
    even = lax.rem(at_ref[1], 2) == 0
    chip, beside, other = ([ref[n] for n in range(2)] for ref in (chip_ref, beside_ref, other_ref))
    low = [jnp.where(even, beside[n], other[n]) for n in range(2)]
    high = [jnp.where(even, other[n], beside[n]) for n in range(2)]
    window = low + chip + high
    for n in range(6):
        window_ref[n] = window[n]
    for n in range(4):
        onward_ref[n] = jnp.where(even, window[n + 2], window[n])


def exact_by_last(x, y):
    return lax.dot_general(x, y, BY_LAST, precision=EXACT, preferred_element_type=F32)


def three_by_last(x, y):
    (xh, xl), (yh, yl) = halves(x), halves(y)
    xh, xl, yh, yl = (z.astype(BF16) for z in (xh, xl, yh, yl))
    high = lax.dot_general(xh, yh, BY_LAST, preferred_element_type=F32)
    cross = lax.dot_general(xl, yh, BY_LAST, preferred_element_type=F32)
    return high + (cross + lax.dot_general(xh, yl, BY_LAST, preferred_element_type=F32))


def top_kernel(at_ref, admissible_ref, every_ref, top_ref, slab_ref, down_ref):
    here = at_ref[1]
    sectors = top_ref.shape[0]

    def couple(t, sums):
        apart = lax.rem(t - here + sectors, sectors)
        distant = jnp.logical_and(apart > REACH, apart < sectors - REACH)
        allowed = jnp.where(distant, admissible_ref[0, t], 0).astype(F32)
        coupling = top_ref[t]
        both = every_ref[t] * allowed
        rows = (both[0:1, :RANK], both[0:1, RANK:], both[1:2, :RANK])
        return tuple(s + coupling * row for s, row in zip(sums, rows))

    nothing = jnp.zeros((RANK, RANK), F32)
    sums = lax.fori_loop(0, sectors, couple, (nothing,) * 3, unroll=16)
    lane = lax.broadcasted_iota(jnp.int32, (RANK, 128), 1)
    columns = jnp.zeros((RANK, 128), F32)
    for r in range(3):
        columns = jnp.where(lane == r, jnp.sum(sums[r], axis=1, keepdims=True), columns)
    local = jnp.transpose(columns, (1, 0))[:8]
    down_ref[...] = exact_by_last(local, slab_ref[...])


def finish_kernel(at_ref, mask_ref, *refs):
    count = len(refs) - 3
    local, out_ref = refs[:count], refs[count]
    far_ref, ring_ref = refs[count + 1 :]
    coupling_ref, window_ref, onward_ref, back_ref = local[:4]
    down_ref, transfer_ref, basis_ref, own_ref, side_ref, beyond_ref = local[4:]
    slab = down_ref[...]

    here = at_ref[1]
    odd = lax.rem(here, 2)
    for n in range(4):
        ring_ref[n] = jnp.where(odd == 0, onward_ref[n], back_ref[n])
        ring_ref[n + 10] = jnp.where(odd == 0, back_ref[n], onward_ref[n])
    for n in range(6):
        ring_ref[n + 4] = window_ref[n]
    total = jnp.zeros((3 * ROWS, 3 * RANK), F32)
    for q in range(2 * (REACH - 1)):
        around = q + 2 if q < REACH - 1 else 3 - q
        rows = ring_ref[odd + (REACH + around)]
        gap = jnp.zeros((ROWS - TALL, RANK), F32)
        third = rows[TALL : TALL + TALL // 2]
        stacked = jnp.concatenate(
            [rows[:TALL, :RANK], gap, rows[:TALL, RANK:], gap, third[:, :RANK], third[:, RANK:], gap], 0
        )
        coupling = jnp.concatenate(
            [coupling_ref[3 * q + b] * mask_ref[0, 3 * q + b].astype(F32) for b in range(3)], 0
        )
        total = total + three_by_last(stacked, coupling)
    far = []
    for r in range(3):
        block = total[r * ROWS : (r + 1) * ROWS]
        rows = block[0:LD, :RANK] + block[1 : LD + 1, RANK : 2 * RANK] + block[2 : LD + 2, 2 * RANK :]
        far.append(jnp.concatenate([rows, jnp.zeros((ROWS - LD, RANK), F32)], 0))
    far.append(jnp.zeros((ROWS, RANK), F32))
    columns = jnp.transpose(jnp.concatenate(far, 0), (1, 0))
    far_columns = [columns[:, r * ROWS : (r + 1) * ROWS] for r in range(3)]
    for r in range(3):
        far_ref[r] = jnp.concatenate([far_columns[r], jnp.zeros((RANK, RANK - ROWS), F32)], 1)

    place = lax.broadcasted_iota(jnp.int32, (RANK, RANK), 1)

    def leaf(l, _):
        basis = basis_ref[l]
        transfer = transfer_ref[l]
        near = own_ref[l] + side_ref[l] + beyond_ref[l]
        for r in range(3):
            terms = transfer * slab[r : r + 1] + jnp.where(place == l, far_ref[r], 0.0)
            column = jnp.sum(terms, axis=1, keepdims=True)
            out_ref[r, pl.ds(l, 1), :] = jnp.sum(basis * column, axis=0, keepdims=True) + near[4 + r : 5 + r]
        return 0

    lax.fori_loop(0, LD, leaf, 0, unroll=8)


def upward(*args):
    outs = (shaped(LD, 8, LEAF), shaped(8, 8, LEAF + 128))
    scratch = [pltpu.VMEM(x.shape, F32) for x in args[1:]] + [pltpu.SemaphoreType.DMA((4 + 2 * UP_PARTS,))]
    return call(upward_kernel, outs, [SMEM] + [HBM] * 6, scratch, flops=10**9, vmem=FULL)(*args)


def near_own(wire):
    scratch = near_scratch(TALL, 3 * TURN_OWN)
    return call(near_own_kernel, shaped(LD, 8, LEAF), [VMEM], scratch, flops=9 * 10**9)(wire)


def near_side(beyond, *args):
    kernel = functools.partial(near_side_kernel, beyond)
    scratch = near_scratch(TALL + 1, 3 * TURN)
    return call(kernel, shaped(LD, 8, LEAF), [SMEM, VMEM, VMEM], scratch, flops=9 * 10**9, bytes=2 * 10**7)(*args)


def finish(*args):
    scratch = [pltpu.VMEM((3, RANK, RANK), F32), pltpu.VMEM((14, PACKED, 128), F32)]
    ins = [SMEM] * 2 + [VMEM] * (len(args) - 2)
    return call(finish_kernel, shaped(RHS, LD, LEAF), ins, scratch, flops=4 * 10**9)(*args)


def body(
    values,
    offsets,
    stiffness,
    leaf_basis,
    transfer,
    slab_transfer_matrices,
    leaf_coupling_matrices,
    leaf_admissible_mask,
    top_coupling,
    top_admissible,
):
    at = jnp.stack([lax.axis_index("along"), lax.axis_index("blk")]).astype(jnp.int32)
    sectors = lax.axis_size("blk")
    values = values[:, 0]
    offsets = offsets[:, 0]
    basis = leaf_basis[0]
    transfer = transfer[0]
    slab = slab_transfer_matrices[0, 0]

    wire, slots = upward(at, values, offsets, stiffness[0], basis, transfer, slab)
    came = lax.all_to_all(slots, "along", 0, 0, tiled=True)
    own = near_own(wire)
    came, own = lax.optimization_barrier((came, own))
    tall = call(tall_kernel, shaped(TALL, 8, LEAF), [SMEM, VMEM, VMEM])(at, came, wire)
    tall, came = lax.optimization_barrier((tall, came))
    whole = call(whole_kernel, shaped(sectors, 2, 128), [VMEM])(came)
    flip = [(i, i ^ 1) for i in range(sectors)]
    step_out = [(i, (i + 1 if i % 2 else i - 1) % sectors) for i in range(sectors)]
    stride = [(i, (i + 3 if i % 2 else i - 3) % sectors) for i in range(sectors)]
    partner = lax.ppermute(tall, "blk", flip)
    records = call(pair_records_kernel, shaped(TALL + ROWS // 8, 8, LEAF), [VMEM] * 2)(tall, partner)
    records, partner = lax.optimization_barrier((records, partner))
    came = lax.ppermute(records, "blk", step_out)
    side = near_side(False, at, tall, partner)
    came, side = lax.optimization_barrier((came, side))
    every = lax.all_to_all(whole, "blk", 0, 0, tiled=True)
    beside = call(beside_kernel, shaped(2, PACKED, 128), [SMEM, VMEM])(at, came)
    other = lax.ppermute(beside, "blk", flip)
    partner, beside = lax.optimization_barrier((partner, beside))
    chip = call(chip_kernel, shaped(2, PACKED, 128), [SMEM, VMEM, VMEM])(at, tall, partner)
    window, onward = call(
        window_kernel, (shaped(6, PACKED, 128), shaped(4, PACKED, 128)), [SMEM] + [VMEM] * 3
    )(at, chip, beside, other)
    onward = lax.ppermute(onward, "blk", stride)
    window, came, every = lax.optimization_barrier((window, came, every))
    beyond = near_side(True, at, tall, came)
    onward, beyond, every = lax.optimization_barrier((onward, beyond, every))
    back = lax.ppermute(onward, "blk", flip)
    down = call(top_kernel, shaped(8, RANK), [SMEM] * 2 + [VMEM] * 3, flops=10**9)(
        at, top_admissible, every, top_coupling[0], slab
    )
    out = finish(
        at, leaf_admissible_mask, leaf_coupling_matrices[0], window, onward, back, down,
        transfer, basis, own, side, beyond,
    )
    return out[:, None]


def solution(mesh):
    return jax.shard_map(
        body,
        mesh=mesh,
        in_specs=(
            P(None, "blk", "along", None),
            P(None, "blk", "along", None),
            P("blk", "along", None),
            P("blk", "along", None, None),
            P("blk", "along", None, None),
            P("blk", "along", None, None),
            P("blk", None, None, None),
            P("blk", None),
            P("blk", None, None, None),
            P("blk", None),
        ),
        out_specs=P(None, "blk", "along", None),
        check_vma=False,
    )
```

```python
import functools
import math

import jax
import jax.numpy as jnp
from jax import lax
from jax.experimental import pallas as pl
from jax.experimental.pallas import tpu as pltpu
from jax.sharding import PartitionSpec as P

REACH = 6
LEAF = 256
RANK = 64
RHS = 3
LD = 24
TALL = LD + 2
ROWS = 32
PACKED = 40
SHARPNESS = 2.0
KERNEL_SCALE = 0.125
LOG2E = math.log2(math.e)
F32 = jnp.float32
BF16 = jnp.bfloat16
EXACT = lax.Precision.HIGHEST
VMEM = pl.BlockSpec(memory_space=pltpu.VMEM)
HBM = pl.BlockSpec(memory_space=pltpu.HBM)
SMEM = pl.BlockSpec(memory_space=pltpu.SMEM)
BY_LAST = (((1,), (1,)), ((), ()))
MIB = 2**20
FULL = 60 * MIB + 128 * 1024
TURN_OWN = 6
TURN = 3
UP_PARTS = 4
UP_LEAVES = LD // UP_PARTS


def call(kernel, outs, ins, scratch=(), flops=0, bytes=1 << 20, vmem=16 * MIB):
    return pl.pallas_call(
        kernel,
        out_shape=outs,
        in_specs=ins,
        out_specs=jax.tree.map(lambda _: VMEM, outs),
        scratch_shapes=list(scratch),
        compiler_params=pltpu.CompilerParams(vmem_limit_bytes=vmem),
        cost_estimate=pl.CostEstimate(flops=flops, bytes_accessed=bytes, transcendentals=0),
    )


def shaped(*shape):
    return jax.ShapeDtypeStruct(shape, F32)


def halves(x):
    high = x.astype(BF16).astype(F32)
    return high, x - high


def upward_kernel(
    values_hbm, offsets_hbm, stiffness_hbm, basis_hbm, transfer_hbm, slab_hbm, wire_ref, slots_ref,
    values_ref, offsets_ref, stiffness_ref, basis_ref, transfer_ref, slab_ref, sems,
):
    lane = lax.broadcasted_iota(jnp.int32, (RANK, 128), 1)
    small = [
        pltpu.make_async_copy(source, target, sems.at[n])
        for n, (source, target) in enumerate(
            ((values_hbm, values_ref), (offsets_hbm, offsets_ref), (stiffness_hbm, stiffness_ref), (slab_hbm, slab_ref))
        )
    ]
    large = []
    for part in range(UP_PARTS):
        piece = pl.ds(part * UP_LEAVES, UP_LEAVES)
        large.append(
            [
                pltpu.make_async_copy(source.at[piece], target.at[piece], sems.at[4 + 2 * part + n])
                for n, (source, target) in enumerate(((basis_hbm, basis_ref), (transfer_hbm, transfer_ref)))
            ]
        )
    for copy in small + [copy for pair in large for copy in pair]:
        copy.start()
    for copy in small:
        copy.wait()

    def record(l, _):
        row = pl.ds(l, 1)
        for r in range(3):
            wire_ref[l, r : r + 1, :] = offsets_ref[r, row, :] - 0.5
            wire_ref[l, 4 + r : 5 + r, :] = values_ref[r, row, :]
        wire_ref[l, 3:4, :] = stiffness_ref[row, :]
        return 0

    lax.fori_loop(0, LD, record, 0, unroll=4)

    def leaf(l, carry):
        sums, columns = carry
        row = pl.ds(l, 1)
        new_sums = []
        basis = basis_ref[l]
        transfer = transfer_ref[l]
        for r in range(3):
            column = jnp.sum(basis * values_ref[r, row, :], axis=1, keepdims=True)
            new_sums.append(sums[r] + transfer * column)
            columns = jnp.where(lane == r * ROWS + l, column, columns)
        return tuple(new_sums), columns

    nothing = jnp.zeros((RANK, RANK), F32)
    carry = ((nothing,) * 3, jnp.zeros((RANK, 128), F32))
    for part in range(UP_PARTS):
        for copy in large[part]:
            copy.wait()
        carry = lax.fori_loop(part * UP_LEAVES, (part + 1) * UP_LEAVES, leaf, carry, unroll=UP_LEAVES)
    sums, columns = carry
    rows = jnp.transpose(columns, (1, 0))
    coefs = jnp.concatenate(
        [rows[:LD], rows[ROWS : ROWS + LD], rows[2 * ROWS : 2 * ROWS + LD], jnp.zeros((LD, RANK), F32)], 1
    )
    for l in range(LD):
        wire_ref[l, 7:8, :] = coefs[l : l + 1]
    slab_rows = jnp.concatenate(
        [jnp.sum(s, axis=0, keepdims=True) for s in sums] + [jnp.zeros((5, RANK), F32)], 0
    )
    share = jnp.dot(slab_rows, slab_ref[...], precision=EXACT, preferred_element_type=F32)
    share = jnp.concatenate([share, jnp.zeros((8, 128 - RANK), F32)], 1)
    here = lax.axis_index("along")
    for j in range(8):
        slots_ref[j, :, :LEAF] = jnp.where(j < here, wire_ref[0], wire_ref[LD - 1])
        slots_ref[j, :, LEAF:] = share


def tall_kernel(came_ref, wire_ref, tall_ref):
    here = lax.axis_index("along")
    lower = came_ref[jnp.maximum(here - 1, 0), :, :LEAF]
    upper = came_ref[jnp.minimum(here + 1, 7), :, :LEAF]
    tall_ref[0] = jnp.where(here > 0, lower, 0.0)
    tall_ref[1 : LD + 1] = wire_ref[...]
    tall_ref[LD + 1] = jnp.where(here < 7, upper, 0.0)


def whole_kernel(came_ref, whole_ref):
    total = came_ref[0, :, LEAF:]
    for j in range(1, 8):
        total = total + came_ref[j, :, LEAF:]
    both = jnp.concatenate(
        [
            jnp.concatenate([total[0:1, :RANK], total[1:2, :RANK]], 1),
            jnp.concatenate([total[2:3, :RANK], jnp.zeros((1, RANK), F32)], 1),
        ],
        0,
    )
    whole_ref[...] = jnp.broadcast_to(both[None], whole_ref.shape)


def source_side(leaf, around, steps, slot, points_ref, loads_ref):
    high, low = halves(leaf)
    points_ref[slot] = jnp.transpose(jnp.concatenate([high, low, low, high], 0), (1, 0)).astype(BF16)
    c0, c1, c2 = leaf[0:1], leaf[1:2], leaf[2:3]
    flat = (c0 + around) * (c0 + around) + c2 * c2
    for step in steps:
        weight = jnp.exp2((-SHARPNESS * LOG2E) * (flat + (c1 + step) * (c1 + step))) * leaf[3:4]
        loads_ref[slot, step + 1] = jnp.concatenate(halves(leaf * weight), 0).astype(BF16)


def target_points(leaf):
    row = lax.broadcasted_iota(jnp.int32, leaf.shape, 0)
    high, low = halves(jnp.where(row < 3, leaf * (2 * SHARPNESS * LOG2E), 0.0))
    return jnp.concatenate([high, low, high, low], 0).astype(BF16)


def pair_kernels(target, points_ref, slot, pairs_ref, place):
    points = points_ref[pl.ds(slot, 3)].reshape(3 * LEAF, 32)
    pairs = jnp.exp2(jnp.dot(points, target, preferred_element_type=F32))
    for step in range(3):
        pair = pairs[step * LEAF : (step + 1) * LEAF]
        high = pair.astype(BF16)
        pairs_ref[place + step, 0] = high
        pairs_ref[place + step, 1] = (pair - high.astype(F32)).astype(BF16)


def pair_kernel(target, points_ref, slot, pairs_ref, place):
    power = jnp.dot(points_ref[slot], target, preferred_element_type=F32)
    pair = jnp.exp2(power)
    high = pair.astype(BF16)
    pairs_ref[place, 0] = high
    pairs_ref[place, 1] = (pair - high.astype(F32)).astype(BF16)


def pair_sum(leaf, loads_ref, slot, pairs_ref, place, around, step):
    c0, c1, c2 = leaf[0:1], leaf[1:2], leaf[2:3]
    loads = loads_ref[slot, step + 1]
    rows = jnp.dot(loads, pairs_ref[place, 0], preferred_element_type=F32) + jnp.dot(
        loads, pairs_ref[place, 1], preferred_element_type=F32
    )
    power = (2 * SHARPNESS * LOG2E) * (around * c0 + step * c1) - (SHARPNESS * LOG2E) * (c0 * c0 + c1 * c1 + c2 * c2)
    weight = jnp.exp2(power) * (KERNEL_SCALE * leaf[3:4])
    return weight * (rows[:8] + rows[8:])


def near_own_kernel(wire_ref, near_ref, points_ref, loads_ref, pairs_ref):
    points_ref[0] = jnp.zeros((LEAF, 32), BF16)
    points_ref[LD + 1] = jnp.zeros((LEAF, 32), BF16)
    loads_ref[0] = jnp.zeros((3, 16, LEAF), BF16)
    loads_ref[LD + 1] = jnp.zeros((3, 16, LEAF), BF16)

    def prepare(l, _):
        source_side(wire_ref[l], 0, (-1, 0, 1), l + 1, points_ref, loads_ref)
        return 0

    lax.fori_loop(0, LD, prepare, 0, unroll=12)

    def turn(g, _):
        leaves = [g * TURN_OWN + n for n in range(TURN_OWN)]
        places = [(n, step) for n in range(TURN_OWN) for step in (-1, 0, 1)]
        targets = [target_points(wire_ref[l]) for l in leaves]
        for n in range(TURN_OWN):
            pair_kernels(targets[n], points_ref, leaves[n], pairs_ref, 3 * n)
        totals = [jnp.zeros((8, LEAF), F32)] * TURN_OWN
        for place, (n, step) in enumerate(places):
            totals[n] += pair_sum(wire_ref[leaves[n]], loads_ref, leaves[n] + 1 + step, pairs_ref, place, 0, step)
        for n in range(TURN_OWN):
            near_ref[leaves[n]] = totals[n]
        return 0

    lax.fori_loop(0, LD // TURN_OWN, turn, 0)


def near_side_kernel(beyond, tall_ref, came_ref, near_ref, points_ref, loads_ref, pairs_ref):
    odd = lax.rem(lax.axis_index("blk"), 2)
    around = ((2 * odd - 1) if beyond else (1 - 2 * odd)).astype(F32)

    def prepare(l, _):
        source_side(came_ref[l], around, (-1, 0, 1), l, points_ref, loads_ref)
        return 0

    lax.fori_loop(0, TALL, prepare, 0, unroll=13)
    end, end_leaf, end_step = (LD + 1, LD - 1, 1) if beyond else (0, 0, -1)
    source_side(tall_ref[end], 0, (end_step,), TALL, points_ref, loads_ref)

    def turn(g, _):
        leaves = [g * TURN + n for n in range(TURN)]
        places = [(n, step) for n in range(TURN) for step in (-1, 0, 1)]
        targets = [target_points(tall_ref[l + 1]) for l in leaves]
        for n in range(TURN):
            pair_kernels(targets[n], points_ref, leaves[n], pairs_ref, 3 * n)
        totals = [jnp.zeros((8, LEAF), F32)] * TURN
        for place, (n, step) in enumerate(places):
            slot = leaves[n] + 1 + step
            totals[n] += pair_sum(tall_ref[leaves[n] + 1], loads_ref, slot, pairs_ref, place, around, step)
        for n in range(TURN):
            near_ref[leaves[n]] = totals[n]
        return 0

    lax.fori_loop(0, LD // TURN, turn, 0)
    here = tall_ref[end_leaf + 1]
    pair_kernel(target_points(here), points_ref, TALL, pairs_ref, 0)
    near_ref[end_leaf] += pair_sum(here, loads_ref, TALL, pairs_ref, 0, 0, end_step)


def near_scratch(leaves, places):
    return [
        pltpu.VMEM((leaves, LEAF, 32), BF16),
        pltpu.VMEM((leaves, 3, 16, LEAF), BF16),
        pltpu.VMEM((places, 2, LEAF, LEAF), BF16),
    ]


def packed(rows):
    third = rows[:, 2 * RANK : 3 * RANK]
    third = jnp.concatenate([third[: TALL // 2], third[TALL // 2 :]], 1)
    return jnp.concatenate([rows[:, : 2 * RANK], third, jnp.zeros((PACKED - TALL - TALL // 2, 128), F32)], 0)


def coefs_of(tall_ref):
    return jnp.concatenate([tall_ref[l, 7:8, :] for l in range(TALL)], 0)


def pair_records_kernel(tall_ref, partner_ref, records_ref):
    records_ref[:TALL] = tall_ref[...]
    rows = jnp.concatenate([coefs_of(partner_ref), jnp.zeros((ROWS - TALL, LEAF), F32)], 0)
    for n in range(ROWS // 8):
        records_ref[TALL + n] = rows[8 * n : 8 * n + 8]


def beside_kernel(came_ref, beside_ref):
    even = lax.rem(lax.axis_index("blk"), 2) == 0
    first = packed(coefs_of(came_ref))
    second = packed(jnp.concatenate([came_ref[TALL + n] for n in range(ROWS // 8)], 0)[:TALL])
    beside_ref[0] = jnp.where(even, second, first)
    beside_ref[1] = jnp.where(even, first, second)


def chip_kernel(tall_ref, partner_ref, chip_ref):
    even = lax.rem(lax.axis_index("blk"), 2) == 0
    own, partner = packed(coefs_of(tall_ref)), packed(coefs_of(partner_ref))
    chip_ref[0] = jnp.where(even, own, partner)
    chip_ref[1] = jnp.where(even, partner, own)


def window_kernel(chip_ref, beside_ref, other_ref, window_ref, onward_ref):
    even = lax.rem(lax.axis_index("blk"), 2) == 0
    chip, beside, other = ([ref[n] for n in range(2)] for ref in (chip_ref, beside_ref, other_ref))
    low = [jnp.where(even, beside[n], other[n]) for n in range(2)]
    high = [jnp.where(even, other[n], beside[n]) for n in range(2)]
    window = low + chip + high
    for n in range(6):
        window_ref[n] = window[n]
    for n in range(4):
        onward_ref[n] = jnp.where(even, window[n + 2], window[n])


def exact_by_last(x, y):
    return lax.dot_general(x, y, BY_LAST, precision=EXACT, preferred_element_type=F32)


def three_by_last(x, y):
    (xh, xl), (yh, yl) = halves(x), halves(y)
    xh, xl, yh, yl = (z.astype(BF16) for z in (xh, xl, yh, yl))
    high = lax.dot_general(xh, yh, BY_LAST, preferred_element_type=F32)
    cross = lax.dot_general(xl, yh, BY_LAST, preferred_element_type=F32)
    return high + (cross + lax.dot_general(xh, yl, BY_LAST, preferred_element_type=F32))


def top_kernel(admissible_ref, every_ref, top_ref, slab_ref, down_ref, first_ref, second_ref):
    sectors = top_ref.shape[0]
    apart = lax.rem(lax.broadcasted_iota(jnp.int32, (8, sectors), 1) - lax.axis_index("blk") + sectors, sectors)
    distant = jnp.logical_and(apart > REACH, apart < sectors - REACH)
    allowed = jnp.where(distant, admissible_ref[...], 0).astype(F32)
    allowed = jnp.transpose(jnp.concatenate([allowed, jnp.zeros((8, 128 - sectors), F32)], 1), (1, 0))[:sectors, :1]
    first_ref[...] = every_ref[:, 0, :] * allowed
    second_ref[...] = every_ref[:, 1, :] * allowed

    def couple(t, sums):
        coupling = top_ref[t]
        first, second = first_ref[pl.ds(t, 1), :], second_ref[pl.ds(t, 1), :]
        rows = (first[:, :RANK], first[:, RANK:], second[:, :RANK])
        return tuple(s + coupling * row for s, row in zip(sums, rows))

    nothing = jnp.zeros((RANK, RANK), F32)
    sums = lax.fori_loop(0, sectors, couple, (nothing,) * 3, unroll=16)
    lane = lax.broadcasted_iota(jnp.int32, (RANK, 128), 1)
    columns = jnp.zeros((RANK, 128), F32)
    for r in range(3):
        columns = jnp.where(lane == r, jnp.sum(sums[r], axis=1, keepdims=True), columns)
    local = jnp.transpose(columns, (1, 0))[:8]
    down_ref[...] = exact_by_last(local, slab_ref[...])


def finish_kernel(mask_ref, *refs):
    count = len(refs) - 3
    local, out_ref = refs[:count], refs[count]
    far_ref, ring_ref = refs[count + 1 :]
    coupling_ref, window_ref, onward_ref, back_ref = local[:4]
    down_ref, transfer_ref, basis_ref, own_ref, side_ref, beyond_ref = local[4:]
    slab = down_ref[...]

    here = lax.axis_index("blk")
    odd = lax.rem(here, 2)
    for n in range(4):
        ring_ref[n] = jnp.where(odd == 0, onward_ref[n], back_ref[n])
        ring_ref[n + 10] = jnp.where(odd == 0, back_ref[n], onward_ref[n])
    for n in range(6):
        ring_ref[n + 4] = window_ref[n]
    mask = mask_ref[...].astype(F32)
    total = jnp.zeros((3 * ROWS, 3 * RANK), F32)
    for q in range(2 * (REACH - 1)):
        around = q + 2 if q < REACH - 1 else 3 - q
        rows = ring_ref[odd + (REACH + around)]
        gap = jnp.zeros((ROWS - TALL, RANK), F32)
        third = rows[TALL : TALL + TALL // 2]
        stacked = jnp.concatenate(
            [rows[:TALL, :RANK], gap, rows[:TALL, RANK:], gap, third[:, :RANK], third[:, RANK:], gap], 0
        )
        coupling = jnp.concatenate(
            [coupling_ref[3 * q + b] * mask[:, 3 * q + b : 3 * q + b + 1] for b in range(3)], 0
        )
        total = total + three_by_last(stacked, coupling)
    far = []
    for r in range(3):
        block = total[r * ROWS : (r + 1) * ROWS]
        rows = block[0:LD, :RANK] + block[1 : LD + 1, RANK : 2 * RANK] + block[2 : LD + 2, 2 * RANK :]
        far.append(jnp.concatenate([rows, jnp.zeros((ROWS - LD, RANK), F32)], 0))
    far.append(jnp.zeros((ROWS, RANK), F32))
    columns = jnp.transpose(jnp.concatenate(far, 0), (1, 0))
    far_columns = [columns[:, r * ROWS : (r + 1) * ROWS] for r in range(3)]
    for r in range(3):
        far_ref[r] = jnp.concatenate([far_columns[r], jnp.zeros((RANK, RANK - ROWS), F32)], 1)

    place = lax.broadcasted_iota(jnp.int32, (RANK, RANK), 1)

    def leaf(l, _):
        basis = basis_ref[l]
        transfer = transfer_ref[l]
        near = own_ref[l] + side_ref[l] + beyond_ref[l]
        for r in range(3):
            terms = transfer * slab[r : r + 1] + jnp.where(place == l, far_ref[r], 0.0)
            column = jnp.sum(terms, axis=1, keepdims=True)
            out_ref[r, pl.ds(l, 1), :] = jnp.sum(basis * column, axis=0, keepdims=True) + near[4 + r : 5 + r]
        return 0

    lax.fori_loop(0, LD, leaf, 0, unroll=8)


def upward(*args):
    outs = (shaped(LD, 8, LEAF), shaped(8, 8, LEAF + 128))
    scratch = [pltpu.VMEM(x.shape, F32) for x in args] + [pltpu.SemaphoreType.DMA((4 + 2 * UP_PARTS,))]
    return call(upward_kernel, outs, [HBM] * 6, scratch, flops=10**9, vmem=FULL)(*args)


def near_own(wire):
    scratch = near_scratch(TALL, 3 * TURN_OWN)
    return call(near_own_kernel, shaped(LD, 8, LEAF), [VMEM], scratch, flops=9 * 10**9)(wire)


def near_side(beyond, *args):
    kernel = functools.partial(near_side_kernel, beyond)
    scratch = near_scratch(TALL + 1, 3 * TURN)
    return call(kernel, shaped(LD, 8, LEAF), [VMEM, VMEM], scratch, flops=9 * 10**9, bytes=2 * 10**7)(*args)


def finish(*args):
    scratch = [pltpu.VMEM((3, RANK, RANK), F32), pltpu.VMEM((14, PACKED, 128), F32)]
    ins = [VMEM] * len(args)
    return call(finish_kernel, shaped(RHS, LD, LEAF), ins, scratch, flops=4 * 10**9)(*args)


def top(*args):
    scratch = [pltpu.VMEM((args[2].shape[0], 128), F32)] * 2
    return call(top_kernel, shaped(8, RANK), [VMEM] * 4, scratch, flops=10**9)(*args)


def body(
    values,
    offsets,
    stiffness,
    leaf_basis,
    transfer,
    slab_transfer_matrices,
    leaf_coupling_matrices,
    leaf_admissible_mask,
    top_coupling,
    top_admissible,
):
    sectors = lax.axis_size("blk")
    values = values[:, 0]
    offsets = offsets[:, 0]
    basis = leaf_basis[0]
    transfer = transfer[0]
    slab = slab_transfer_matrices[0, 0]

    wire, slots = upward(values, offsets, stiffness[0], basis, transfer, slab)
    came = lax.all_to_all(slots, "along", 0, 0, tiled=True)
    own = near_own(wire)
    came, own = lax.optimization_barrier((came, own))
    tall = call(tall_kernel, shaped(TALL, 8, LEAF), [VMEM, VMEM])(came, wire)
    tall, came = lax.optimization_barrier((tall, came))
    whole = call(whole_kernel, shaped(sectors, 2, 128), [VMEM])(came)
    flip = [(i, i ^ 1) for i in range(sectors)]
    step_out = [(i, (i + 1 if i % 2 else i - 1) % sectors) for i in range(sectors)]
    stride = [(i, (i + 3 if i % 2 else i - 3) % sectors) for i in range(sectors)]
    partner = lax.ppermute(tall, "blk", flip)
    records = call(pair_records_kernel, shaped(TALL + ROWS // 8, 8, LEAF), [VMEM] * 2)(tall, partner)
    records, partner = lax.optimization_barrier((records, partner))
    came = lax.ppermute(records, "blk", step_out)
    side = near_side(False, tall, partner)
    came, side = lax.optimization_barrier((came, side))
    every = lax.all_to_all(whole, "blk", 0, 0, tiled=True)
    beside = call(beside_kernel, shaped(2, PACKED, 128), [VMEM])(came)
    other = lax.ppermute(beside, "blk", flip)
    partner, beside = lax.optimization_barrier((partner, beside))
    chip = call(chip_kernel, shaped(2, PACKED, 128), [VMEM, VMEM])(tall, partner)
    window, onward = call(
        window_kernel, (shaped(6, PACKED, 128), shaped(4, PACKED, 128)), [VMEM] * 3
    )(chip, beside, other)
    onward = lax.ppermute(onward, "blk", stride)
    window, came, every = lax.optimization_barrier((window, came, every))
    beyond = near_side(True, tall, came)
    onward, beyond, every = lax.optimization_barrier((onward, beyond, every))
    back = lax.ppermute(onward, "blk", flip)
    down = top(
        top_admissible, every, top_coupling[0], slab
    )
    out = finish(
        leaf_admissible_mask, leaf_coupling_matrices[0], window, onward, back, down,
        transfer, basis, own, side, beyond,
    )
    return out[:, None]


def solution(mesh):
    return jax.shard_map(
        body,
        mesh=mesh,
        in_specs=(
            P(None, "blk", "along", None),
            P(None, "blk", "along", None),
            P("blk", "along", None),
            P("blk", "along", None, None),
            P("blk", "along", None, None),
            P("blk", "along", None, None),
            P("blk", None, None, None),
            P("blk", None),
            P("blk", None, None, None),
            P("blk", None),
        ),
        out_specs=P(None, "blk", "along", None),
        check_vma=False,
    )
```

```python
import functools
import math

import jax
import jax.numpy as jnp
from jax import lax
from jax.experimental import pallas as pl
from jax.experimental.pallas import tpu as pltpu
from jax.sharding import PartitionSpec as P

REACH = 6
LEAF = 256
RANK = 64
RHS = 3
LD = 24
TALL = LD + 2
ROWS = 32
PACKED = 40
SHARPNESS = 2.0
KERNEL_SCALE = 0.125
LOG2E = math.log2(math.e)
F32 = jnp.float32
BF16 = jnp.bfloat16
EXACT = lax.Precision.HIGHEST
VMEM = pl.BlockSpec(memory_space=pltpu.VMEM)
HBM = pl.BlockSpec(memory_space=pltpu.HBM)
SMEM = pl.BlockSpec(memory_space=pltpu.SMEM)
BY_LAST = (((1,), (1,)), ((), ()))
MIB = 2**20
FULL = 60 * MIB + 128 * 1024
TURN_OWN = 6
TURN = 3
UP_PARTS = 4
UP_LEAVES = LD // UP_PARTS


def call(kernel, outs, ins, scratch=(), flops=0, bytes=1 << 20, vmem=16 * MIB):
    return pl.pallas_call(
        kernel,
        out_shape=outs,
        in_specs=ins,
        out_specs=jax.tree.map(lambda _: VMEM, outs),
        scratch_shapes=list(scratch),
        compiler_params=pltpu.CompilerParams(vmem_limit_bytes=vmem),
        cost_estimate=pl.CostEstimate(flops=flops, bytes_accessed=bytes, transcendentals=0),
    )


def shaped(*shape):
    return jax.ShapeDtypeStruct(shape, F32)


def halves(x):
    high = x.astype(BF16).astype(F32)
    return high, x - high


def upward_kernel(
    values_hbm, offsets_hbm, stiffness_hbm, basis_hbm, transfer_hbm, slab_hbm, wire_ref, slots_ref,
    values_ref, offsets_ref, stiffness_ref, basis_ref, transfer_ref, slab_ref, sems,
):
    lane = lax.broadcasted_iota(jnp.int32, (RANK, 128), 1)
    small = [
        pltpu.make_async_copy(source, target, sems.at[n])
        for n, (source, target) in enumerate(
            ((values_hbm, values_ref), (offsets_hbm, offsets_ref), (stiffness_hbm, stiffness_ref), (slab_hbm, slab_ref))
        )
    ]
    large = []
    for part in range(UP_PARTS):
        piece = pl.ds(part * UP_LEAVES, UP_LEAVES)
        large.append(
            [
                pltpu.make_async_copy(source.at[piece], target.at[piece], sems.at[4 + 2 * part + n])
                for n, (source, target) in enumerate(((basis_hbm, basis_ref), (transfer_hbm, transfer_ref)))
            ]
        )
    for copy in small + [copy for pair in large for copy in pair]:
        copy.start()
    for copy in small:
        copy.wait()

    def record(l, _):
        row = pl.ds(l, 1)
        for r in range(3):
            wire_ref[l, r : r + 1, :] = offsets_ref[r, row, :] - 0.5
            wire_ref[l, 4 + r : 5 + r, :] = values_ref[r, row, :]
        wire_ref[l, 3:4, :] = stiffness_ref[row, :]
        return 0

    lax.fori_loop(0, LD, record, 0, unroll=4)

    def leaf(l, carry):
        sums, columns = carry
        row = pl.ds(l, 1)
        new_sums = []
        basis = basis_ref[l]
        transfer = transfer_ref[l]
        for r in range(3):
            column = jnp.sum(basis * values_ref[r, row, :], axis=1, keepdims=True)
            new_sums.append(sums[r] + transfer * column)
            columns = jnp.where(lane == r * ROWS + l, column, columns)
        return tuple(new_sums), columns

    nothing = jnp.zeros((RANK, RANK), F32)
    carry = ((nothing,) * 3, jnp.zeros((RANK, 128), F32))
    for part in range(UP_PARTS):
        for copy in large[part]:
            copy.wait()
        carry = lax.fori_loop(part * UP_LEAVES, (part + 1) * UP_LEAVES, leaf, carry, unroll=UP_LEAVES)
    sums, columns = carry
    rows = jnp.transpose(columns, (1, 0))
    coefs = jnp.concatenate(
        [rows[:LD], rows[ROWS : ROWS + LD], rows[2 * ROWS : 2 * ROWS + LD], jnp.zeros((LD, RANK), F32)], 1
    )
    for l in range(LD):
        wire_ref[l, 7:8, :] = coefs[l : l + 1]
    slab_rows = jnp.concatenate(
        [jnp.sum(s, axis=0, keepdims=True) for s in sums] + [jnp.zeros((5, RANK), F32)], 0
    )
    share = jnp.dot(slab_rows, slab_ref[...], precision=EXACT, preferred_element_type=F32)
    share = jnp.concatenate([share, jnp.zeros((8, 128 - RANK), F32)], 1)
    here = lax.axis_index("along")
    for j in range(8):
        slots_ref[j, :, :LEAF] = jnp.where(j < here, wire_ref[0], wire_ref[LD - 1])
        slots_ref[j, :, LEAF:] = share


def tall_kernel(came_ref, wire_ref, tall_ref):
    here = lax.axis_index("along")
    lower = came_ref[jnp.maximum(here - 1, 0), :, :LEAF]
    upper = came_ref[jnp.minimum(here + 1, 7), :, :LEAF]
    tall_ref[0] = jnp.where(here > 0, lower, 0.0)
    tall_ref[1 : LD + 1] = wire_ref[...]
    tall_ref[LD + 1] = jnp.where(here < 7, upper, 0.0)


def whole_kernel(came_ref, whole_ref):
    total = came_ref[0, :, LEAF:]
    for j in range(1, 8):
        total = total + came_ref[j, :, LEAF:]
    both = jnp.concatenate(
        [
            jnp.concatenate([total[0:1, :RANK], total[1:2, :RANK]], 1),
            jnp.concatenate([total[2:3, :RANK], jnp.zeros((1, RANK), F32)], 1),
        ],
        0,
    )
    whole_ref[...] = jnp.broadcast_to(both[None], whole_ref.shape)


def source_side(leaf, around, steps, slot, points_ref, loads_ref):
    high, low = halves(leaf)
    points_ref[slot] = jnp.transpose(jnp.concatenate([high, low, low, high], 0), (1, 0)).astype(BF16)
    c0, c1, c2 = leaf[0:1], leaf[1:2], leaf[2:3]
    flat = (c0 + around) * (c0 + around) + c2 * c2
    for step in steps:
        weight = jnp.exp2((-SHARPNESS * LOG2E) * (flat + (c1 + step) * (c1 + step))) * leaf[3:4]
        loads_ref[slot, step + 1] = jnp.concatenate(halves(leaf * weight), 0).astype(BF16)


def target_points(leaf):
    row = lax.broadcasted_iota(jnp.int32, leaf.shape, 0)
    high, low = halves(jnp.where(row < 3, leaf * (2 * SHARPNESS * LOG2E), 0.0))
    return jnp.concatenate([high, low, high, low], 0).astype(BF16)


def pair_kernels(target, points_ref, slot, pairs_ref, place):
    points = points_ref[pl.ds(slot, 3)].reshape(3 * LEAF, 32)
    pairs = jnp.exp2(jnp.dot(points, target, preferred_element_type=F32))
    for step in range(3):
        pair = pairs[step * LEAF : (step + 1) * LEAF]
        high = pair.astype(BF16)
        pairs_ref[place + step, 0] = high
        pairs_ref[place + step, 1] = (pair - high.astype(F32)).astype(BF16)


def pair_kernel(target, points_ref, slot, pairs_ref, place):
    power = jnp.dot(points_ref[slot], target, preferred_element_type=F32)
    pair = jnp.exp2(power)
    high = pair.astype(BF16)
    pairs_ref[place, 0] = high
    pairs_ref[place, 1] = (pair - high.astype(F32)).astype(BF16)


def pair_sum(leaf, loads_ref, slot, pairs_ref, place, around, step):
    c0, c1, c2 = leaf[0:1], leaf[1:2], leaf[2:3]
    loads = loads_ref[slot, step + 1]
    rows = jnp.dot(loads, pairs_ref[place, 0], preferred_element_type=F32) + jnp.dot(
        loads, pairs_ref[place, 1], preferred_element_type=F32
    )
    power = (2 * SHARPNESS * LOG2E) * (around * c0 + step * c1) - (SHARPNESS * LOG2E) * (c0 * c0 + c1 * c1 + c2 * c2)
    weight = jnp.exp2(power) * (KERNEL_SCALE * leaf[3:4])
    return weight * (rows[:8] + rows[8:])


def near_own_kernel(wire_ref, near_ref, points_ref, loads_ref, pairs_ref):
    points_ref[0] = jnp.zeros((LEAF, 32), BF16)
    points_ref[LD + 1] = jnp.zeros((LEAF, 32), BF16)
    loads_ref[0] = jnp.zeros((3, 16, LEAF), BF16)
    loads_ref[LD + 1] = jnp.zeros((3, 16, LEAF), BF16)

    def prepare(l, _):
        source_side(wire_ref[l], 0, (-1, 0, 1), l + 1, points_ref, loads_ref)
        return 0

    lax.fori_loop(0, LD, prepare, 0, unroll=12)

    def turn(g, _):
        leaves = [g * TURN_OWN + n for n in range(TURN_OWN)]
        places = [(n, step) for n in range(TURN_OWN) for step in (-1, 0, 1)]
        targets = [target_points(wire_ref[l]) for l in leaves]
        for n in range(TURN_OWN):
            pair_kernels(targets[n], points_ref, leaves[n], pairs_ref, 3 * n)
        totals = [jnp.zeros((8, LEAF), F32)] * TURN_OWN
        for place, (n, step) in enumerate(places):
            totals[n] += pair_sum(wire_ref[leaves[n]], loads_ref, leaves[n] + 1 + step, pairs_ref, place, 0, step)
        for n in range(TURN_OWN):
            near_ref[leaves[n]] = totals[n]
        return 0

    lax.fori_loop(0, LD // TURN_OWN, turn, 0)


def near_side_kernel(beyond, tall_ref, came_ref, near_ref, points_ref, loads_ref, pairs_ref):
    odd = lax.rem(lax.axis_index("blk"), 2)
    around = ((2 * odd - 1) if beyond else (1 - 2 * odd)).astype(F32)

    def prepare(l, _):
        source_side(came_ref[l], around, (-1, 0, 1), l, points_ref, loads_ref)
        return 0

    lax.fori_loop(0, TALL, prepare, 0, unroll=13)
    end, end_leaf, end_step = (LD + 1, LD - 1, 1) if beyond else (0, 0, -1)
    source_side(tall_ref[end], 0, (end_step,), TALL, points_ref, loads_ref)

    def turn(g, _):
        leaves = [g * TURN + n for n in range(TURN)]
        places = [(n, step) for n in range(TURN) for step in (-1, 0, 1)]
        targets = [target_points(tall_ref[l + 1]) for l in leaves]
        for n in range(TURN):
            pair_kernels(targets[n], points_ref, leaves[n], pairs_ref, 3 * n)
        totals = [jnp.zeros((8, LEAF), F32)] * TURN
        for place, (n, step) in enumerate(places):
            slot = leaves[n] + 1 + step
            totals[n] += pair_sum(tall_ref[leaves[n] + 1], loads_ref, slot, pairs_ref, place, around, step)
        for n in range(TURN):
            near_ref[leaves[n]] = totals[n]
        return 0

    lax.fori_loop(0, LD // TURN, turn, 0)
    here = tall_ref[end_leaf + 1]
    pair_kernel(target_points(here), points_ref, TALL, pairs_ref, 0)
    near_ref[end_leaf] += pair_sum(here, loads_ref, TALL, pairs_ref, 0, 0, end_step)


def near_scratch(leaves, places):
    return [
        pltpu.VMEM((leaves, LEAF, 32), BF16),
        pltpu.VMEM((leaves, 3, 16, LEAF), BF16),
        pltpu.VMEM((places, 2, LEAF, LEAF), BF16),
    ]


def packed(rows):
    third = rows[:, 2 * RANK : 3 * RANK]
    third = jnp.concatenate([third[: TALL // 2], third[TALL // 2 :]], 1)
    return jnp.concatenate([rows[:, : 2 * RANK], third, jnp.zeros((PACKED - TALL - TALL // 2, 128), F32)], 0)


def coefs_of(tall_ref):
    return jnp.concatenate([tall_ref[l, 7:8, :] for l in range(TALL)], 0)


def pair_records_kernel(tall_ref, partner_ref, records_ref):
    records_ref[:TALL] = tall_ref[...]
    rows = jnp.concatenate([coefs_of(partner_ref), jnp.zeros((ROWS - TALL, LEAF), F32)], 0)
    for n in range(ROWS // 8):
        records_ref[TALL + n] = rows[8 * n : 8 * n + 8]


def is_even():
    return lax.rem(lax.axis_index("blk"), 2) == 0


def quad_kernel(tall_ref, partner_ref, came_ref, quad_ref):
    own, partner = packed(coefs_of(tall_ref)), packed(coefs_of(partner_ref))
    first = packed(coefs_of(came_ref))
    second = packed(jnp.concatenate([came_ref[TALL + n] for n in range(ROWS // 8)], 0)[:TALL])
    for n, (if_even, if_odd) in enumerate(((second, partner), (first, own), (own, first), (partner, second))):
        quad_ref[n] = jnp.where(is_even(), if_even, if_odd)


def outer_kernel(quad_ref, onward_ref, outer_ref):
    for n in range(6):
        if_even = onward_ref[n] if n < 4 else quad_ref[n - 4]
        if_odd = quad_ref[n + 2] if n < 2 else onward_ref[n - 2]
        outer_ref[n] = jnp.where(is_even(), if_even, if_odd)


def exact_by_last(x, y):
    return lax.dot_general(x, y, BY_LAST, precision=EXACT, preferred_element_type=F32)


def three_by_last(x, y):
    (xh, xl), (yh, yl) = halves(x), halves(y)
    xh, xl, yh, yl = (z.astype(BF16) for z in (xh, xl, yh, yl))
    high = lax.dot_general(xh, yh, BY_LAST, preferred_element_type=F32)
    cross = lax.dot_general(xl, yh, BY_LAST, preferred_element_type=F32)
    return high + (cross + lax.dot_general(xh, yl, BY_LAST, preferred_element_type=F32))


def top_kernel(admissible_ref, every_ref, top_ref, slab_ref, down_ref, first_ref, second_ref):
    sectors = top_ref.shape[0]
    apart = lax.rem(lax.broadcasted_iota(jnp.int32, (8, sectors), 1) - lax.axis_index("blk") + sectors, sectors)
    distant = jnp.logical_and(apart > REACH, apart < sectors - REACH)
    allowed = jnp.where(distant, admissible_ref[...], 0).astype(F32)
    allowed = jnp.transpose(jnp.concatenate([allowed, jnp.zeros((8, 128 - sectors), F32)], 1), (1, 0))[:sectors, :1]
    first_ref[...] = every_ref[:, 0, :] * allowed
    second_ref[...] = every_ref[:, 1, :] * allowed

    def couple(t, sums):
        coupling = top_ref[t]
        first, second = first_ref[pl.ds(t, 1), :], second_ref[pl.ds(t, 1), :]
        rows = (first[:, :RANK], first[:, RANK:], second[:, :RANK])
        return tuple(s + coupling * row for s, row in zip(sums, rows))

    nothing = jnp.zeros((RANK, RANK), F32)
    sums = lax.fori_loop(0, sectors, couple, (nothing,) * 3, unroll=16)
    lane = lax.broadcasted_iota(jnp.int32, (RANK, 128), 1)
    columns = jnp.zeros((RANK, 128), F32)
    for r in range(3):
        columns = jnp.where(lane == r, jnp.sum(sums[r], axis=1, keepdims=True), columns)
    local = jnp.transpose(columns, (1, 0))[:8]
    down_ref[...] = exact_by_last(local, slab_ref[...])


def finish_kernel(mask_ref, *refs):
    count = len(refs) - 3
    local, out_ref = refs[:count], refs[count]
    far_ref, ring_ref = refs[count + 1 :]
    coupling_ref, quad_ref, outer_ref, other_ref = local[:4]
    down_ref, transfer_ref, basis_ref, own_ref, side_ref, beyond_ref = local[4:]
    slab = down_ref[...]

    here = lax.axis_index("blk")
    odd = lax.rem(here, 2)
    for n in range(6):
        ring_ref[n] = jnp.where(odd == 0, outer_ref[n], other_ref[n])
        ring_ref[n + 8] = jnp.where(odd == 0, other_ref[n], outer_ref[n])
    for n in range(2):
        ring_ref[n + 6] = jnp.where(odd == 0, quad_ref[n + 2], quad_ref[n])
    mask = mask_ref[...].astype(F32)
    total = jnp.zeros((3 * ROWS, 3 * RANK), F32)
    for q in range(2 * (REACH - 1)):
        around = q + 2 if q < REACH - 1 else 3 - q
        rows = ring_ref[odd + (REACH + around)]
        gap = jnp.zeros((ROWS - TALL, RANK), F32)
        third = rows[TALL : TALL + TALL // 2]
        stacked = jnp.concatenate(
            [rows[:TALL, :RANK], gap, rows[:TALL, RANK:], gap, third[:, :RANK], third[:, RANK:], gap], 0
        )
        coupling = jnp.concatenate(
            [coupling_ref[3 * q + b] * mask[:, 3 * q + b : 3 * q + b + 1] for b in range(3)], 0
        )
        total = total + three_by_last(stacked, coupling)
    far = []
    for r in range(3):
        block = total[r * ROWS : (r + 1) * ROWS]
        rows = block[0:LD, :RANK] + block[1 : LD + 1, RANK : 2 * RANK] + block[2 : LD + 2, 2 * RANK :]
        far.append(jnp.concatenate([rows, jnp.zeros((ROWS - LD, RANK), F32)], 0))
    far.append(jnp.zeros((ROWS, RANK), F32))
    columns = jnp.transpose(jnp.concatenate(far, 0), (1, 0))
    far_columns = [columns[:, r * ROWS : (r + 1) * ROWS] for r in range(3)]
    for r in range(3):
        far_ref[r] = jnp.concatenate([far_columns[r], jnp.zeros((RANK, RANK - ROWS), F32)], 1)

    place = lax.broadcasted_iota(jnp.int32, (RANK, RANK), 1)

    def leaf(l, _):
        basis = basis_ref[l]
        transfer = transfer_ref[l]
        near = own_ref[l] + side_ref[l] + beyond_ref[l]
        for r in range(3):
            terms = transfer * slab[r : r + 1] + jnp.where(place == l, far_ref[r], 0.0)
            column = jnp.sum(terms, axis=1, keepdims=True)
            out_ref[r, pl.ds(l, 1), :] = jnp.sum(basis * column, axis=0, keepdims=True) + near[4 + r : 5 + r]
        return 0

    lax.fori_loop(0, LD, leaf, 0, unroll=8)


def upward(*args):
    outs = (shaped(LD, 8, LEAF), shaped(8, 8, LEAF + 128))
    scratch = [pltpu.VMEM(x.shape, F32) for x in args] + [pltpu.SemaphoreType.DMA((4 + 2 * UP_PARTS,))]
    return call(upward_kernel, outs, [HBM] * 6, scratch, flops=10**9, vmem=FULL)(*args)


def near_own(wire):
    scratch = near_scratch(TALL, 3 * TURN_OWN)
    return call(near_own_kernel, shaped(LD, 8, LEAF), [VMEM], scratch, flops=9 * 10**9)(wire)


def near_side(beyond, *args):
    kernel = functools.partial(near_side_kernel, beyond)
    scratch = near_scratch(TALL + 1, 3 * TURN)
    return call(kernel, shaped(LD, 8, LEAF), [VMEM, VMEM], scratch, flops=9 * 10**9, bytes=2 * 10**7)(*args)


def finish(*args):
    scratch = [pltpu.VMEM((3, RANK, RANK), F32), pltpu.VMEM((14, PACKED, 128), F32)]
    ins = [VMEM] * len(args)
    return call(finish_kernel, shaped(RHS, LD, LEAF), ins, scratch, flops=4 * 10**9)(*args)


def top(*args):
    scratch = [pltpu.VMEM((args[2].shape[0], 128), F32)] * 2
    return call(top_kernel, shaped(8, RANK), [VMEM] * 4, scratch, flops=10**9)(*args)


def body(
    values,
    offsets,
    stiffness,
    leaf_basis,
    transfer,
    slab_transfer_matrices,
    leaf_coupling_matrices,
    leaf_admissible_mask,
    top_coupling,
    top_admissible,
):
    sectors = lax.axis_size("blk")
    values = values[:, 0]
    offsets = offsets[:, 0]
    basis = leaf_basis[0]
    transfer = transfer[0]
    slab = slab_transfer_matrices[0, 0]

    wire, slots = upward(values, offsets, stiffness[0], basis, transfer, slab)
    came = lax.all_to_all(slots, "along", 0, 0, tiled=True)
    own = near_own(wire)
    came, own = lax.optimization_barrier((came, own))
    tall = call(tall_kernel, shaped(TALL, 8, LEAF), [VMEM, VMEM])(came, wire)
    tall, came = lax.optimization_barrier((tall, came))
    whole = call(whole_kernel, shaped(sectors, 2, 128), [VMEM])(came)
    flip = [(i, i ^ 1) for i in range(sectors)]
    step_out = [(i, (i + 1 if i % 2 else i - 1) % sectors) for i in range(sectors)]
    stride = [(i, (i - 4 if i % 2 else i + 4) % sectors) for i in range(sectors)]
    partner = lax.ppermute(tall, "blk", flip)
    records = call(pair_records_kernel, shaped(TALL + ROWS // 8, 8, LEAF), [VMEM] * 2)(tall, partner)
    records, partner = lax.optimization_barrier((records, partner))
    came = lax.ppermute(records, "blk", step_out)
    side = near_side(False, tall, partner)
    came, side = lax.optimization_barrier((came, side))
    every = lax.all_to_all(whole, "blk", 0, 0, tiled=True)
    quad = call(quad_kernel, shaped(4, PACKED, 128), [VMEM] * 3)(tall, partner, came)
    onward = lax.ppermute(quad, "blk", stride)
    quad, came, every = lax.optimization_barrier((quad, came, every))
    beyond = near_side(True, tall, came)
    onward, beyond, every = lax.optimization_barrier((onward, beyond, every))
    outer = call(outer_kernel, shaped(6, PACKED, 128), [VMEM] * 2)(quad, onward)
    other = lax.ppermute(outer, "blk", flip)
    down = top(
        top_admissible, every, top_coupling[0], slab
    )
    out = finish(
        leaf_admissible_mask, leaf_coupling_matrices[0], quad, outer, other, down,
        transfer, basis, own, side, beyond,
    )
    return out[:, None]


def solution(mesh):
    return jax.shard_map(
        body,
        mesh=mesh,
        in_specs=(
            P(None, "blk", "along", None),
            P(None, "blk", "along", None),
            P("blk", "along", None),
            P("blk", "along", None, None),
            P("blk", "along", None, None),
            P("blk", "along", None, None),
            P("blk", None, None, None),
            P("blk", None),
            P("blk", None, None, None),
            P("blk", None),
        ),
        out_specs=P(None, "blk", "along", None),
        check_vma=False,
    )
```

```python
import functools
import math

import jax
import jax.numpy as jnp
from jax import lax
from jax.experimental import pallas as pl
from jax.experimental.pallas import tpu as pltpu
from jax.sharding import PartitionSpec as P

REACH = 6
LEAF = 256
RANK = 64
RHS = 3
LD = 24
TALL = LD + 2
ROWS = 32
PACKED = 40
SHARPNESS = 2.0
KERNEL_SCALE = 0.125
LOG2E = math.log2(math.e)
F32 = jnp.float32
BF16 = jnp.bfloat16
EXACT = lax.Precision.HIGHEST
VMEM = pl.BlockSpec(memory_space=pltpu.VMEM)
HBM = pl.BlockSpec(memory_space=pltpu.HBM)
SMEM = pl.BlockSpec(memory_space=pltpu.SMEM)
BY_LAST = (((1,), (1,)), ((), ()))
MIB = 2**20
FULL = 60 * MIB + 128 * 1024
TURN_OWN = 6
TURN = 3
EARLY = 18
LATE = LD - EARLY
UP_PARTS = 4
UP_LEAVES = LD // UP_PARTS


def call(kernel, outs, ins, scratch=(), flops=0, bytes=1 << 20, vmem=16 * MIB):
    return pl.pallas_call(
        kernel,
        out_shape=outs,
        in_specs=ins,
        out_specs=jax.tree.map(lambda _: VMEM, outs),
        scratch_shapes=list(scratch),
        compiler_params=pltpu.CompilerParams(vmem_limit_bytes=vmem),
        cost_estimate=pl.CostEstimate(flops=flops, bytes_accessed=bytes, transcendentals=0),
    )


def shaped(*shape):
    return jax.ShapeDtypeStruct(shape, F32)


def halves(x):
    high = x.astype(BF16).astype(F32)
    return high, x - high


def upward_kernel(
    values_hbm, offsets_hbm, stiffness_hbm, basis_hbm, transfer_hbm, slab_hbm, wire_ref, slots_ref,
    values_ref, offsets_ref, stiffness_ref, basis_ref, transfer_ref, slab_ref, sems,
):
    lane = lax.broadcasted_iota(jnp.int32, (RANK, 128), 1)
    small = [
        pltpu.make_async_copy(source, target, sems.at[n])
        for n, (source, target) in enumerate(
            ((values_hbm, values_ref), (offsets_hbm, offsets_ref), (stiffness_hbm, stiffness_ref), (slab_hbm, slab_ref))
        )
    ]
    large = []
    for part in range(UP_PARTS):
        piece = pl.ds(part * UP_LEAVES, UP_LEAVES)
        large.append(
            [
                pltpu.make_async_copy(source.at[piece], target.at[piece], sems.at[4 + 2 * part + n])
                for n, (source, target) in enumerate(((basis_hbm, basis_ref), (transfer_hbm, transfer_ref)))
            ]
        )
    for copy in small + [copy for pair in large for copy in pair]:
        copy.start()
    for copy in small:
        copy.wait()

    def record(l, _):
        row = pl.ds(l, 1)
        for r in range(3):
            wire_ref[l, r : r + 1, :] = offsets_ref[r, row, :] - 0.5
            wire_ref[l, 4 + r : 5 + r, :] = values_ref[r, row, :]
        wire_ref[l, 3:4, :] = stiffness_ref[row, :]
        return 0

    lax.fori_loop(0, LD, record, 0, unroll=4)

    def leaf(l, carry):
        sums, columns = carry
        row = pl.ds(l, 1)
        new_sums = []
        basis = basis_ref[l]
        transfer = transfer_ref[l]
        for r in range(3):
            column = jnp.sum(basis * values_ref[r, row, :], axis=1, keepdims=True)
            new_sums.append(sums[r] + transfer * column)
            columns = jnp.where(lane == r * ROWS + l, column, columns)
        return tuple(new_sums), columns

    nothing = jnp.zeros((RANK, RANK), F32)
    carry = ((nothing,) * 3, jnp.zeros((RANK, 128), F32))
    for part in range(UP_PARTS):
        for copy in large[part]:
            copy.wait()
        carry = lax.fori_loop(part * UP_LEAVES, (part + 1) * UP_LEAVES, leaf, carry, unroll=UP_LEAVES)
    sums, columns = carry
    rows = jnp.transpose(columns, (1, 0))
    coefs = jnp.concatenate(
        [rows[:LD], rows[ROWS : ROWS + LD], rows[2 * ROWS : 2 * ROWS + LD], jnp.zeros((LD, RANK), F32)], 1
    )
    for l in range(LD):
        wire_ref[l, 7:8, :] = coefs[l : l + 1]
    slab_rows = jnp.concatenate(
        [jnp.sum(s, axis=0, keepdims=True) for s in sums] + [jnp.zeros((5, RANK), F32)], 0
    )
    share = jnp.dot(slab_rows, slab_ref[...], precision=EXACT, preferred_element_type=F32)
    share = jnp.concatenate([share, jnp.zeros((8, 128 - RANK), F32)], 1)
    here = lax.axis_index("along")
    for j in range(8):
        slots_ref[j, :, :LEAF] = jnp.where(j < here, wire_ref[0], wire_ref[LD - 1])
        slots_ref[j, :, LEAF:] = share


def tall_kernel(came_ref, wire_ref, tall_ref):
    here = lax.axis_index("along")
    lower = came_ref[jnp.maximum(here - 1, 0), :, :LEAF]
    upper = came_ref[jnp.minimum(here + 1, 7), :, :LEAF]
    tall_ref[0] = jnp.where(here > 0, lower, 0.0)
    tall_ref[1 : LD + 1] = wire_ref[...]
    tall_ref[LD + 1] = jnp.where(here < 7, upper, 0.0)


def whole_kernel(came_ref, whole_ref):
    total = came_ref[0, :, LEAF:]
    for j in range(1, 8):
        total = total + came_ref[j, :, LEAF:]
    both = jnp.concatenate(
        [
            jnp.concatenate([total[0:1, :RANK], total[1:2, :RANK]], 1),
            jnp.concatenate([total[2:3, :RANK], jnp.zeros((1, RANK), F32)], 1),
        ],
        0,
    )
    whole_ref[...] = jnp.broadcast_to(both[None], whole_ref.shape)


def source_side(leaf, around, steps, slot, points_ref, loads_ref):
    high, low = halves(leaf)
    points_ref[slot] = jnp.transpose(jnp.concatenate([high, low, low, high], 0), (1, 0)).astype(BF16)
    c0, c1, c2 = leaf[0:1], leaf[1:2], leaf[2:3]
    flat = (c0 + around) * (c0 + around) + c2 * c2
    for step in steps:
        weight = jnp.exp2((-SHARPNESS * LOG2E) * (flat + (c1 + step) * (c1 + step))) * leaf[3:4]
        loads_ref[slot, step + 1] = jnp.concatenate(halves(leaf * weight), 0).astype(BF16)


def target_points(leaf):
    row = lax.broadcasted_iota(jnp.int32, leaf.shape, 0)
    high, low = halves(jnp.where(row < 3, leaf * (2 * SHARPNESS * LOG2E), 0.0))
    return jnp.concatenate([high, low, high, low], 0).astype(BF16)


def pair_kernels(target, points_ref, slot, pairs_ref, place):
    points = points_ref[pl.ds(slot, 3)].reshape(3 * LEAF, 32)
    pairs = jnp.exp2(jnp.dot(points, target, preferred_element_type=F32))
    for step in range(3):
        pair = pairs[step * LEAF : (step + 1) * LEAF]
        high = pair.astype(BF16)
        pairs_ref[place + step, 0] = high
        pairs_ref[place + step, 1] = (pair - high.astype(F32)).astype(BF16)


def pair_kernel(target, points_ref, slot, pairs_ref, place):
    power = jnp.dot(points_ref[slot], target, preferred_element_type=F32)
    pair = jnp.exp2(power)
    high = pair.astype(BF16)
    pairs_ref[place, 0] = high
    pairs_ref[place, 1] = (pair - high.astype(F32)).astype(BF16)


def pair_sum(leaf, loads_ref, slot, pairs_ref, place, around, step):
    c0, c1, c2 = leaf[0:1], leaf[1:2], leaf[2:3]
    loads = loads_ref[slot, step + 1]
    rows = jnp.dot(loads, pairs_ref[place, 0], preferred_element_type=F32) + jnp.dot(
        loads, pairs_ref[place, 1], preferred_element_type=F32
    )
    power = (2 * SHARPNESS * LOG2E) * (around * c0 + step * c1) - (SHARPNESS * LOG2E) * (c0 * c0 + c1 * c1 + c2 * c2)
    weight = jnp.exp2(power) * (KERNEL_SCALE * leaf[3:4])
    return weight * (rows[:8] + rows[8:])


def near_own_kernel(wire_ref, near_ref, points_ref, loads_ref, pairs_ref):
    points_ref[0] = jnp.zeros((LEAF, 32), BF16)
    loads_ref[0] = jnp.zeros((3, 16, LEAF), BF16)

    def prepare(l, _):
        source_side(wire_ref[l], 0, (-1, 0, 1), l + 1, points_ref, loads_ref)
        return 0

    lax.fori_loop(0, EARLY + 1, prepare, 0, unroll=EARLY + 1)

    def turn(g, _):
        leaves = [g * TURN_OWN + n for n in range(TURN_OWN)]
        places = [(n, step) for n in range(TURN_OWN) for step in (-1, 0, 1)]
        targets = [target_points(wire_ref[l]) for l in leaves]
        for n in range(TURN_OWN):
            pair_kernels(targets[n], points_ref, leaves[n], pairs_ref, 3 * n)
        totals = [jnp.zeros((8, LEAF), F32)] * TURN_OWN
        for place, (n, step) in enumerate(places):
            totals[n] += pair_sum(wire_ref[leaves[n]], loads_ref, leaves[n] + 1 + step, pairs_ref, place, 0, step)
        for n in range(TURN_OWN):
            near_ref[leaves[n]] = totals[n]
        return 0

    lax.fori_loop(0, EARLY // TURN_OWN, turn, 0)
    near_ref[EARLY:] = jnp.zeros((LD - EARLY, 8, LEAF), F32)


def near_side_kernel(beyond, tall_ref, came_ref, near_ref, points_ref, loads_ref, pairs_ref):
    odd = lax.rem(lax.axis_index("blk"), 2)
    around = ((2 * odd - 1) if beyond else (1 - 2 * odd)).astype(F32)

    def prepare(l, _):
        source_side(came_ref[l], around, (-1, 0, 1), l, points_ref, loads_ref)
        return 0

    lax.fori_loop(0, TALL, prepare, 0, unroll=13)

    def add_leaves(leaves, slots, side):
        count = len(leaves)
        places = [(n, step) for n in range(count) for step in (-1, 0, 1)]
        targets = [target_points(tall_ref[l + 1]) for l in leaves]
        for n in range(count):
            pair_kernels(targets[n], points_ref, slots[n], pairs_ref, 3 * n)
        totals = [jnp.zeros((8, LEAF), F32)] * count
        for place, (n, step) in enumerate(places):
            slot = slots[n] + 1 + step
            totals[n] += pair_sum(tall_ref[leaves[n] + 1], loads_ref, slot, pairs_ref, place, side, step)
        return totals

    def turn(g, _):
        leaves = [g * TURN + n for n in range(TURN)]
        for l, total in zip(leaves, add_leaves(leaves, leaves, around)):
            near_ref[l] = total
        return 0

    lax.fori_loop(0, LD // TURN, turn, 0)
    if beyond:
        return
    for n in range(LATE + 2):
        source_side(tall_ref[EARLY + n], 0, (-1, 0, 1), TALL + n, points_ref, loads_ref)
    for first in range(0, LATE, TURN):
        leaves = [EARLY + first + n for n in range(TURN)]
        slots = [TALL + first + n for n in range(TURN)]
        for l, total in zip(leaves, add_leaves(leaves, slots, 0)):
            near_ref[l] += total
    last = TALL + LATE + 2
    source_side(tall_ref[0], 0, (-1,), last, points_ref, loads_ref)
    here = tall_ref[1]
    pair_kernel(target_points(here), points_ref, last, pairs_ref, 0)
    near_ref[0] += pair_sum(here, loads_ref, last, pairs_ref, 0, 0, -1)


def near_scratch(leaves, places):
    return [
        pltpu.VMEM((leaves, LEAF, 32), BF16),
        pltpu.VMEM((leaves, 3, 16, LEAF), BF16),
        pltpu.VMEM((places, 2, LEAF, LEAF), BF16),
    ]


def packed(rows):
    third = rows[:, 2 * RANK : 3 * RANK]
    third = jnp.concatenate([third[: TALL // 2], third[TALL // 2 :]], 1)
    return jnp.concatenate([rows[:, : 2 * RANK], third, jnp.zeros((PACKED - TALL - TALL // 2, 128), F32)], 0)


def coefs_of(tall_ref):
    return jnp.concatenate([tall_ref[l, 7:8, :] for l in range(TALL)], 0)


def pair_records_kernel(tall_ref, partner_ref, records_ref):
    records_ref[:TALL] = tall_ref[...]
    rows = jnp.concatenate([coefs_of(partner_ref), jnp.zeros((ROWS - TALL, LEAF), F32)], 0)
    for n in range(ROWS // 8):
        records_ref[TALL + n] = rows[8 * n : 8 * n + 8]


def is_even():
    return lax.rem(lax.axis_index("blk"), 2) == 0


def quad_kernel(tall_ref, partner_ref, came_ref, quad_ref):
    own, partner = packed(coefs_of(tall_ref)), packed(coefs_of(partner_ref))
    first = packed(coefs_of(came_ref))
    second = packed(jnp.concatenate([came_ref[TALL + n] for n in range(ROWS // 8)], 0)[:TALL])
    for n, (if_even, if_odd) in enumerate(((second, partner), (first, own), (own, first), (partner, second))):
        quad_ref[n] = jnp.where(is_even(), if_even, if_odd)


def outer_kernel(quad_ref, onward_ref, outer_ref):
    for n in range(6):
        if_even = onward_ref[n] if n < 4 else quad_ref[n - 4]
        if_odd = quad_ref[n + 2] if n < 2 else onward_ref[n - 2]
        outer_ref[n] = jnp.where(is_even(), if_even, if_odd)


def exact_by_last(x, y):
    return lax.dot_general(x, y, BY_LAST, precision=EXACT, preferred_element_type=F32)


def three_by_last(x, y):
    (xh, xl), (yh, yl) = halves(x), halves(y)
    xh, xl, yh, yl = (z.astype(BF16) for z in (xh, xl, yh, yl))
    high = lax.dot_general(xh, yh, BY_LAST, preferred_element_type=F32)
    cross = lax.dot_general(xl, yh, BY_LAST, preferred_element_type=F32)
    return high + (cross + lax.dot_general(xh, yl, BY_LAST, preferred_element_type=F32))


def top_kernel(admissible_ref, every_ref, top_ref, slab_ref, down_ref, first_ref, second_ref):
    sectors = top_ref.shape[0]
    apart = lax.rem(lax.broadcasted_iota(jnp.int32, (8, sectors), 1) - lax.axis_index("blk") + sectors, sectors)
    distant = jnp.logical_and(apart > REACH, apart < sectors - REACH)
    allowed = jnp.where(distant, admissible_ref[...], 0).astype(F32)
    allowed = jnp.transpose(jnp.concatenate([allowed, jnp.zeros((8, 128 - sectors), F32)], 1), (1, 0))[:sectors, :1]
    first_ref[...] = every_ref[:, 0, :] * allowed
    second_ref[...] = every_ref[:, 1, :] * allowed

    def couple(t, sums):
        coupling = top_ref[t]
        first, second = first_ref[pl.ds(t, 1), :], second_ref[pl.ds(t, 1), :]
        rows = (first[:, :RANK], first[:, RANK:], second[:, :RANK])
        return tuple(s + coupling * row for s, row in zip(sums, rows))

    nothing = jnp.zeros((RANK, RANK), F32)
    sums = lax.fori_loop(0, sectors, couple, (nothing,) * 3, unroll=16)
    lane = lax.broadcasted_iota(jnp.int32, (RANK, 128), 1)
    columns = jnp.zeros((RANK, 128), F32)
    for r in range(3):
        columns = jnp.where(lane == r, jnp.sum(sums[r], axis=1, keepdims=True), columns)
    local = jnp.transpose(columns, (1, 0))[:8]
    down_ref[...] = exact_by_last(local, slab_ref[...])


def finish_kernel(mask_ref, *refs):
    count = len(refs) - 3
    local, out_ref = refs[:count], refs[count]
    far_ref, ring_ref = refs[count + 1 :]
    coupling_ref, quad_ref, outer_ref, other_ref = local[:4]
    down_ref, transfer_ref, basis_ref, own_ref, side_ref, beyond_ref = local[4:]
    slab = down_ref[...]

    here = lax.axis_index("blk")
    odd = lax.rem(here, 2)
    for n in range(6):
        ring_ref[n] = jnp.where(odd == 0, outer_ref[n], other_ref[n])
        ring_ref[n + 8] = jnp.where(odd == 0, other_ref[n], outer_ref[n])
    for n in range(2):
        ring_ref[n + 6] = jnp.where(odd == 0, quad_ref[n + 2], quad_ref[n])
    mask = mask_ref[...].astype(F32)
    total = jnp.zeros((3 * ROWS, 3 * RANK), F32)
    for q in range(2 * (REACH - 1)):
        around = q + 2 if q < REACH - 1 else 3 - q
        rows = ring_ref[odd + (REACH + around)]
        gap = jnp.zeros((ROWS - TALL, RANK), F32)
        third = rows[TALL : TALL + TALL // 2]
        stacked = jnp.concatenate(
            [rows[:TALL, :RANK], gap, rows[:TALL, RANK:], gap, third[:, :RANK], third[:, RANK:], gap], 0
        )
        coupling = jnp.concatenate(
            [coupling_ref[3 * q + b] * mask[:, 3 * q + b : 3 * q + b + 1] for b in range(3)], 0
        )
        total = total + three_by_last(stacked, coupling)
    far = []
    for r in range(3):
        block = total[r * ROWS : (r + 1) * ROWS]
        rows = block[0:LD, :RANK] + block[1 : LD + 1, RANK : 2 * RANK] + block[2 : LD + 2, 2 * RANK :]
        far.append(jnp.concatenate([rows, jnp.zeros((ROWS - LD, RANK), F32)], 0))
    far.append(jnp.zeros((ROWS, RANK), F32))
    columns = jnp.transpose(jnp.concatenate(far, 0), (1, 0))
    far_columns = [columns[:, r * ROWS : (r + 1) * ROWS] for r in range(3)]
    for r in range(3):
        far_ref[r] = jnp.concatenate([far_columns[r], jnp.zeros((RANK, RANK - ROWS), F32)], 1)

    place = lax.broadcasted_iota(jnp.int32, (RANK, RANK), 1)

    def leaf(l, _):
        basis = basis_ref[l]
        transfer = transfer_ref[l]
        near = own_ref[l] + side_ref[l] + beyond_ref[l]
        for r in range(3):
            terms = transfer * slab[r : r + 1] + jnp.where(place == l, far_ref[r], 0.0)
            column = jnp.sum(terms, axis=1, keepdims=True)
            out_ref[r, pl.ds(l, 1), :] = jnp.sum(basis * column, axis=0, keepdims=True) + near[4 + r : 5 + r]
        return 0

    lax.fori_loop(0, LD, leaf, 0, unroll=8)


def upward(*args):
    outs = (shaped(LD, 8, LEAF), shaped(8, 8, LEAF + 128))
    scratch = [pltpu.VMEM(x.shape, F32) for x in args] + [pltpu.SemaphoreType.DMA((4 + 2 * UP_PARTS,))]
    return call(upward_kernel, outs, [HBM] * 6, scratch, flops=10**9, vmem=FULL)(*args)


def near_own(wire):
    scratch = near_scratch(TALL, 3 * TURN_OWN)
    return call(near_own_kernel, shaped(LD, 8, LEAF), [VMEM], scratch, flops=9 * 10**9)(wire)


def near_side(beyond, *args):
    kernel = functools.partial(near_side_kernel, beyond)
    scratch = near_scratch(TALL + LATE + 3, 3 * TURN)
    return call(kernel, shaped(LD, 8, LEAF), [VMEM, VMEM], scratch, flops=9 * 10**9, bytes=2 * 10**7)(*args)


def finish(*args):
    scratch = [pltpu.VMEM((3, RANK, RANK), F32), pltpu.VMEM((14, PACKED, 128), F32)]
    ins = [VMEM] * len(args)
    return call(finish_kernel, shaped(RHS, LD, LEAF), ins, scratch, flops=4 * 10**9)(*args)


def top(*args):
    scratch = [pltpu.VMEM((args[2].shape[0], 128), F32)] * 2
    return call(top_kernel, shaped(8, RANK), [VMEM] * 4, scratch, flops=10**9)(*args)


def body(
    values,
    offsets,
    stiffness,
    leaf_basis,
    transfer,
    slab_transfer_matrices,
    leaf_coupling_matrices,
    leaf_admissible_mask,
    top_coupling,
    top_admissible,
):
    sectors = lax.axis_size("blk")
    values = values[:, 0]
    offsets = offsets[:, 0]
    basis = leaf_basis[0]
    transfer = transfer[0]
    slab = slab_transfer_matrices[0, 0]

    wire, slots = upward(values, offsets, stiffness[0], basis, transfer, slab)
    came = lax.all_to_all(slots, "along", 0, 0, tiled=True)
    own = near_own(wire)
    came, own = lax.optimization_barrier((came, own))
    tall = call(tall_kernel, shaped(TALL, 8, LEAF), [VMEM, VMEM])(came, wire)
    tall, came = lax.optimization_barrier((tall, came))
    whole = call(whole_kernel, shaped(sectors, 2, 128), [VMEM])(came)
    flip = [(i, i ^ 1) for i in range(sectors)]
    step_out = [(i, (i + 1 if i % 2 else i - 1) % sectors) for i in range(sectors)]
    stride = [(i, (i - 4 if i % 2 else i + 4) % sectors) for i in range(sectors)]
    partner = lax.ppermute(tall, "blk", flip)
    records = call(pair_records_kernel, shaped(TALL + ROWS // 8, 8, LEAF), [VMEM] * 2)(tall, partner)
    records, partner = lax.optimization_barrier((records, partner))
    came = lax.ppermute(records, "blk", step_out)
    side = near_side(False, tall, partner)
    came, side = lax.optimization_barrier((came, side))
    every = lax.all_to_all(whole, "blk", 0, 0, tiled=True)
    quad = call(quad_kernel, shaped(4, PACKED, 128), [VMEM] * 3)(tall, partner, came)
    onward = lax.ppermute(quad, "blk", stride)
    quad, came, every = lax.optimization_barrier((quad, came, every))
    beyond = near_side(True, tall, came)
    onward, beyond, every = lax.optimization_barrier((onward, beyond, every))
    outer = call(outer_kernel, shaped(6, PACKED, 128), [VMEM] * 2)(quad, onward)
    other = lax.ppermute(outer, "blk", flip)
    down = top(
        top_admissible, every, top_coupling[0], slab
    )
    out = finish(
        leaf_admissible_mask, leaf_coupling_matrices[0], quad, outer, other, down,
        transfer, basis, own, side, beyond,
    )
    return out[:, None]


def solution(mesh):
    return jax.shard_map(
        body,
        mesh=mesh,
        in_specs=(
            P(None, "blk", "along", None),
            P(None, "blk", "along", None),
            P("blk", "along", None),
            P("blk", "along", None, None),
            P("blk", "along", None, None),
            P("blk", "along", None, None),
            P("blk", None, None, None),
            P("blk", None),
            P("blk", None, None, None),
            P("blk", None),
        ),
        out_specs=P(None, "blk", "along", None),
        check_vma=False,
    )
```
